32 devices in a mesh: seq: 8 (over z, x), wa: 4 (over y, core).
Axes of the slice: x: 2, y: 2, z: 4, core: 2. Of those that a mesh axis runs over, the one named last changes fastest.
Arguments:
- inputs: bfloat16 [2, 4096, 768], P(None, 'seq', 'wa'), may hold values from -6 to 6
- targets: bfloat16 [2, 4096, 768], P(None, 'seq'), may hold values from -6 to 6
- lengths: int32 [2], replicated, may hold values from 2048 to 4096, as said below
- positions: int32 [2, 4096], P(None, 'seq'), may hold values from 0 to 8190, as said below
- ema_decay: float32 [768, 16], P('wa'), may hold values from 0 to 1
- ema_feed: float32 [768, 16], P('wa'), may hold values from -4 to 4
- ema_read: float32 [768, 16], P('wa'), may hold values from -1.5 to 1.5
- ema_skip: float32 [768], P('wa'), may hold values from -3 to 3
- zeta_proj: bfloat16 [768, 128], replicated, may hold values from -0.21875 to 0.21875
- zeta_bias: float32 [128], replicated, may hold values from -3 to 3
- query_gain: float32 [128], replicated, may hold values from 1.5 to 4
- query_shift: float32 [128], replicated, may hold values from -3 to 3
- key_gain: float32 [128], replicated, may hold values from 1.5 to 4
- rel_bias: float32 [255], replicated, may hold values from -4 to 4
- reset_proj: bfloat16 [768, 1536], P(None, 'wa'), may hold values from -0.21875 to 0.21875
- reset_bias: float32 [1536], P('wa'), may hold values from -3 to 3
- value_proj: bfloat16 [768, 1536], P(None, 'wa'), may hold values from -0.21875 to 0.21875
- value_bias: float32 [1536], P('wa'), may hold values from -3 to 3
- update_proj: bfloat16 [768, 768], P('wa'), may hold values from -0.21875 to 0.21875
- update_bias: float32 [768], replicated, may hold values from -3 to 3
- mixer_proj: bfloat16 [768, 768], P('wa'), may hold values from -0.21875 to 0.21875
- output_proj: bfloat16 [1536, 768], P('wa'), may hold values from -0.4375 to 0.4375
- output_bias: float32 [768], replicated, may hold values from -3 to 3
- first_gain: float32 [768], replicated, may hold values from 0.25 to 1.75
- first_shift: float32 [768], replicated, may hold values from -3 to 3
- up_proj: bfloat16 [768, 1536], P(None, 'wa'), may hold values from -0.21875 to 0.21875
- up_bias: bfloat16 [1536], P('wa'), may hold values from -3 to 3
- down_proj: bfloat16 [1536, 768], P('wa'), may hold values from -0.15625 to 0.15625
- down_bias: float32 [768], replicated, may hold values from -3 to 3
- second_gain: float32 [768], replicated, may hold values from 0.25 to 1.75
- second_shift: float32 [768], replicated, may hold values from -3 to 3
Outputs:
- block_out: bfloat16 [2, 4096, 768], P(None, 'seq', 'wa')
- input_grad: float32 [2, 4096, 768], P(None, 'seq', 'wa')
- teacher_loss: float32 [], replicated
- decay_grad: float32 [768, 16], P('wa')
- feed_grad: float32 [768, 16], P('wa')
- read_grad: float32 [768, 16], P('wa')
- skip_grad: float32 [768], P('wa')
- zeta_grad: float32 [768, 128], replicated
- zbias_grad: float32 [128], replicated
- qgain_grad: float32 [128], replicated
- qshift_grad: float32 [128], replicated
- kgain_grad: float32 [128], replicated
- rel_grad: float32 [255], replicated
- reset_grad: float32 [768, 1536], P(None, 'wa')
- rbias_grad: float32 [1536], P('wa')
- value_grad: float32 [768, 1536], P(None, 'wa')
- vbias_grad: float32 [1536], P('wa')
- update_grad: float32 [768, 768], P('wa')
- ubias_grad: float32 [768], replicated
- mixer_grad: float32 [768, 768], P('wa')
- output_grad: float32 [1536, 768], P('wa')
- obias_grad: float32 [768], replicated
- gainone_grad: float32 [768], replicated
- shiftone_grad: float32 [768], replicated
- up_grad: float32 [768, 1536], P(None, 'wa')
- upbias_grad: float32 [1536], P('wa')
- down_grad: float32 [1536, 768], P('wa')
- downbias_grad: float32 [768], replicated
- gaintwo_grad: float32 [768], replicated
- shifttwo_grad: float32 [768], replicated
The draws below stay inside these ranges and needn't reach their ends.
Inputs may be any that keep to these rules, and one draw needn't show every extreme that they name: `lengths`: one sequence is complete. `positions`: within each sequence the ids start at 0 and rise by 1 or 2 from one token to the next; in one sequence every rise is 2.
All inputs are finite; a program needn't handle non-finite values.
Results may differ from the reference program's by a relative error of at most 0.0181.
The reference program's roundings to bfloat16 on the way count: a program that leaves them out, or rounds other values in their place, can miss the bound.
Values may be sent and summed in bfloat16 or wider, within the bound.
No kernel may reach another device: no remote copies, remote signals or barrier semaphores. Data moves between devices by JAX's collectives and lax.ppermute only.
A program may use at most 192 MiB of HBM per device.

```python
import math
import jax
import jax.numpy as jnp
from jax import lax

D = 768
NDIM = 16
Z = 128
V = 1536
FF = 1536
GROUP = 128
SEQS = 2
SEQ_LEN = 4096
TOKENS = 8192
BUCKETS = 255


def ema_pair(key):
    base_key = jax.random.fold_in(key, 5)
    key_pick, key_slow, key_fast, key_sign = jax.random.split(base_key, 4)
    slow_share = 0.5
    pick_vals = jax.random.uniform(key_pick, (D, NDIM))
    slow_len = jnp.exp(jax.random.uniform(key_slow, (D, NDIM), minval=jnp.log(1.0 * SEQ_LEN), maxval=jnp.log(8.0 * SEQ_LEN)))
    fast_len = jnp.exp(jax.random.uniform(key_fast, (D, NDIM), minval=jnp.log(GROUP / 4.0), maxval=jnp.log(GROUP / 2.0)))
    memory = jnp.where(pick_vals < slow_share, slow_len, fast_len)
    decays = jnp.exp(-1.0 / memory)
    sign_vals = jnp.clip(jax.random.normal(key_sign, (D, NDIM)), -4.0, 4.0)
    feed_vals = jnp.sqrt(-jnp.expm1(-2.0 / memory)) * sign_vals
    return (decays.astype(jnp.float32), feed_vals.astype(jnp.float32))


def draw_ema_decay(key, part):
    return ema_pair(key)[0]


def draw_ema_feed(key, part):
    return ema_pair(key)[1]


def draw_lengths(key, part):
    key_len, key_pick = jax.random.split(jax.random.fold_in(key, 11))
    drawn_len = jax.random.randint(key_len, (SEQS,), SEQ_LEN // 2, SEQ_LEN + 1)
    chosen = jax.random.randint(key_pick, (), 0, SEQS)
    return jnp.where(jnp.arange(SEQS) == chosen, SEQ_LEN, drawn_len).astype(jnp.int32)


def draw_positions(key, part):
    key_step, key_pick = jax.random.split(jax.random.fold_in(key, 13))
    step_sizes = jax.random.randint(key_step, (SEQS, SEQ_LEN), 1, 3)
    chosen = jax.random.randint(key_pick, (), 0, SEQS)
    step_sizes = jnp.where(jnp.arange(SEQS)[:, None] == chosen, 2, step_sizes)
    ramp_ids = jnp.cumsum(step_sizes, axis=1) - step_sizes[:, :1]
    return ramp_ids.astype(jnp.int32)


def shard_levels(own_key, dims, cuts, smallest, largest):
    level, own = 1.0, jax.random.fold_in(own_key, 6)
    for axis_at, blocks in cuts:
        heights = jnp.exp(jax.random.uniform(jax.random.fold_in(own, axis_at), (blocks,), jnp.float32, smallest / len(cuts), largest / len(cuts)))
        level = level * jnp.repeat(heights, dims[axis_at] // blocks).reshape([-1 if axis == axis_at else 1 for axis in range(len(dims))])
    return level


def normal_values(stream_key, extent, width, most, cuts=(), held_as=jnp.bfloat16):
    values = width * jax.random.normal(stream_key, extent, jnp.float32)
    if cuts:
        values = values * shard_levels(stream_key, extent, cuts, -0.22, 0.18)
    return jnp.clip(values, -most, most).astype(held_as)


def setup_inputs(seed: int = 0) -> dict:
    splits = jax.random.split(jax.random.key(seed), 32)
    inputs = normal_values(splits[0], (SEQS, SEQ_LEN, D), 1.0, 6.0, ((1, 8), (2, 4)))
    targets = normal_values(splits[1], (SEQS, SEQ_LEN, D), 1.0, 6.0, ((1, 8),))
    lengths = draw_lengths(jax.random.fold_in(splits[31], 71), 0)
    positions = draw_positions(jax.random.fold_in(splits[31], 71), 0)
    ema_decay = draw_ema_decay(jax.random.fold_in(splits[31], 71), 0)
    ema_feed = draw_ema_feed(jax.random.fold_in(splits[31], 71), 0)
    ema_read = normal_values(splits[6], (D, NDIM), NDIM ** -0.5, 1.5, ((0, 4),), jnp.float32)
    ema_skip = normal_values(splits[7], (D,), 1.0, 3.0, ((0, 4),), jnp.float32)
    zeta_proj = normal_values(splits[8], (D, Z), D ** -0.5, 0.21875)
    zeta_bias = normal_values(splits[9], (Z,), 0.5, 3.0, (), jnp.float32)
    query_gain = jnp.clip(jnp.exp(jax.random.uniform(splits[10], (Z,), jnp.float32, math.log(1.5), math.log(4.0))), 1.5, 4.0)
    query_shift = normal_values(splits[11], (Z,), 0.5, 3.0, (), jnp.float32)
    key_gain = jnp.clip(jnp.exp(jax.random.uniform(splits[12], (Z,), jnp.float32, math.log(1.5), math.log(4.0))), 1.5, 4.0)
    rel_bias = normal_values(splits[13], (BUCKETS,), 1.0, 4.0, (), jnp.float32)
    reset_proj = normal_values(splits[14], (D, V), D ** -0.5, 0.21875, ((1, 4),))
    reset_bias = normal_values(splits[15], (V,), 0.5, 3.0, ((0, 4),), jnp.float32)
    value_proj = normal_values(splits[16], (D, V), D ** -0.5, 0.21875, ((1, 4),))
    value_bias = normal_values(splits[17], (V,), 0.5, 3.0, ((0, 4),), jnp.float32)
    update_proj = normal_values(splits[18], (D, D), D ** -0.5, 0.21875, ((0, 4),))
    update_bias = normal_values(splits[19], (D,), 0.5, 3.0, (), jnp.float32)
    mixer_proj = normal_values(splits[20], (D, D), D ** -0.5, 0.21875, ((0, 4),))
    output_proj = normal_values(splits[21], (V, D), (V // 8) ** -0.5, 0.4375, ((0, 4),))
    output_bias = normal_values(splits[22], (D,), 0.5, 3.0, (), jnp.float32)
    first_gain = jnp.clip(1.0 + 0.15 * jax.random.normal(splits[23], (D,), jnp.float32), 0.25, 1.75)
    first_shift = normal_values(splits[24], (D,), 0.3, 3.0, (), jnp.float32)
    up_proj = normal_values(splits[25], (D, FF), D ** -0.5, 0.21875, ((1, 4),))
    up_bias = normal_values(splits[26], (FF,), 0.5, 3.0, ((0, 4),))
    down_proj = normal_values(splits[27], (FF, D), FF ** -0.5, 0.15625, ((0, 4),))
    down_bias = normal_values(splits[28], (D,), 0.3, 3.0, (), jnp.float32)
    second_gain = jnp.clip(1.0 + 0.15 * jax.random.normal(splits[29], (D,), jnp.float32), 0.25, 1.75)
    second_shift = normal_values(splits[30], (D,), 0.3, 3.0, (), jnp.float32)
    return {"inputs": inputs, "targets": targets, "lengths": lengths, "positions": positions, "ema_decay": ema_decay, "ema_feed": ema_feed, "ema_read": ema_read, "ema_skip": ema_skip, "zeta_proj": zeta_proj, "zeta_bias": zeta_bias, "query_gain": query_gain, "query_shift": query_shift, "key_gain": key_gain, "rel_bias": rel_bias, "reset_proj": reset_proj, "reset_bias": reset_bias, "value_proj": value_proj, "value_bias": value_bias, "update_proj": update_proj, "update_bias": update_bias, "mixer_proj": mixer_proj, "output_proj": output_proj, "output_bias": output_bias, "first_gain": first_gain, "first_shift": first_shift, "up_proj": up_proj, "up_bias": up_bias, "down_proj": down_proj, "down_bias": down_bias, "second_gain": second_gain, "second_shift": second_shift}


EPSILON = 1e-05
HIGHEST = lax.Precision.HIGHEST

@jax.custom_vjp
def low(v):
    return lax.optimization_barrier(v.astype(jnp.bfloat16)).astype(jnp.float32)

@jax.custom_vjp
def low_back(v):
    return v

def low_keep(v):
    return (low(v), None)

def low_pass(kept, grad):
    return (grad,)

def back_keep(v):
    return (v, None)

def back_low(kept, grad):
    return (low(grad),)
low.defvjp(low_keep, low_pass)
low_back.defvjp(back_keep, back_low)

def matmul(left_side, right_side):
    return jnp.dot(left_side, right_side, precision=HIGHEST, preferred_element_type=jnp.float32)

def layer_norm(values, scales, offsets):
    center = values - lax.optimization_barrier(jnp.mean(values, axis=-1, keepdims=True))
    inv_scale = lax.rsqrt(lax.optimization_barrier(jnp.mean(center * center, axis=-1, keepdims=True)) + EPSILON)
    return center * inv_scale * scales + offsets

def ema_group(state_now, tok_block, decay, feed, read, skip):

    def ema_step(carry_state, column):
        carry_state = decay * carry_state + feed * column[:, :, None]
        return (carry_state, lax.optimization_barrier(jnp.sum(read * carry_state, axis=-1)) + skip * column)
    return lax.scan(ema_step, state_now, tok_block)

def ema_apply(signal, decay, feed, read, skip):
    blocks = jnp.transpose(signal.reshape(SEQS, SEQ_LEN // GROUP, GROUP, D), (1, 2, 0, 3))

    def run_block(state_now, tok_block):
        return jax.checkpoint(ema_group)(state_now, tok_block, decay, feed, read, skip)
    zero_state = jnp.zeros((SEQS, D, NDIM), jnp.float32)
    final_state, outputs = lax.scan(run_block, zero_state, blocks)
    return jnp.transpose(outputs, (2, 0, 1, 3)).reshape(TOKENS, D)

def forward(params, targets_f, weights_row, positions, true_count):
    inputs_f, ema_decay, ema_feed, ema_read, ema_skip, zeta_proj, zeta_bias, query_gain, query_shift, key_gain, rel_bias, reset_proj, reset_bias, value_proj, value_bias, update_proj, update_bias, mixer_proj, output_proj, output_bias, first_gain, first_shift, up_proj, up_bias, down_proj, down_bias, second_gain, second_shift = params
    ema_val = ema_apply(inputs_f, ema_decay, ema_feed, ema_read, ema_skip)
    mixed_in = low(jax.nn.silu(ema_val))
    zeta_act = jax.nn.silu(low_back(matmul(mixed_in, zeta_proj) + zeta_bias))
    queries = low(zeta_act * query_gain + query_shift)
    key_vals = low(zeta_act * key_gain)
    reset_gate = jax.nn.silu(low_back(matmul(mixed_in, reset_proj) + reset_bias))
    values = low(jax.nn.silu(low_back(matmul(inputs_f, value_proj) + value_bias)))
    update_gate = jax.nn.sigmoid(low_back(matmul(mixed_in, update_proj) + update_bias))
    n_groups = TOKENS // GROUP
    query_blocks = queries.reshape(n_groups, GROUP, Z)
    key_blocks = key_vals.reshape(n_groups, GROUP, Z)
    value_blocks = values.reshape(n_groups, GROUP, V)
    pos_blocks = positions.reshape(n_groups, GROUP)
    distance = jnp.clip(pos_blocks[:, :, None] - pos_blocks[:, None, :], 0, BUCKETS - 1)
    causal = jnp.arange(GROUP)[:, None] >= jnp.arange(GROUP)[None, :]
    raw_scores = jnp.einsum('cqz,ckz->cqk', query_blocks, key_blocks, precision=HIGHEST) * Z ** (-0.5) + rel_bias[distance]
    scores = jnp.where(causal, low_back(raw_scores), -jnp.inf)
    attn_probs = low(jax.nn.softmax(scores, axis=-1))
    attended = low_back(jnp.einsum('cqk,ckv->cqv', attn_probs, value_blocks, precision=HIGHEST).reshape(TOKENS, V))
    gated = low(reset_gate * attended)
    out_act = jax.nn.silu(low_back(matmul(mixed_in, mixer_proj) + matmul(gated, output_proj) + output_bias))
    block_mid = update_gate * out_act + (1.0 - update_gate) * inputs_f
    first_out = layer_norm(block_mid, first_gain, first_shift)
    up_act = low(jax.nn.silu(low_back(matmul(low(first_out), up_proj) + up_bias)))
    ffn_out = low_back(matmul(up_act, down_proj) + down_bias)
    second_out = layer_norm(first_out + ffn_out, second_gain, second_shift)
    misfit = second_out - targets_f
    teacher = jnp.sum(weights_row * lax.optimization_barrier(jnp.sum(misfit * misfit, axis=1))) / (2.0 * D * true_count)
    return (teacher * (TOKENS * D), (second_out, teacher))

def reference(inputs, targets, lengths, positions, ema_decay, ema_feed, ema_read, ema_skip, zeta_proj, zeta_bias, query_gain, query_shift, key_gain, rel_bias, reset_proj, reset_bias, value_proj, value_bias, update_proj, update_bias, mixer_proj, output_proj, output_bias, first_gain, first_shift, up_proj, up_bias, down_proj, down_bias, second_gain, second_shift):
    targets_f = targets.astype(jnp.float32).reshape(TOKENS, D)
    flat_pos = positions.reshape(TOKENS)
    weights_row = (jnp.arange(SEQ_LEN)[None, :] < lengths[:, None]).astype(jnp.float32).reshape(TOKENS)
    true_count = jnp.sum(lengths).astype(jnp.float32)
    params = (inputs.astype(jnp.float32).reshape(TOKENS, D), ema_decay, ema_feed, ema_read, ema_skip, zeta_proj.astype(jnp.float32), zeta_bias, query_gain, query_shift, key_gain, rel_bias, reset_proj.astype(jnp.float32), reset_bias, value_proj.astype(jnp.float32), value_bias, update_proj.astype(jnp.float32), update_bias, mixer_proj.astype(jnp.float32), output_proj.astype(jnp.float32), output_bias, first_gain, first_shift, up_proj.astype(jnp.float32), up_bias.astype(jnp.float32), down_proj.astype(jnp.float32), down_bias, second_gain, second_shift)

    def wrapped(*flat):
        return forward(flat, targets_f, weights_row, flat_pos, true_count)
    scaled, pullback, extras = jax.vjp(wrapped, *params, has_aux=True)
    grads = pullback(jnp.ones_like(scaled))
    second_out, teacher = extras
    return (second_out.reshape(SEQS, SEQ_LEN, D).astype(jnp.bfloat16), grads[0].reshape(SEQS, SEQ_LEN, D), teacher, grads[1], grads[2], grads[3], grads[4], grads[5], grads[6], grads[7], grads[8], grads[9], grads[10], grads[11], grads[12], grads[13], grads[14], grads[15], grads[16], grads[17], grads[18], grads[19], grads[20], grads[21], grads[22], grads[23], grads[24], grads[25], grads[26], grads[27])
```

```python
import functools

import jax
import jax.numpy as jnp
from jax import lax
from jax.experimental import pallas as pl
from jax.experimental.pallas import tpu as pltpu
from jax.sharding import PartitionSpec as P

Z = 128
GROUP = 128
LANES = 128
CHUNKS = 8
BIAS_ROWS = 32
HIDE_ENDS, HIDE_VALUES, HIDE_ONE, HIDE_TWO, HIDE_BACK, HIDE_LAST = 20, 20, 20, 40, 60, 15
SHARE_BITS = 1
EPSILON = 1e-05
BF = jnp.bfloat16
F32 = jnp.float32
VMEM = pltpu.MemorySpace.VMEM
SMEM = pltpu.MemorySpace.SMEM


def dot(a, b):
    return jnp.dot(a, b, preferred_element_type=F32)


def dot_nt(a, b):
    return lax.dot_general(a, b, (((1,), (1,)), ((), ())), preferred_element_type=F32)


def dot_tn(a, b):
    return lax.dot_general(a, b, (((0,), (0,)), ((), ())), preferred_element_type=F32)


def sigmoid(v):
    return 1.0 / (1.0 + jnp.exp(-v))


def slope(v):
    s = sigmoid(v)
    return s * (1.0 + v * (1.0 - s))


def row(ref):
    return ref[...].reshape(1, ref.shape[0])


def colsum(v):
    return jnp.sum(v, axis=0, keepdims=True)


def normalise(v):
    center = v - jnp.mean(v, axis=-1, keepdims=True)
    inv = lax.rsqrt(jnp.mean(center * center, axis=-1, keepdims=True) + EPSILON)
    return center * inv, inv


def norm_back(grad, normed, inv, gain):
    scaled = grad * gain
    one = jnp.mean(scaled, axis=-1, keepdims=True)
    two = jnp.mean(scaled * normed, axis=-1, keepdims=True)
    return inv * (scaled - one - normed * two)


class Box:
    def __init__(self, **parts):
        self.__dict__.update(parts)


jax.tree_util.register_pytree_node(
    Box, lambda box: (tuple(vars(box).values()), tuple(vars(box))), lambda names, parts: Box(**dict(zip(names, parts)))
)


def whole(space=VMEM):
    return pl.BlockSpec(memory_space=space)


def run(kernel, ins, outs, scratch, after=(), vectors=None, limit=48, hides=0):
    body, count = kernel, len(ins)
    vectors = vectors or Box()
    outs.token = ((8, LANES), F32, VMEM)
    fetched = len(vars(vectors))
    ins = ins + [(vectors, pltpu.MemorySpace.HBM), (list(after), pl.ANY)]
    scratch = Box(
        body=scratch, vec=jax.tree.map(lambda a: pltpu.VMEM(a.shape, a.dtype), vectors),
        sem=pltpu.SemaphoreType.DMA((max(fetched, 1),)),
    )

    def kernel(*refs):
        hbm, out, s = refs[count], refs[count + 2], refs[count + 3]
        copies = [
            pltpu.make_async_copy(vars(hbm)[name], vars(s.vec)[name], s.sem.at[i]) for i, name in enumerate(vars(hbm))
        ]
        for copy in copies:
            copy.start()
        if fetched:
            s.body.vec = s.vec
            s.body.wait = lambda: [copy.wait() for copy in copies]
        out.token[...] = jnp.zeros_like(out.token)
        body(*refs[:count], out, s.body)

    specs = [jax.tree.map(lambda _, space=space: whole(space), tree) for tree, space in ins]
    trees = [tree for tree, _ in ins]
    leaf = lambda entry: isinstance(entry, tuple)
    shapes = jax.tree.map(lambda e: jax.ShapeDtypeStruct(e[0], e[1]), outs, is_leaf=leaf)
    out_specs = jax.tree.map(lambda e: whole(e[2]), outs, is_leaf=leaf)
    return pl.pallas_call(
        kernel,
        out_shape=(shapes,),
        in_specs=specs,
        out_specs=(out_specs,),
        scratch_shapes=[scratch],
        compiler_params=pltpu.CompilerParams(vmem_limit_bytes=limit * 2**20),
        cost_estimate=pl.CostEstimate(flops=1 + int(hides * 1.15e9), bytes_accessed=1, transcendentals=0),
    )(*trees)[0]


def beside(hides, *deps):
    def kernel(ins, out, s):
        pass

    return run(kernel, [(list(deps), pl.ANY)], Box(), Box(), hides=hides)


def pack(pieces, meta, regions, out):
    height = out.own.shape[0]
    for ref, at, rows, top, left in regions:
        out.packed[top : top + rows, left : left + ref.shape[1]] = ref[at : at + rows, :]

    def piece(j):
        for ref, at, rows, top, left in regions:
            low, high = max(top, j * height), min(top + rows, (j + 1) * height)
            if low < high:
                out.own[low - j * height : high - j * height, left : left + ref.shape[1]] = ref[at + low - top : at + high - top, :]

    for j in range(pieces):
        pl.when(meta[1] == j)(lambda j=j: piece(j))


def pack_first(pieces, meta, reset, value, rel, out, s):
    units = reset.shape[1]
    s.wait()
    s.rows[...] = jnp.zeros_like(s.rows)
    for left, ref in ((0, s.vec.reset), (units, s.vec.value)):
        rest = row(ref)
        for i in range(3):
            high = rest.astype(BF).astype(F32)
            s.rows[i : i + 1, left : left + units] = high
            rest = rest - high
    s.rows[3:4, :units] = row(s.vec.up).astype(F32)
    s.bias[...] = s.rows[...].astype(BF)
    out.rel[...] = jnp.zeros_like(out.rel)
    out.rel[0:1, : rel.shape[0]] = row(rel)
    wide = reset.shape[0]
    pack(pieces, meta, [(reset, 0, wide, 0, 0), (value, 0, wide, 0, units), (s.bias, 0, BIAS_ROWS, wide, 0)], out)


def pack_second(pieces, meta, update, mixer, output, out, s):
    width, units = update.shape[0], output.shape[0]
    pack(pieces, meta, [(update, 0, width, 0, 0), (mixer, 0, width, width, 0), (output, 0, units, 2 * width, 0)], out)


def pack_third(pieces, meta, up, down, out, s):
    hidden = up.shape[1]
    depth = up.shape[0] // (down.shape[1] // hidden)
    regions = [(up, at, depth, 0, at // depth * hidden) for at in range(0, up.shape[0], depth)]
    pack(pieces, meta, regions + [(down, 0, hidden, depth, 0)], out)


def lane_groups(seqs, width):
    groups = []
    rest = width % LANES
    for s in range(seqs):
        for c in range(0, width - rest, LANES):
            groups.append([(s, c, LANES, 0)])
    tile, lane = [], 0
    for s in range(seqs if rest else 0):
        if lane + rest > LANES:
            groups.append(tile)
            tile, lane = [], 0
        tile.append((s, width - rest, rest, lane))
        lane += rest
    if tile:
        groups.append(tile)
    return groups


def join(parts):
    rows = parts[0].shape[0]
    used = sum(p.shape[1] for p in parts)
    if used < LANES:
        parts = parts + [jnp.zeros((rows, LANES - used), parts[0].dtype)]
    return parts[0] if len(parts) == 1 else jnp.concatenate(parts, axis=1)


def rows_of(group, ref):
    return join([ref[:, c : c + w] for _, c, w, _ in group])


def tokens_of(group, get):
    return join([get(s, c, w) for s, c, w, _ in group])


def spread(row):
    return jnp.broadcast_to(row, (CHUNKS, LANES))


def power(v, count):
    while count > 1:
        v = v * v
        count //= 2
    return v


def shifted(v, by):
    at = lax.broadcasted_iota(jnp.int32, v.shape, 0)
    moved = pltpu.roll(v, by % CHUNKS, 0)
    keep = at >= by if by > 0 else at < CHUNKS + by
    return jnp.where(keep, moved, 0.0)


def chunk_scan(ends, chunk_decay, sign):
    run_sum, factor, step = ends, chunk_decay, 1
    while step < CHUNKS:
        run_sum = run_sum + factor * shifted(run_sum, sign * step)
        factor, step = factor * factor, step * 2
    return run_sum, shifted(run_sum, sign)


def rank_power(chunk_decay, reverse):
    at = lax.broadcasted_iota(jnp.int32, chunk_decay.shape, 0)
    at = CHUNKS - 1 - at if reverse else at
    result, factor, bit = jnp.ones_like(chunk_decay), chunk_decay, 1
    while bit < CHUNKS:
        result = jnp.where((at & bit) != 0, result * factor, result)
        factor, bit = factor * factor, bit * 2
    return result


def steps_of(length, body, carry, reverse=False, unroll=4):
    def block(i, state):
        for u in range(unroll):
            t = i * unroll + u
            state = body(length - 1 - t if reverse else t, state)
        return state

    return lax.fori_loop(0, length // unroll, block, carry)


def at_step(ref, g, t, length):
    return ref.at[g, pl.ds(t, CHUNKS, stride=length), :]


def ema_ends(groups, comps, blocks, meta, x_ref, decay_ref, out, s):
    rows = x_ref.shape[1]
    part = x_ref.shape[0] * rows // blocks
    copies = []
    for k in range(blocks):
        at = (meta[0] ^ k) * part
        source = x_ref.at[at // rows, pl.ds(pl.multiple_of(at % rows, part), part), :]
        copies.append(pltpu.make_async_copy(source, out.r[k], s.sem.at[k]))
    for copy in copies:
        copy.start()
    length = x_ref.shape[1] // CHUNKS
    for g, group in enumerate(groups):
        s.x[g] = tokens_of(group, lambda q, c, w: x_ref[q, :, c : c + w].astype(F32))
        decay = rows_of(group, decay_ref)
        decays = [spread(decay[n : n + 1]) for n in range(comps)]

        def body(t, state):
            now = at_step(s.x, g, t, length)[...]
            return tuple(decays[n] * state[n] + now for n in range(comps))

        ends = steps_of(length, body, (jnp.zeros((CHUNKS, LANES), F32),) * comps)
        for n in range(comps):
            total, before = chunk_scan(ends[n], power(decays[n], length), 1)
            out.before[g, n] = before
            out.fade[g, n : n + 1, :] = power(decay[n : n + 1], length * CHUNKS)
            out.end[g, n : n + 1, :] = total[CHUNKS - 1 :]
    for copy in copies:
        copy.wait()


def carried(parts, device_decay, rank, reverse):
    total, passed = jnp.zeros_like(device_decay), jnp.ones_like(device_decay)
    for i, part in enumerate(parts):
        counts = ((rank // (1 << i)) % 2) == (0 if reverse else 1)
        total = jnp.where(counts, total + passed * part, total)
        passed = jnp.where(counts, passed * device_decay, passed)
        device_decay = device_decay * device_decay
    return total


def ema_values(groups, comps, blocks, meta, x_ref, decay_ref, mix_ref, skip_ref, before_ref, got, out, s):
    length = x_ref.shape[1] // CHUNKS
    width = x_ref.shape[2]
    seqs, rows = x_ref.shape[0], x_ref.shape[1]
    for g, group in enumerate(groups):
        s.x[g] = tokens_of(group, lambda q, c, w: x_ref[q, :, c : c + w].astype(F32))
        decay, mix, skip = rows_of(group, decay_ref), rows_of(group, mix_ref), rows_of(group, skip_ref)
        decays = [spread(decay[n : n + 1]) for n in range(comps)]
        mixes = [spread(mix[n : n + 1]) for n in range(comps)]
        skip = spread(skip)
        state_in = carried([part[g] for part in got], power(decay, length * CHUNKS), meta[2], False)
        start = []
        for n in range(comps):
            ranks = rank_power(power(decays[n], length), False)
            start.append(before_ref[g, n] + ranks * spread(state_in[n : n + 1]))
            out.start[g, n] = start[n]

        def body(t, state):
            now = at_step(s.x, g, t, length)[...]
            state = tuple(decays[n] * state[n] + now for n in range(comps))
            terms = [mixes[n] * state[n] for n in range(comps)] + [skip * now]
            while len(terms) > 1:
                terms = [a + b for a, b in zip(terms[::2], terms[1::2])] + (terms[-1:] if len(terms) % 2 else [])
            at_step(s.y, g, t, length)[...] = terms[0]
            return state

        steps_of(length, body, tuple(start))
        for q, c, w, lane in group:
            value = s.y[g, :, lane : lane + w]
            out.value[q, :, c : c + w] = value
            s.mixed[pl.ds(q * rows, rows), c : c + w] = (value * sigmoid(value)).astype(BF)
    part = seqs * rows // blocks
    copies = [
        pltpu.make_async_copy(
            s.mixed.at[pl.ds(pl.multiple_of((meta[0] ^ k) * part, part), part), :], out.m[k], s.sem.at[k]
        )
        for k in range(blocks)
    ]
    for copy in copies:
        copy.start()
    for copy in copies:
        copy.wait()


def ema_back_ends(groups, comps, blocks, meta, grads, value_ref, decay_ref, out, s):
    length = value_ref.shape[1] // CHUNKS
    rows = value_ref.shape[1]
    part = value_ref.shape[0] * rows // blocks
    copies = [
        pltpu.make_async_copy(
            grads[k], s.grad.at[pl.ds(pl.multiple_of((meta[0] ^ k) * part, part), part), :], s.sem.at[k]
        )
        for k in range(blocks)
    ]
    for copy in copies:
        copy.start()
    for copy in copies:
        copy.wait()
    for g, group in enumerate(groups):

        def load(q, c, w):
            return s.grad[pl.ds(q * rows, rows), c : c + w].astype(F32) * slope(value_ref[q, :, c : c + w])

        out.grad[g] = tokens_of(group, load)
        decay = rows_of(group, decay_ref)
        decays = [spread(decay[n : n + 1]) for n in range(comps)]

        def body(t, state):
            now = at_step(out.grad, g, t, length)[...]
            return tuple(decays[n] * state[n] + now for n in range(comps))

        ends = steps_of(length, body, (jnp.zeros((CHUNKS, LANES), F32),) * comps, reverse=True)
        for n in range(comps):
            total, after = chunk_scan(ends[n], power(decays[n], length), -1)
            out.after[g, n] = after
            out.first[g, n : n + 1, :] = total[:1]


def ema_back(groups, comps, blocks, meta, x_ref, grad_ref, rests, decay_ref, mix_ref, skip_ref, start_ref, after_ref, got, out, s):
    length = x_ref.shape[1] // CHUNKS
    seqs, rows = x_ref.shape[0], x_ref.shape[1]
    part = seqs * rows // blocks
    copies = [
        pltpu.make_async_copy(
            rests[k], s.rest.at[pl.ds(pl.multiple_of((meta[0] ^ k) * part, part), part), :], s.sem.at[k]
        )
        for k in range(blocks)
    ]
    for copy in copies:
        copy.start()
    out.sums[...] = jnp.zeros_like(out.sums)
    half = comps // 2
    for g, group in enumerate(groups):
        s.x[g] = tokens_of(group, lambda q, c, w: x_ref[q, :, c : c + w].astype(F32))
        decay, mix, skip = rows_of(group, decay_ref), rows_of(group, mix_ref), rows_of(group, skip_ref)
        decays = [spread(decay[n : n + 1]) for n in range(comps)]
        mixes = [spread(mix[n : n + 1]) for n in range(comps)]
        skip = spread(skip)

        def forward(t, state):
            now = at_step(s.x, g, t, length)[...]
            for n in range(comps):
                s.states[t, n] = state[n]
            return tuple(decays[n] * state[n] + now for n in range(comps))

        steps_of(length, forward, tuple(start_ref[g, n] for n in range(comps)))
        grad_in = carried([p[g] for p in got], power(decay, length * CHUNKS), meta[2], True)
        for h in range(2):
            mine = range(h * half, (h + 1) * half)
            begin = []
            for n in mine:
                ranks = rank_power(power(decays[n], length), True)
                begin.append(after_ref[g, n] + ranks * spread(grad_in[n : n + 1]))
            zero = (jnp.zeros((CHUNKS, LANES), F32),) * half

            def backward(t, carry):
                grads, moments, changes, skips = carry
                now, up = at_step(s.x, g, t, length)[...], at_step(grad_ref, g, t, length)[...]
                grads = tuple(decays[n] * grads[i] + up for i, n in enumerate(mine))
                moments = tuple(moments[i] + grads[i] * now for i in range(half))
                changes = tuple(changes[i] + grads[i] * s.states[t, n] for i, n in enumerate(mine))
                terms = [mixes[n] * grads[i] for i, n in enumerate(mine)]
                if h == 0:
                    terms.append(skip * up)
                    skips = skips + up * now
                else:
                    terms.append(at_step(s.y, g, t, length)[...])
                while len(terms) > 1:
                    terms = [a + b for a, b in zip(terms[::2], terms[1::2])] + (terms[-1:] if len(terms) % 2 else [])
                at_step(s.y, g, t, length)[...] = terms[0]
                return grads, moments, changes, skips

            _, moments, changes, skips = steps_of(length, backward, (tuple(begin), zero, zero, zero[0]), reverse=True, unroll=2)
            for q, c, w, lane in group:
                for i, n in enumerate(mine):
                    out.sums[n : n + 1, c : c + w] += colsum(changes[i])[:, lane : lane + w]
                    out.sums[comps + n : comps + n + 1, c : c + w] += colsum(moments[i])[:, lane : lane + w]
                if h == 0:
                    out.sums[2 * comps : 2 * comps + 1, c : c + w] += colsum(skips)[:, lane : lane + w]
    for copy in copies:
        copy.wait()
    width = x_ref.shape[2]
    for q in range(seqs):
        out.block[q] = s.rest[pl.ds(q * rows, rows), width:]
    for g, group in enumerate(groups):
        for q, c, w, lane in group:
            rest = s.rest[pl.ds(q * rows, rows), c : c + w].astype(F32)
            out.grad[q, :, c : c + w] = s.y[g, :, lane : lane + w] + rest


def weight_copies(meta, shards, dst, sem, first):
    copies = []
    for k, pieces in enumerate(shards):
        height = dst.shape[1] // len(pieces)
        for j, piece in enumerate(pieces):
            target = dst.at[k]
            if len(pieces) > 1:
                target = dst.at[k, pl.ds(pl.multiple_of((meta[1] ^ j) * height, height), height), :]
            copies.append(pltpu.make_async_copy(piece, target, sem.at[first + len(copies)]))
    return copies


def block_copies(meta, blocks, dst, sem, first):
    return [
        pltpu.make_async_copy(block, dst.at[meta[0] ^ k], sem.at[first + k]) for k, block in enumerate(blocks)
    ]


def positions_of(ref, start, g):
    at = start + g * GROUP
    length = ref.shape[1]
    columns = pl.ds(pl.multiple_of(at % length, GROUP), GROUP)
    place = ref[0:1, columns]
    for q in range(1, ref.shape[0]):
        place = jnp.where(at // length == q, ref[q : q + 1, columns], place)
    return place


def attend_forward(peers, meta, mixed, raw, first, second, out, s):
    vec = s.vec
    blocks = block_copies(meta, mixed, s.mixed, s.sem, 0)
    blocks += block_copies(meta, raw, s.raw, s.sem, peers)
    ones = weight_copies(meta, first, s.one, s.sem, 2 * peers)
    twos = weight_copies(meta, second, s.two, s.sem, 2 * peers + len(ones))
    for copy in blocks + ones + twos:
        copy.start()
    for copy in blocks:
        copy.wait()
    width = s.mixed.shape[2]
    units = s.one.shape[2] // 2
    rows, wide = out.mixed.shape
    groups = rows // GROUP
    for b in range(peers):
        out.mixed[:, b * width : (b + 1) * width] = s.mixed[b]
        out.raw[:, b * width : (b + 1) * width] = s.raw[b]
    s.wait()
    zeta_pre = dot(out.mixed[...], vec.zeta[...]) + row(vec.zeta_bias)
    out.zeta_pre[...] = zeta_pre
    act = zeta_pre * sigmoid(zeta_pre)
    queries = (act * row(vec.query_gain) + row(vec.query_shift)).astype(BF)
    keys = (act * row(vec.key_gain)).astype(BF)
    out.queries[...] = queries
    out.keys[...] = keys
    causal = lax.broadcasted_iota(jnp.int32, (GROUP, GROUP), 0) >= lax.broadcasted_iota(jnp.int32, (GROUP, GROUP), 1)
    for g in range(groups):
        at = slice(g * GROUP, (g + 1) * GROUP)
        place = jnp.broadcast_to(positions_of(vec.positions, meta[0] * rows, g).astype(F32), (GROUP, GROUP))
        distance = jnp.clip((place.T - place).astype(jnp.int32), 0, 2 * GROUP - 2)
        low = jnp.take_along_axis(
            jnp.broadcast_to(vec.rel[0:1, :GROUP], (GROUP, GROUP)), distance & (GROUP - 1), axis=1
        )
        high = jnp.take_along_axis(
            jnp.broadcast_to(vec.rel[0:1, GROUP:], (GROUP, GROUP)), distance & (GROUP - 1), axis=1
        )
        scores = dot_nt(queries[at], keys[at]) * Z**-0.5 + jnp.where(distance < GROUP, low, high)
        scores = jnp.where(causal, scores, -jnp.inf)
        shifted_exp = jnp.exp(scores - jnp.max(scores, axis=-1, keepdims=True))
        out.probs[at, :] = shifted_exp / jnp.sum(shifted_exp, axis=-1, keepdims=True)
    for copy in ones:
        copy.wait()
    for copy in twos:
        copy.wait()
    s.pre[...] = jnp.zeros_like(s.pre)
    s.gate[...] = jnp.zeros_like(s.gate)

    def shard(k, carry):
        biases = s.one[k, wide : wide + 16, :].astype(F32)
        bias = biases[0:1] + biases[1:2] + biases[2:3]
        out.up_bias[k] = jnp.broadcast_to(biases[3:4, :units], (8, units))
        reset_pre = dot(out.mixed[...], s.one[k, :wide, :units]) + bias[:, :units]
        value_pre = dot(out.raw[...], s.one[k, :wide, units:]) + bias[:, units:]
        values = (value_pre * sigmoid(value_pre)).astype(BF)
        out.reset_pre[k] = reset_pre
        out.value_pre[k] = value_pre
        out.values[k] = values
        for g in range(groups):
            at = slice(g * GROUP, (g + 1) * GROUP)
            out.attended[k, at, :] = dot(out.probs[at, :].astype(BF), values[at])
        gated = (reset_pre * sigmoid(reset_pre) * out.attended[k]).astype(BF)
        out.gated[k] = gated
        block = s.mixed[meta[0] ^ k]
        s.gate[...] += dot(block, s.two[k, :width, :])
        s.pre[...] += dot(block, s.two[k, width : 2 * width, :]) + dot(gated, s.two[k, 2 * width :, :])
        return carry

    lax.fori_loop(0, peers, shard, 0)
    out_pre = s.pre[...] + row(vec.output_bias)
    out.out_pre[...] = out_pre
    gate = sigmoid(s.gate[...] + row(vec.update_bias))
    out.gate[...] = gate
    mid = gate * (out_pre * sigmoid(out_pre)) + (1.0 - gate) * out.raw[...].astype(F32)
    normed, inv = normalise(mid)
    out.normed[...] = normed
    out.inv[...] = inv


def feed_forward(peers, ranks, meta, lengths, third, normed_ref, inv_ref, targets, out, s):
    vec = s.vec
    rows = normed_ref.shape[0]
    seqs, seq_rows = targets.shape[0], targets.shape[1]
    seq, offset = meta[0] * rows // seq_rows, pl.multiple_of(meta[0] * rows % seq_rows, rows)
    fetch = pltpu.make_async_copy(targets.at[seq, pl.ds(offset, rows), :], s.targets, s.target_sem)
    fetch.start()
    threes = weight_copies(meta, third, s.three, s.sem, 0)
    for copy in threes:
        copy.start()
    rows, width = normed_ref.shape
    s.wait()
    units = vec.up_bias.shape[2]
    fold = width // units
    depth = width // fold
    first = normed_ref[...] * row(vec.first_gain) + row(vec.first_shift)
    s.first[...] = first.astype(BF)
    s.total[...] = first + row(vec.down_bias)
    for copy in threes:
        copy.wait()

    def forward(k, carry):
        pre = vec.up_bias[k, 0:1, :]
        for j in range(fold):
            pre = pre + dot(
                s.first[:, j * depth : (j + 1) * depth], s.three[k, :depth, j * units : (j + 1) * units]
            )
        s.up_pre[k] = pre
        act = (pre * sigmoid(pre)).astype(BF)
        s.act[k] = act
        s.total[...] += dot(act, s.three[k, depth:, :])
        return carry

    lax.fori_loop(0, peers, forward, 0)
    normed, inv = normalise(s.total[...])
    second = normed * row(vec.second_gain) + row(vec.second_shift)
    piece = width // peers
    for b in range(peers):
        out.second[b] = second[:, b * piece : (b + 1) * piece].astype(BF)
    fetch.wait()
    misfit = second - s.targets[...].astype(F32)
    place = lax.broadcasted_iota(jnp.int32, (rows, 1), 0) + (meta[2] * seq_rows + offset)
    weight = (place < lengths[seq]).astype(F32)
    tokens = lengths[0]
    for q in range(1, seqs):
        tokens = tokens + lengths[q]
    true_count = jnp.broadcast_to(tokens, (rows, 1)).astype(F32)
    losses = jnp.sum(misfit * misfit, axis=1, keepdims=True) * (weight / (2.0 * width * true_count))
    out.sums[...] = jnp.zeros_like(out.sums)
    out.sums[5:6, :] = jnp.broadcast_to(jnp.sum(losses, axis=0, keepdims=True), (1, width))
    grad_out = misfit * (weight * (seqs * seq_rows * ranks / true_count))
    out.sums[0:1, :] = colsum(grad_out * normed)
    out.sums[1:2, :] = colsum(grad_out)
    second_grad = norm_back(grad_out, normed, inv, row(vec.second_gain))
    ffn_grad = second_grad.astype(BF)
    s.grad[...] = ffn_grad
    out.sums[2:3, :] = colsum(ffn_grad.astype(F32))
    s.total[...] = second_grad

    def backward(k, carry):
        keep = k // 2
        down = dot_tn(s.act[k], s.grad[...]).astype(BF)
        up_grad = (dot_nt(s.grad[...], s.three[k, depth:, :]) * slope(s.up_pre[k])).astype(BF)
        out.up_bias[k] = jnp.broadcast_to(colsum(up_grad.astype(F32)), (8, units))
        s.upg[...] = up_grad
        ups = [dot_tn(s.first[:, j * depth : (j + 1) * depth], s.upg[...]).astype(BF) for j in range(fold)]

        def store(which):
            out.grads[which][keep, depth:, :] = down
            for j in range(fold):
                out.grads[which][keep, :depth, j * units : (j + 1) * units] = ups[j]

        pl.when(k % 2 == 0)(lambda: store(0))
        pl.when(k % 2 == 1)(lambda: store(1))
        for j in range(fold):
            s.total[:, j * depth : (j + 1) * depth] += dot_nt(
                s.upg[...], s.three[k, :depth, j * units : (j + 1) * units]
            )
        return carry

    lax.fori_loop(0, peers, backward, 0)
    first_grad = s.total[...]
    out.sums[3:4, :] = colsum(first_grad * normed_ref[...])
    out.sums[4:5, :] = colsum(first_grad)
    out.mid_grad[...] = norm_back(first_grad, normed_ref[...], inv_ref[...], row(vec.first_gain))


def attend_back_one(peers, meta, second, mixed_ref, raw_ref, mid_ref, pre_ref, gate_ref, reset_ref, attended_ref, gated_ref, out, s):
    twos = weight_copies(meta, second, s.two, s.sem, 0)
    for copy in twos:
        copy.start()
    rows, wide = mixed_ref.shape
    width = wide // peers
    for b in range(peers):
        s.mixed[b] = mixed_ref[:, b * width : (b + 1) * width]
    mid, gate, pre = mid_ref[...], gate_ref[...], pre_ref[...]
    pre_grad = (mid * gate * slope(pre)).astype(BF)
    s.pre_grad[...] = pre_grad
    gate_grad = (mid * (pre * sigmoid(pre) - raw_ref[...].astype(F32)) * gate * (1.0 - gate)).astype(BF)
    s.gate_grad[...] = gate_grad
    out.direct[...] = mid * (1.0 - gate)
    out.sums[...] = jnp.zeros_like(out.sums)
    out.sums[0:1, :] = colsum(pre_grad.astype(F32))
    out.sums[1:2, :] = colsum(gate_grad.astype(F32))
    for copy in twos:
        copy.wait()

    def shard(k, carry):
        keep = k // 2
        s.block[...] = s.mixed[meta[0] ^ k]
        update = dot_tn(s.block[...], s.gate_grad[...]).astype(BF)
        mixer = dot_tn(s.block[...], s.pre_grad[...]).astype(BF)
        output = dot_tn(gated_ref[k], s.pre_grad[...]).astype(BF)

        def store(which):
            out.grads[which][keep, :width, :] = update
            out.grads[which][keep, width : 2 * width, :] = mixer
            out.grads[which][keep, 2 * width :, :] = output

        pl.when(k % 2 == 0)(lambda: store(0))
        pl.when(k % 2 == 1)(lambda: store(1))
        out.mixed_grad[k] = dot_nt(s.gate_grad[...], s.two[k, :width, :]) + dot_nt(
            s.pre_grad[...], s.two[k, width : 2 * width, :]
        )
        gated_grad = dot_nt(s.pre_grad[...], s.two[k, 2 * width :, :])
        reset = reset_ref[k]
        out.attend_grad[k] = (gated_grad * (reset * sigmoid(reset))).astype(BF)
        reset_grad = (gated_grad * attended_ref[k] * slope(reset)).astype(BF)
        out.reset_grad[k] = reset_grad
        out.bias[k] = jnp.broadcast_to(colsum(reset_grad.astype(F32)), (8, reset_grad.shape[1]))
        return carry

    lax.fori_loop(0, peers, shard, 0)


def attend_back_two(
    peers, meta, first, mixed_ref, raw_ref, value_pre_ref, values_ref, probs_ref, agrad_ref, rgrad_ref, direct_ref, local_ref,
    queries_ref, keys_ref, zeta_pre_ref, second_ref, out, s,
):
    vec = s.vec
    ones = weight_copies(meta, first, s.one, s.sem, 0)
    for copy in ones:
        copy.start()
    rows, wide = mixed_ref.shape
    width = wide // peers
    units = values_ref.shape[2]
    groups = rows // GROUP
    s.wait()
    act = zeta_pre_ref[...] * sigmoid(zeta_pre_ref[...])
    line = lax.broadcasted_iota(jnp.int32, (2 * GROUP, GROUP), 0)
    buckets = jnp.zeros((1, 2 * GROUP), F32)
    for g in range(groups):
        at = slice(g * GROUP, (g + 1) * GROUP)

        def score(k, total):
            return total + dot_nt(agrad_ref[k, at, :], values_ref[k, at, :])

        prob_grad = lax.fori_loop(0, peers, score, jnp.zeros((GROUP, GROUP), F32))
        probs = probs_ref[at, :]
        row_dot = jnp.sum(probs * prob_grad, axis=-1, keepdims=True)
        sgrad = (probs * (prob_grad - row_dot)).astype(BF)
        s.query_grad[at, :] = dot(sgrad, keys_ref[at, :]) * Z**-0.5
        s.key_grad[at, :] = dot_tn(sgrad, queries_ref[at, :]) * Z**-0.5
        ahead = positions_of(vec.positions, meta[0] * rows, g)
        ahead = ahead - ahead[:, 0:1]
        to_row = (line == ahead).astype(BF)
        to_column = (line == 2 * GROUP - 1 - ahead).astype(BF)
        table = dot(to_row, dot_nt(sgrad, to_column).astype(BF))
        buckets = buckets + colsum(pltpu.roll(table, 1, 1, stride=1, stride_axis=0))
    out.rel[...] = jnp.broadcast_to(buckets, (8, 2 * GROUP))
    query_grad, key_grad = s.query_grad[...], s.key_grad[...]
    zeta_grad = (query_grad * row(vec.query_gain) + key_grad * row(vec.key_gain)) * slope(zeta_pre_ref[...])
    zeta_grad = zeta_grad.astype(BF)
    out.sums[...] = jnp.zeros_like(out.sums)
    out.sums[0:1, :] = colsum(zeta_grad.astype(F32))
    out.sums[1:2, :] = colsum(query_grad * act)
    out.sums[2:3, :] = colsum(query_grad)
    out.sums[3:4, :] = colsum(key_grad * act)
    out.zeta[...] = dot_tn(mixed_ref[...], zeta_grad)
    s.mixed[...] = dot_nt(zeta_grad, vec.zeta[...])
    s.raw[...] = direct_ref[...]
    for copy in ones:
        copy.wait()

    def shard(k, carry):
        keep = k // 2
        for g in range(groups):
            at = slice(g * GROUP, (g + 1) * GROUP)
            vals_grad = dot_tn(probs_ref[at, :].astype(BF), agrad_ref[k, at, :])
            s.vgrad[at, :] = (vals_grad * slope(value_pre_ref[k, at, :])).astype(BF)
        out.bias[k] = jnp.broadcast_to(colsum(s.vgrad[...].astype(F32)), (8, units))
        reset = dot_tn(mixed_ref[...], rgrad_ref[k]).astype(BF)
        value = dot_tn(raw_ref[...], s.vgrad[...]).astype(BF)

        def store(which):
            out.grads[which][keep, :, :units] = reset
            out.grads[which][keep, :, units:] = value

        pl.when(k % 2 == 0)(lambda: store(0))
        pl.when(k % 2 == 1)(lambda: store(1))
        s.mixed[...] += dot_nt(rgrad_ref[k], s.one[k, :wide, :units])
        s.raw[...] += dot_nt(s.vgrad[...], s.one[k, :wide, units:])
        return carry

    lax.fori_loop(0, peers, shard, 0)
    for b in range(peers):
        at = slice(b * width, (b + 1) * width)
        s.mixed_out[b] = (s.mixed[:, at] + local_ref[meta[0] ^ b]).astype(BF)
        s.raw_out[b, :, :width] = s.raw[:, at].astype(BF)
        s.raw_out[b, :, width:] = second_ref[b]
    sends = []
    for k in range(peers):
        sends.append(pltpu.make_async_copy(s.mixed_out.at[meta[0] ^ k], out.m[k], s.sem.at[2 * k]))
        sends.append(pltpu.make_async_copy(s.raw_out.at[meta[0] ^ k], out.r[k], s.sem.at[2 * k + 1]))
    for copy in sends:
        copy.start()
    for copy in sends:
        copy.wait()


def swap(x, axis, by):
    size = lax.axis_size(axis)
    return lax.ppermute(x, axis, [(i, i ^ by) for i in range(size)])


def later_than(x, *marks):
    for mark in marks:
        x, mark.token = lax.optimization_barrier((x, mark.token))
    return x


def exchange(blocks, axis):
    return [blocks[0]] + [swap(blocks[k], axis, k) for k in range(1, len(blocks))]


def group_totals(total, fade, axis, reverse):
    result = []
    for bit in bits_of(lax.axis_size(axis)):
        other = swap(total, axis, bit)
        result.append(other)
        upper = ((lax.axis_index(axis) // bit) % 2) == (0 if reverse else 1)
        total = jnp.where(upper, total + fade * other, other + fade * total)
        fade = fade * fade
    return result


def far_pieces(pack):
    return [swap(pack.own, "wa", k) for k in range(2, lax.axis_size("wa"), 2)]


def next_pieces(came):
    return [swap(piece, "seq", j) for piece in came for j in range(1, 1 << SHARE_BITS)]


def all_shards(pack, came, beyond):
    others = (1 << SHARE_BITS) - 1
    shards = [[pack.packed]]
    shards += [[came[i]] + beyond[i * others : (i + 1) * others] for i in range(len(came))]
    return [pieces for even in shards for pieces in (even, [swap(piece, "wa", 1) for piece in even])]


def plus(a, b):
    return (a.astype(F32) + b.astype(F32)).astype(a.dtype)


def core_sums(grads, *deps):
    return plus(grads[0], later_than(swap(grads[1], "wa", 1), *deps))


def shard_sum(parts, *deps):
    step = 2
    while parts.shape[0] > 1:
        parts = plus(parts[::2], later_than(swap(parts[1::2], "wa", step), *deps))
        step *= 2
    return parts[0]


def keep_rows(total, bit, *deps):
    here = (lax.axis_index("seq") // bit) % 2
    height = total.shape[-2] // 2
    mine = lax.dynamic_slice_in_dim(total, here * height, height, total.ndim - 2)
    theirs = lax.dynamic_slice_in_dim(total, (1 - here) * height, height, total.ndim - 2)
    return plus(mine, later_than(swap(theirs, "seq", bit), *deps))


def all_rows(total, bits):
    for bit in bits[::-1]:
        here = (lax.axis_index("seq") // bit) % 2
        other = swap(total, "seq", bit)
        total = jnp.where(
            here == 0, jnp.concatenate([total, other], axis=0), jnp.concatenate([other, total], axis=0)
        )
    return total


def sum_small(exact, rough, route):
    for axis, bit in route:
        high = lax.reduce_precision(exact, 8, 7)
        sent = jnp.concatenate([high.astype(BF), (exact - high).astype(BF), rough.astype(BF)])
        total = sent.astype(F32) + swap(sent, axis, bit).astype(F32)
        rows = exact.shape[0]
        exact, rough = total[:rows] + total[rows : 2 * rows], total[2 * rows :]
    return exact, rough


def bits_of(size):
    return [1 << b for b in range(size.bit_length() - 1)]


def per_device(
    inputs, targets, lengths, positions, ema_decay, ema_feed, ema_read, ema_skip, zeta_proj, zeta_bias, query_gain, query_shift,
    key_gain, rel_bias, reset_proj, reset_bias, value_proj, value_bias, update_proj, update_bias, mixer_proj, output_proj,
    output_bias, first_gain, first_shift, up_proj, up_bias, down_proj, down_bias, second_gain, second_shift,
):
    seqs, seq_rows, width = inputs.shape
    wide = targets.shape[2]
    comps = ema_decay.shape[1]
    peers, ranks = lax.axis_size("wa"), lax.axis_size("seq")
    me, rank = lax.axis_index("wa"), lax.axis_index("seq")
    tok_rows = seqs * seq_rows
    rows = tok_rows // peers
    n_groups = rows // GROUP
    units, hidden = reset_proj.shape[1], up_proj.shape[1]
    fold = wide // hidden
    depth = wide // fold
    total_tokens = tok_rows * ranks
    groups = lane_groups(seqs, width)
    tiles = len(groups)
    pieces = 1 << SHARE_BITS
    place = rank % pieces
    meta = jnp.stack([me, place, rank]).astype(jnp.int32)
    hbm = pltpu.MemorySpace.HBM
    sems = pltpu.SemaphoreType.DMA

    def packed(kernel, shape, arrays, scratch=None, vectors=None, **outs):
        return run(
            functools.partial(kernel, pieces),
            [(meta, SMEM)] + [(a, VMEM) for a in arrays],
            Box(packed=(shape, BF, VMEM), own=((shape[0] // pieces,) + shape[1:], BF, VMEM), **outs),
            scratch or Box(),
            vectors=vectors,
        )

    one_shape, two_shape, three_shape = (wide + BIAS_ROWS, 2 * units), (2 * width + units, wide), (depth + hidden, wide)
    pack_one = packed(
        pack_first, one_shape, [reset_proj, value_proj, rel_bias],
        Box(rows=pltpu.VMEM((BIAS_ROWS, 2 * units), F32), bias=pltpu.VMEM((BIAS_ROWS, 2 * units), BF)),
        Box(reset=reset_bias, value=value_bias, up=up_bias), rel=((8, 2 * GROUP), F32, VMEM),
    )

    decay_rows, mix_rows = ema_decay.T, (ema_feed * ema_read).T
    skip_row = ema_skip[None, :]
    ends = run(
        functools.partial(ema_ends, groups, comps, peers),
        [(meta, SMEM), (inputs, VMEM), (decay_rows, VMEM)],
        Box(r=[((rows, width), BF, hbm)] * peers, before=((tiles, comps, CHUNKS, LANES), F32, VMEM), end=((tiles, comps, LANES), F32, VMEM), fade=((tiles, comps, LANES), F32, VMEM)),
        Box(x=pltpu.VMEM((tiles, seq_rows, LANES), F32), sem=sems((peers,))),
        after=[pack_one.own],
        hides=HIDE_ENDS,
    )
    def gate(*arrays):
        ends.token, *arrays = lax.optimization_barrier((ends.token,) + arrays)
        return arrays

    pack_two = packed(pack_second, two_shape, gate(update_proj, mixer_proj, output_proj))
    pack_three = packed(pack_third, three_shape, gate(up_proj, down_proj))
    came_one = [later_than(x, ends) for x in far_pieces(pack_one)]
    pack_two.own, came_one[0] = lax.optimization_barrier((pack_two.own, came_one[0]))
    came_two = far_pieces(pack_two)
    next_one = next_pieces(came_one)
    raw_blocks = exchange(ends.r, "wa")
    earlier = group_totals(ends.end, ends.fade, "seq", False)
    earlier[-1], *raw_blocks = lax.optimization_barrier((earlier[-1], *raw_blocks))
    outs = Box(
        value=((seqs, seq_rows, width), F32, VMEM),
        start=((tiles, comps, CHUNKS, LANES), F32, VMEM),
    )
    outs.m = [((rows, width), BF, hbm)] * peers
    ema = run(
        functools.partial(ema_values, groups, comps, peers),
        [(meta, SMEM), (inputs, VMEM), (decay_rows, VMEM), (mix_rows, VMEM), (skip_row, VMEM), (ends.before, VMEM), (earlier, VMEM)],
        outs,
        Box(
            x=pltpu.VMEM((tiles, seq_rows, LANES), F32),
            y=pltpu.VMEM((tiles, seq_rows, LANES), F32),
            mixed=pltpu.VMEM((tok_rows, width), BF),
            sem=sems((peers,)),
        ),
        after=came_two + next_one,
        hides=HIDE_VALUES,
    )
    mixed_blocks = exchange(ema.m, "wa")
    held = (pack_three.own, pack_one.packed, pack_two.packed, *mixed_blocks)
    pack_three.own, pack_one.packed, pack_two.packed, *mixed_blocks = lax.optimization_barrier(held)
    came_three = far_pieces(pack_three)
    shards_one = all_shards(pack_one, came_one, next_one)
    shards_two = all_shards(pack_two, came_two, next_pieces(came_two))
    shards_three = all_shards(pack_three, came_three, next_pieces(came_three))

    count = len(jax.tree.leaves(shards_one))
    vec = Box(
        zeta=zeta_proj, zeta_bias=zeta_bias, query_gain=query_gain, query_shift=query_shift,
        key_gain=key_gain, rel=pack_one.rel, positions=positions,
        output_bias=output_bias, update_bias=update_bias,
    )
    fwd = run(
        functools.partial(attend_forward, peers),
        [(meta, SMEM), (mixed_blocks, hbm), (raw_blocks, hbm), (shards_one, hbm), (shards_two, hbm)],
        Box(
            mixed=((rows, wide), BF, VMEM), raw=((rows, wide), BF, VMEM), zeta_pre=((rows, Z), F32, VMEM),
            queries=((rows, Z), BF, VMEM), keys=((rows, Z), BF, VMEM), probs=((rows, GROUP), F32, VMEM),
            reset_pre=((peers, rows, units), F32, VMEM), value_pre=((peers, rows, units), F32, VMEM),
            values=((peers, rows, units), BF, VMEM), attended=((peers, rows, units), F32, VMEM),
            gated=((peers, rows, units), BF, VMEM), out_pre=((rows, wide), F32, VMEM), gate=((rows, wide), F32, VMEM),
            normed=((rows, wide), F32, VMEM), inv=((rows, 1), F32, VMEM), up_bias=((peers, 8, units), F32, VMEM),
        ),
        Box(
            mixed=pltpu.VMEM((peers, rows, width), BF), raw=pltpu.VMEM((peers, rows, width), BF),
            one=pltpu.VMEM((peers,) + one_shape, BF), two=pltpu.VMEM((peers,) + two_shape, BF),
            pre=pltpu.VMEM((rows, wide), F32), gate=pltpu.VMEM((rows, wide), F32),
            sem=sems((2 * peers + 2 * count,)),
        ),
        vectors=vec,
        limit=62,
    )

    vec = Box(
        first_gain=first_gain, first_shift=first_shift, down_bias=down_bias,
        second_gain=second_gain, second_shift=second_shift, up_bias=fwd.up_bias,
    )
    outs = Box(
        mid_grad=((rows, wide), F32, VMEM), second=((peers, rows, width), BF, VMEM), sums=((8, wide), F32, VMEM), up_bias=((peers, 8, hidden), F32, VMEM),
        grads=[((peers // 2,) + three_shape, BF, VMEM)] * 2,
    )
    ffn = run(
        functools.partial(feed_forward, peers, ranks),
        [(meta, SMEM), (lengths, SMEM), (shards_three, hbm), (fwd.normed, VMEM), (fwd.inv, VMEM), (targets, hbm)],
        outs,
        Box(
            three=pltpu.VMEM((peers,) + three_shape, BF), first=pltpu.VMEM((rows, wide), BF),
            total=pltpu.VMEM((rows, wide), F32), up_pre=pltpu.VMEM((peers, rows, hidden), F32),
            act=pltpu.VMEM((peers, rows, hidden), BF), grad=pltpu.VMEM((rows, wide), BF),
            upg=pltpu.VMEM((rows, hidden), BF), sem=sems((count,)), targets=pltpu.VMEM((rows, wide), BF), target_sem=sems(()),
        ),
        vectors=vec,
    )
    row_bits = bits_of(ranks)
    third_parts = core_sums(ffn.grads)

    one = run(
        functools.partial(attend_back_one, peers),
        [(meta, SMEM), (shards_two, hbm), (fwd.mixed, VMEM), (fwd.raw, VMEM), (ffn.mid_grad, VMEM), (fwd.out_pre, VMEM),
         (fwd.gate, VMEM), (fwd.reset_pre, VMEM), (fwd.attended, VMEM), (fwd.gated, VMEM)],
        Box(
            direct=((rows, wide), F32, VMEM), sums=((8, wide), F32, VMEM), mixed_grad=((peers, rows, width), F32, VMEM),
            attend_grad=((peers, rows, units), BF, VMEM), reset_grad=((peers, rows, units), BF, VMEM),
            bias=((peers, 8, units), F32, VMEM),
            grads=[((peers // 2,) + two_shape, BF, VMEM)] * 2,
        ),
        Box(
            two=pltpu.VMEM((peers,) + two_shape, BF), mixed=pltpu.VMEM((peers, rows, width), BF),
            block=pltpu.VMEM((rows, width), BF), pre_grad=pltpu.VMEM((rows, wide), BF),
            gate_grad=pltpu.VMEM((rows, wide), BF), sem=sems((count,)),
        ),
        after=[third_parts],
        hides=HIDE_ONE,
    )
    vec = Box(
        zeta=zeta_proj, query_gain=query_gain, key_gain=key_gain, positions=positions,
    )
    outs = Box(
        rel=((8, 2 * GROUP), F32, VMEM), sums=((8, Z), F32, VMEM), zeta=((wide, Z), F32, VMEM),
        bias=((peers, 8, units), F32, VMEM),
        grads=[((peers // 2, wide, 2 * units), BF, VMEM)] * 2,
    )
    outs.m = [((rows, width), BF, hbm)] * peers
    outs.r = [((rows, 2 * width), BF, hbm)] * peers
    two = run(
        functools.partial(attend_back_two, peers),
        [(meta, SMEM), (shards_one, hbm), (fwd.mixed, VMEM), (fwd.raw, VMEM), (fwd.value_pre, VMEM), (fwd.values, VMEM),
         (fwd.probs, VMEM), (one.attend_grad, VMEM), (one.reset_grad, VMEM), (one.direct, VMEM), (one.mixed_grad, VMEM),
         (fwd.queries, VMEM), (fwd.keys, VMEM), (fwd.zeta_pre, VMEM), (ffn.second, VMEM)],
        outs,
        Box(
            one=pltpu.VMEM((peers,) + one_shape, BF), query_grad=pltpu.VMEM((rows, Z), F32),
            key_grad=pltpu.VMEM((rows, Z), F32), mixed=pltpu.VMEM((rows, wide), F32), raw=pltpu.VMEM((rows, wide), F32),
            vgrad=pltpu.VMEM((rows, units), BF), mixed_out=pltpu.VMEM((peers, rows, width), BF),
            raw_out=pltpu.VMEM((peers, rows, 2 * width), BF), sem=sems((max(count, 2 * peers),)),
        ),
        vectors=vec,
    )
    grad_blocks = exchange(two.m, "wa")
    rest_blocks = exchange(two.r, "wa")
    third_rows = keep_rows(third_parts, row_bits[0], two)
    mark = beside(HIDE_TWO, two.rel)
    second_parts = core_sums(one.grads, mark)
    first_parts = core_sums(two.grads, mark)

    back = run(
        functools.partial(ema_back_ends, groups, comps, peers),
        [(meta, SMEM), (grad_blocks, hbm), (ema.value, VMEM), (decay_rows, VMEM)],
        Box(
            grad=((tiles, seq_rows, LANES), F32, VMEM), after=((tiles, comps, CHUNKS, LANES), F32, VMEM),
            first=((tiles, comps, LANES), F32, VMEM),
        ),
        Box(grad=pltpu.VMEM((tok_rows, width), BF), sem=sems((peers,))),
        after=[second_parts, first_parts],
        hides=HIDE_BACK,
    )
    later = group_totals(back.first, ends.fade, "seq", True)
    second_sum = shard_sum(second_parts)
    third_sum = shard_sum(third_rows, back)
    first_sum = keep_rows(first_parts, row_bits[0])
    last = run(
        functools.partial(ema_back, groups, comps, peers),
        [(meta, SMEM), (inputs, VMEM), (back.grad, VMEM), (rest_blocks, hbm), (decay_rows, VMEM), (mix_rows, VMEM), (skip_row, VMEM),
         (ema.start, VMEM), (back.after, VMEM), (later, VMEM)],
        Box(grad=((seqs, seq_rows, width), F32, VMEM), block=((seqs, seq_rows, width), BF, VMEM), sums=((2 * comps + 8, width), F32, VMEM)),
        Box(
            x=pltpu.VMEM((tiles, seq_rows, LANES), F32), y=pltpu.VMEM((tiles, seq_rows, LANES), F32),
            states=pltpu.VMEM((seq_rows // CHUNKS, comps, CHUNKS, LANES), F32), rest=pltpu.VMEM((tok_rows, 2 * width), BF),
            sem=sems((peers,)),
        ),
        after=[second_sum, first_sum],
        hides=HIDE_LAST,
    )

    second_rows = keep_rows(second_sum, row_bits[0], last)
    third_sum = keep_rows(third_sum, row_bits[1], last)
    first_rows = shard_sum(first_sum, last)
    totals = []
    for rows_left, bits in ((third_sum, row_bits[2:]), (second_rows, row_bits[1:]), (first_rows, row_bits[1:])):
        for bit in bits:
            rows_left = keep_rows(rows_left, bit)
        totals.append(all_rows(rows_left, row_bits))
    third_total, second_total, first_total = totals
    shard_sums = jnp.stack([ffn.up_bias[:, 0], one.bias[:, 0], two.bias[:, 0]], axis=1)
    shard_sums = shard_sums[me ^ lax.iota(jnp.int32, peers)]
    shard_tall = 3 * peers * units // Z

    tall = 16 * wide // Z
    small = [
        jnp.concatenate([ffn.sums, one.sums], axis=0).reshape(tall, Z), two.sums, two.rel.reshape(16, Z),
        shard_sums.reshape(shard_tall, Z),
    ]
    small += [mark.token, two.token, back.token, ema.token, ends.token, last.token]
    small.append(jnp.zeros((-sum(part.shape[0] for part in small) % 16, Z), F32))
    small = jnp.concatenate(small, axis=0)
    small, zeta_grad = sum_small(small, two.zeta, [("wa", bit) for bit in bits_of(peers)])
    count = small.shape[0]
    small = jnp.concatenate([small, last.sums.reshape(-1, Z)])
    small, zeta_grad = sum_small(small, zeta_grad, [("seq", bit) for bit in row_bits])
    ema_sums = small[count:].reshape(last.sums.shape)
    decay_grad = ema_sums[:comps].T * (ema_feed * ema_read)
    moment = ema_sums[comps : 2 * comps].T
    feed_grad, read_grad = moment * ema_read, moment * ema_feed
    skip_grad = ema_sums[2 * comps]

    lines = small[:tall].reshape(16, wide)
    zsums = small[tall : tall + 8]
    rel_grad = small[tall + 8 : tall + 10].reshape(2 * GROUP)[: rel_bias.shape[0]]
    shard_sums = small[tall + 24 : tall + 24 + shard_tall].reshape(peers, 3, units)[me]

    up_grad = jnp.concatenate([third_total[:depth, j * hidden : (j + 1) * hidden] for j in range(fold)], axis=0)
    return (
        last.block, last.grad, lines[5, 0] + last.token[0, 0], decay_grad, feed_grad, read_grad, skip_grad, zeta_grad, zsums[0], zsums[1], zsums[2],
        zsums[3], rel_grad, first_total[:, :units].astype(F32), shard_sums[1], first_total[:, units:].astype(F32), shard_sums[2],
        second_total[:width].astype(F32), lines[9], second_total[width : 2 * width].astype(F32), second_total[2 * width :].astype(F32), lines[8], lines[3],
        lines[4], up_grad.astype(F32), shard_sums[0], third_total[depth:].astype(F32), lines[2], lines[0], lines[1],
    )


def solution(mesh):
    return jax.shard_map(
        per_device,
        mesh=mesh,
        in_specs=(
            P(None, "seq", "wa"), P(None, "seq", None), P(), P(None, "seq"), P("wa", None), P("wa", None), P("wa", None), P("wa"),
            P(), P(), P(), P(), P(), P(), P(None, "wa"), P("wa"), P(None, "wa"), P("wa"), P("wa", None), P(), P("wa", None),
            P("wa", None), P(), P(), P(), P(None, "wa"), P("wa"), P("wa", None), P(), P(), P(),
        ),
        out_specs=(
            P(None, "seq", "wa"), P(None, "seq", "wa"), P(), P("wa", None), P("wa", None), P("wa", None), P("wa"), P(), P(), P(),
            P(), P(), P(), P(None, "wa"), P("wa"), P(None, "wa"), P("wa"), P("wa", None), P(), P("wa", None), P("wa", None), P(),
            P(), P(), P(None, "wa"), P("wa"), P("wa", None), P(), P(), P(),
        ),
        check_vma=False,
    )
```

```python
import functools

import jax
import jax.numpy as jnp
from jax import lax
from jax.experimental import pallas as pl
from jax.experimental.pallas import tpu as pltpu
from jax.sharding import PartitionSpec as P

Z = 128
GROUP = 128
LANES = 128
CHUNKS = 8
BIAS_ROWS = 32
HIDE_ENDS, HIDE_VALUES, HIDE_ONE, HIDE_TWO, HIDE_BACK, HIDE_LAST = 20, 20, 20, 40, 60, 15
SHARE_BITS = 1
EPSILON = 1e-05
BF = jnp.bfloat16
F32 = jnp.float32
VMEM = pltpu.MemorySpace.VMEM
SMEM = pltpu.MemorySpace.SMEM


def dot(a, b):
    return jnp.dot(a, b, preferred_element_type=F32)


def dot_nt(a, b):
    return lax.dot_general(a, b, (((1,), (1,)), ((), ())), preferred_element_type=F32)


def dot_tn(a, b):
    return lax.dot_general(a, b, (((0,), (0,)), ((), ())), preferred_element_type=F32)


def sigmoid(v):
    return 1.0 / (1.0 + jnp.exp(-v))


def slope(v):
    s = sigmoid(v)
    return s * (1.0 + v * (1.0 - s))


def row(ref):
    return ref[...].reshape(1, ref.shape[0])


def put_line(ref, at, line):
    for j in range(0, line.shape[1], LANES):
        piece = line[:, j : j + LANES]
        ref[at + j // LANES : at + j // LANES + 1, : piece.shape[1]] = piece


def colsum(v):
    return jnp.sum(v, axis=0, keepdims=True)


def normalise(v):
    center = v - jnp.mean(v, axis=-1, keepdims=True)
    inv = lax.rsqrt(jnp.mean(center * center, axis=-1, keepdims=True) + EPSILON)
    return center * inv, inv


def norm_back(grad, normed, inv, gain):
    scaled = grad * gain
    one = jnp.mean(scaled, axis=-1, keepdims=True)
    two = jnp.mean(scaled * normed, axis=-1, keepdims=True)
    return inv * (scaled - one - normed * two)


class Box:
    def __init__(self, **parts):
        self.__dict__.update(parts)


jax.tree_util.register_pytree_node(
    Box, lambda box: (tuple(vars(box).values()), tuple(vars(box))), lambda names, parts: Box(**dict(zip(names, parts)))
)


def whole(space=VMEM):
    return pl.BlockSpec(memory_space=space)


def run(kernel, ins, outs, scratch, after=(), vectors=None, limit=48, hides=0):
    body, count = kernel, len(ins)
    vectors = vectors or Box()
    outs.token = ((8, LANES), F32, VMEM)
    fetched = len(vars(vectors))
    ins = ins + [(vectors, pltpu.MemorySpace.HBM), (list(after), pl.ANY)]
    scratch = Box(
        body=scratch, vec=jax.tree.map(lambda a: pltpu.VMEM(a.shape, a.dtype), vectors),
        sem=pltpu.SemaphoreType.DMA((max(fetched, 1),)),
    )

    def kernel(*refs):
        hbm, out, s = refs[count], refs[count + 2], refs[count + 3]
        copies = [
            pltpu.make_async_copy(vars(hbm)[name], vars(s.vec)[name], s.sem.at[i]) for i, name in enumerate(vars(hbm))
        ]
        for copy in copies:
            copy.start()
        if fetched:
            s.body.vec = s.vec
            s.body.wait = lambda: [copy.wait() for copy in copies]
        out.token[...] = jnp.zeros_like(out.token)
        body(*refs[:count], out, s.body)

    specs = [jax.tree.map(lambda _, space=space: whole(space), tree) for tree, space in ins]
    trees = [tree for tree, _ in ins]
    leaf = lambda entry: isinstance(entry, tuple)
    shapes = jax.tree.map(lambda e: jax.ShapeDtypeStruct(e[0], e[1]), outs, is_leaf=leaf)
    out_specs = jax.tree.map(lambda e: whole(e[2]), outs, is_leaf=leaf)
    return pl.pallas_call(
        kernel,
        out_shape=(shapes,),
        in_specs=specs,
        out_specs=(out_specs,),
        scratch_shapes=[scratch],
        compiler_params=pltpu.CompilerParams(vmem_limit_bytes=limit * 2**20),
        cost_estimate=pl.CostEstimate(flops=1 + int(hides * 1.15e9), bytes_accessed=1, transcendentals=0),
    )(*trees)[0]


def beside(hides, *deps):
    def kernel(ins, out, s):
        pass

    return run(kernel, [(list(deps), pl.ANY)], Box(), Box(), hides=hides)


def pack(pieces, meta, regions, out):
    height = out.own.shape[0]
    for ref, at, rows, top, left in regions:
        out.packed[top : top + rows, left : left + ref.shape[1]] = ref[at : at + rows, :]

    def piece(j):
        for ref, at, rows, top, left in regions:
            low, high = max(top, j * height), min(top + rows, (j + 1) * height)
            if low < high:
                out.own[low - j * height : high - j * height, left : left + ref.shape[1]] = ref[at + low - top : at + high - top, :]

    for j in range(pieces):
        pl.when(meta[1] == j)(lambda j=j: piece(j))


def pack_first(pieces, meta, reset, value, rel, out, s):
    units = reset.shape[1]
    s.wait()
    s.rows[...] = jnp.zeros_like(s.rows)
    for left, ref in ((0, s.vec.reset), (units, s.vec.value)):
        rest = row(ref)
        for i in range(3):
            high = rest.astype(BF).astype(F32)
            s.rows[i : i + 1, left : left + units] = high
            rest = rest - high
    s.rows[3:4, :units] = row(s.vec.up).astype(F32)
    s.bias[...] = s.rows[...].astype(BF)
    out.rel[...] = jnp.zeros_like(out.rel)
    out.rel[0:1, : rel.shape[0]] = row(rel)
    wide = reset.shape[0]
    pack(pieces, meta, [(reset, 0, wide, 0, 0), (value, 0, wide, 0, units), (s.bias, 0, BIAS_ROWS, wide, 0)], out)


def pack_second(pieces, meta, update, mixer, output, out, s):
    width, units = update.shape[0], output.shape[0]
    pack(pieces, meta, [(update, 0, width, 0, 0), (mixer, 0, width, width, 0), (output, 0, units, 2 * width, 0)], out)


def pack_third(pieces, meta, up, down, out, s):
    hidden = up.shape[1]
    depth = up.shape[0] // (down.shape[1] // hidden)
    regions = [(up, at, depth, 0, at // depth * hidden) for at in range(0, up.shape[0], depth)]
    pack(pieces, meta, regions + [(down, 0, hidden, depth, 0)], out)


def lane_groups(seqs, width):
    groups = []
    rest = width % LANES
    for s in range(seqs):
        for c in range(0, width - rest, LANES):
            groups.append([(s, c, LANES, 0)])
    tile, lane = [], 0
    for s in range(seqs if rest else 0):
        if lane + rest > LANES:
            groups.append(tile)
            tile, lane = [], 0
        tile.append((s, width - rest, rest, lane))
        lane += rest
    if tile:
        groups.append(tile)
    return groups


def join(parts):
    rows = parts[0].shape[0]
    used = sum(p.shape[1] for p in parts)
    if used < LANES:
        parts = parts + [jnp.zeros((rows, LANES - used), parts[0].dtype)]
    return parts[0] if len(parts) == 1 else jnp.concatenate(parts, axis=1)


def rows_of(group, ref):
    return join([ref[:, c : c + w] for _, c, w, _ in group])


def tokens_of(group, get):
    return join([get(s, c, w) for s, c, w, _ in group])


def spread(row):
    return jnp.broadcast_to(row, (CHUNKS, LANES))


def power(v, count):
    while count > 1:
        v = v * v
        count //= 2
    return v


def shifted(v, by):
    at = lax.broadcasted_iota(jnp.int32, v.shape, 0)
    moved = pltpu.roll(v, by % CHUNKS, 0)
    keep = at >= by if by > 0 else at < CHUNKS + by
    return jnp.where(keep, moved, 0.0)


def chunk_scan(ends, chunk_decay, sign):
    run_sum, factor, step = ends, chunk_decay, 1
    while step < CHUNKS:
        run_sum = run_sum + factor * shifted(run_sum, sign * step)
        factor, step = factor * factor, step * 2
    return run_sum, shifted(run_sum, sign)


def rank_power(chunk_decay, reverse):
    at = lax.broadcasted_iota(jnp.int32, chunk_decay.shape, 0)
    at = CHUNKS - 1 - at if reverse else at
    result, factor, bit = jnp.ones_like(chunk_decay), chunk_decay, 1
    while bit < CHUNKS:
        result = jnp.where((at & bit) != 0, result * factor, result)
        factor, bit = factor * factor, bit * 2
    return result


def steps_of(length, body, carry, reverse=False, unroll=4):
    def block(i, state):
        for u in range(unroll):
            t = i * unroll + u
            state = body(length - 1 - t if reverse else t, state)
        return state

    return lax.fori_loop(0, length // unroll, block, carry)


def at_step(ref, g, t, length):
    return ref.at[g, pl.ds(t, CHUNKS, stride=length), :]


def ema_ends(groups, comps, blocks, meta, x_ref, decay_ref, out, s):
    rows = x_ref.shape[1]
    part = x_ref.shape[0] * rows // blocks
    copies = []
    for k in range(blocks):
        at = (meta[0] ^ k) * part
        source = x_ref.at[at // rows, pl.ds(pl.multiple_of(at % rows, part), part), :]
        copies.append(pltpu.make_async_copy(source, out.r[k], s.sem.at[k]))
    for copy in copies:
        copy.start()
    length = x_ref.shape[1] // CHUNKS
    for g, group in enumerate(groups):
        s.x[g] = tokens_of(group, lambda q, c, w: x_ref[q, :, c : c + w].astype(F32))
        decay = rows_of(group, decay_ref)
        decays = [spread(decay[n : n + 1]) for n in range(comps)]

        def body(t, state):
            now = at_step(s.x, g, t, length)[...]
            return tuple(decays[n] * state[n] + now for n in range(comps))

        ends = steps_of(length, body, (jnp.zeros((CHUNKS, LANES), F32),) * comps)
        for n in range(comps):
            total, before = chunk_scan(ends[n], power(decays[n], length), 1)
            out.before[g, n] = before
            out.fade[g, n : n + 1, :] = power(decay[n : n + 1], length * CHUNKS)
            out.end[g, n : n + 1, :] = total[CHUNKS - 1 :]
    for copy in copies:
        copy.wait()


def carried(parts, device_decay, rank, reverse):
    total, passed = jnp.zeros_like(device_decay), jnp.ones_like(device_decay)
    for i, part in enumerate(parts):
        counts = ((rank // (1 << i)) % 2) == (0 if reverse else 1)
        total = jnp.where(counts, total + passed * part, total)
        passed = jnp.where(counts, passed * device_decay, passed)
        device_decay = device_decay * device_decay
    return total


def ema_values(groups, comps, blocks, meta, x_ref, decay_ref, mix_ref, skip_ref, before_ref, got, out, s):
    length = x_ref.shape[1] // CHUNKS
    width = x_ref.shape[2]
    seqs, rows = x_ref.shape[0], x_ref.shape[1]
    for g, group in enumerate(groups):
        s.x[g] = tokens_of(group, lambda q, c, w: x_ref[q, :, c : c + w].astype(F32))
        decay, mix, skip = rows_of(group, decay_ref), rows_of(group, mix_ref), rows_of(group, skip_ref)
        decays = [spread(decay[n : n + 1]) for n in range(comps)]
        mixes = [spread(mix[n : n + 1]) for n in range(comps)]
        skip = spread(skip)
        state_in = carried([part[g] for part in got], power(decay, length * CHUNKS), meta[2], False)
        start = []
        for n in range(comps):
            ranks = rank_power(power(decays[n], length), False)
            start.append(before_ref[g, n] + ranks * spread(state_in[n : n + 1]))
            out.start[g, n] = start[n]

        def body(t, state):
            now = at_step(s.x, g, t, length)[...]
            state = tuple(decays[n] * state[n] + now for n in range(comps))
            terms = [mixes[n] * state[n] for n in range(comps)] + [skip * now]
            while len(terms) > 1:
                terms = [a + b for a, b in zip(terms[::2], terms[1::2])] + (terms[-1:] if len(terms) % 2 else [])
            at_step(s.y, g, t, length)[...] = terms[0]
            return state

        steps_of(length, body, tuple(start))
        for q, c, w, lane in group:
            value = s.y[g, :, lane : lane + w]
            out.value[q, :, c : c + w] = value
            s.mixed[pl.ds(q * rows, rows), c : c + w] = (value * sigmoid(value)).astype(BF)
    part = seqs * rows // blocks
    copies = [
        pltpu.make_async_copy(
            s.mixed.at[pl.ds(pl.multiple_of((meta[0] ^ k) * part, part), part), :], out.m[k], s.sem.at[k]
        )
        for k in range(blocks)
    ]
    for copy in copies:
        copy.start()
    for copy in copies:
        copy.wait()


def ema_back_ends(groups, comps, blocks, meta, grads, value_ref, decay_ref, out, s):
    length = value_ref.shape[1] // CHUNKS
    rows = value_ref.shape[1]
    part = value_ref.shape[0] * rows // blocks
    copies = [
        pltpu.make_async_copy(
            grads[k], s.grad.at[pl.ds(pl.multiple_of((meta[0] ^ k) * part, part), part), :], s.sem.at[k]
        )
        for k in range(blocks)
    ]
    for copy in copies:
        copy.start()
    for copy in copies:
        copy.wait()
    for g, group in enumerate(groups):

        def load(q, c, w):
            return s.grad[pl.ds(q * rows, rows), c : c + w].astype(F32) * slope(value_ref[q, :, c : c + w])

        out.grad[g] = tokens_of(group, load)
        decay = rows_of(group, decay_ref)
        decays = [spread(decay[n : n + 1]) for n in range(comps)]

        def body(t, state):
            now = at_step(out.grad, g, t, length)[...]
            return tuple(decays[n] * state[n] + now for n in range(comps))

        ends = steps_of(length, body, (jnp.zeros((CHUNKS, LANES), F32),) * comps, reverse=True)
        for n in range(comps):
            total, after = chunk_scan(ends[n], power(decays[n], length), -1)
            out.after[g, n] = after
            out.first[g, n : n + 1, :] = total[:1]


def ema_join(groups, blocks, meta, part_ref, rests, out, s):
    seqs, rows, width = out.grad.shape
    part = seqs * rows // blocks
    copies = [
        pltpu.make_async_copy(
            rests[k], s.rest.at[pl.ds(pl.multiple_of((meta[0] ^ k) * part, part), part), :], s.sem.at[k]
        )
        for k in range(blocks)
    ]
    for copy in copies:
        copy.start()
    for copy in copies:
        copy.wait()
    for q in range(seqs):
        out.block[q] = s.rest[pl.ds(q * rows, rows), width:]
    for g, group in enumerate(groups):
        for q, c, w, lane in group:
            rest = s.rest[pl.ds(q * rows, rows), c : c + w].astype(F32)
            out.grad[q, :, c : c + w] = part_ref[g, :, lane : lane + w] + rest


def ema_back(groups, comps, meta, x_ref, grad_ref, decay_ref, mix_ref, skip_ref, start_ref, after_ref, got, out, s):
    length = x_ref.shape[1] // CHUNKS
    out.sums[...] = jnp.zeros_like(out.sums)
    half = comps // 2
    for g, group in enumerate(groups):
        s.x[g] = tokens_of(group, lambda q, c, w: x_ref[q, :, c : c + w].astype(F32))
        decay, mix, skip = rows_of(group, decay_ref), rows_of(group, mix_ref), rows_of(group, skip_ref)
        decays = [spread(decay[n : n + 1]) for n in range(comps)]
        mixes = [spread(mix[n : n + 1]) for n in range(comps)]
        skip = spread(skip)

        def forward(t, state):
            now = at_step(s.x, g, t, length)[...]
            for n in range(comps):
                s.states[t, n] = state[n]
            return tuple(decays[n] * state[n] + now for n in range(comps))

        steps_of(length, forward, tuple(start_ref[g, n] for n in range(comps)))
        grad_in = carried([p[g] for p in got], power(decay, length * CHUNKS), meta[2], True)
        for h in range(2):
            mine = range(h * half, (h + 1) * half)
            begin = []
            for n in mine:
                ranks = rank_power(power(decays[n], length), True)
                begin.append(after_ref[g, n] + ranks * spread(grad_in[n : n + 1]))
            zero = (jnp.zeros((CHUNKS, LANES), F32),) * half

            def backward(t, carry):
                grads, moments, changes, skips = carry
                now, up = at_step(s.x, g, t, length)[...], at_step(grad_ref, g, t, length)[...]
                grads = tuple(decays[n] * grads[i] + up for i, n in enumerate(mine))
                moments = tuple(moments[i] + grads[i] * now for i in range(half))
                changes = tuple(changes[i] + grads[i] * s.states[t, n] for i, n in enumerate(mine))
                terms = [mixes[n] * grads[i] for i, n in enumerate(mine)]
                if h == 0:
                    terms.append(skip * up)
                    skips = skips + up * now
                else:
                    terms.append(at_step(out.part, g, t, length)[...])
                while len(terms) > 1:
                    terms = [a + b for a, b in zip(terms[::2], terms[1::2])] + (terms[-1:] if len(terms) % 2 else [])
                at_step(out.part, g, t, length)[...] = terms[0]
                return grads, moments, changes, skips

            _, moments, changes, skips = steps_of(length, backward, (tuple(begin), zero, zero, zero[0]), reverse=True, unroll=2)
            for q, c, w, lane in group:
                for i, n in enumerate(mine):
                    out.sums[c // LANES, n : n + 1, :w] += colsum(changes[i])[:, lane : lane + w]
                    out.sums[c // LANES, comps + n : comps + n + 1, :w] += colsum(moments[i])[:, lane : lane + w]
                if h == 0:
                    out.sums[c // LANES, 2 * comps : 2 * comps + 1, :w] += colsum(skips)[:, lane : lane + w]


def weight_copies(meta, shards, dst, sem, first):
    copies = []
    for k, pieces in enumerate(shards):
        height = dst.shape[1] // len(pieces)
        for j, piece in enumerate(pieces):
            target = dst.at[k]
            if len(pieces) > 1:
                target = dst.at[k, pl.ds(pl.multiple_of((meta[1] ^ j) * height, height), height), :]
            copies.append(pltpu.make_async_copy(piece, target, sem.at[first + len(copies)]))
    return copies


def block_copies(meta, blocks, dst, sem, first):
    return [
        pltpu.make_async_copy(block, dst.at[meta[0] ^ k], sem.at[first + k]) for k, block in enumerate(blocks)
    ]


def positions_of(ref, start, g):
    at = start + g * GROUP
    length = ref.shape[1]
    columns = pl.ds(pl.multiple_of(at % length, GROUP), GROUP)
    place = ref[0:1, columns]
    for q in range(1, ref.shape[0]):
        place = jnp.where(at // length == q, ref[q : q + 1, columns], place)
    return place


def attend_forward(peers, meta, mixed, raw, first, second, out, s):
    vec = s.vec
    blocks = block_copies(meta, mixed, s.mixed, s.sem, 0)
    blocks += block_copies(meta, raw, s.raw, s.sem, peers)
    ones = weight_copies(meta, first, s.one, s.sem, 2 * peers)
    twos = weight_copies(meta, second, s.two, s.sem, 2 * peers + len(ones))
    for copy in blocks + ones + twos:
        copy.start()
    for copy in blocks:
        copy.wait()
    width = s.mixed.shape[2]
    units = s.one.shape[2] // 2
    rows, wide = out.mixed.shape
    groups = rows // GROUP
    for b in range(peers):
        out.mixed[:, b * width : (b + 1) * width] = s.mixed[b]
        out.raw[:, b * width : (b + 1) * width] = s.raw[b]
    s.wait()
    zeta_pre = dot(out.mixed[...], vec.zeta[...]) + row(vec.zeta_bias)
    out.zeta_pre[...] = zeta_pre
    act = zeta_pre * sigmoid(zeta_pre)
    queries = (act * row(vec.query_gain) + row(vec.query_shift)).astype(BF)
    keys = (act * row(vec.key_gain)).astype(BF)
    out.queries[...] = queries
    out.keys[...] = keys
    causal = lax.broadcasted_iota(jnp.int32, (GROUP, GROUP), 0) >= lax.broadcasted_iota(jnp.int32, (GROUP, GROUP), 1)
    for g in range(groups):
        at = slice(g * GROUP, (g + 1) * GROUP)
        place = jnp.broadcast_to(positions_of(vec.positions, meta[0] * rows, g).astype(F32), (GROUP, GROUP))
        distance = jnp.clip((place.T - place).astype(jnp.int32), 0, 2 * GROUP - 2)
        low = jnp.take_along_axis(
            jnp.broadcast_to(vec.rel[0:1, :GROUP], (GROUP, GROUP)), distance & (GROUP - 1), axis=1
        )
        high = jnp.take_along_axis(
            jnp.broadcast_to(vec.rel[0:1, GROUP:], (GROUP, GROUP)), distance & (GROUP - 1), axis=1
        )
        scores = dot_nt(queries[at], keys[at]) * Z**-0.5 + jnp.where(distance < GROUP, low, high)
        scores = jnp.where(causal, scores, -jnp.inf)
        shifted_exp = jnp.exp(scores - jnp.max(scores, axis=-1, keepdims=True))
        out.probs[at, :] = shifted_exp / jnp.sum(shifted_exp, axis=-1, keepdims=True)
    for copy in ones:
        copy.wait()
    for copy in twos:
        copy.wait()
    s.pre[...] = jnp.zeros_like(s.pre)
    s.gate[...] = jnp.zeros_like(s.gate)

    def shard(k, carry):
        biases = s.one[k, wide : wide + 16, :].astype(F32)
        bias = biases[0:1] + biases[1:2] + biases[2:3]
        out.up_bias[k] = jnp.broadcast_to(biases[3:4, :units], (8, units))
        reset_pre = dot(out.mixed[...], s.one[k, :wide, :units]) + bias[:, :units]
        value_pre = dot(out.raw[...], s.one[k, :wide, units:]) + bias[:, units:]
        values = (value_pre * sigmoid(value_pre)).astype(BF)
        out.reset_pre[k] = reset_pre
        out.value_pre[k] = value_pre
        out.values[k] = values
        for g in range(groups):
            at = slice(g * GROUP, (g + 1) * GROUP)
            out.attended[k, at, :] = dot(out.probs[at, :].astype(BF), values[at])
        gated = (reset_pre * sigmoid(reset_pre) * out.attended[k]).astype(BF)
        out.gated[k] = gated
        block = s.mixed[meta[0] ^ k]
        s.gate[...] += dot(block, s.two[k, :width, :])
        s.pre[...] += dot(block, s.two[k, width : 2 * width, :]) + dot(gated, s.two[k, 2 * width :, :])
        return carry

    lax.fori_loop(0, peers, shard, 0)
    out_pre = s.pre[...] + row(vec.output_bias)
    out.out_pre[...] = out_pre
    gate = sigmoid(s.gate[...] + row(vec.update_bias))
    out.gate[...] = gate
    mid = gate * (out_pre * sigmoid(out_pre)) + (1.0 - gate) * out.raw[...].astype(F32)
    normed, inv = normalise(mid)
    out.normed[...] = normed
    out.inv[...] = inv


def feed_forward(peers, ranks, meta, lengths, third, normed_ref, inv_ref, targets, out, s):
    vec = s.vec
    rows = normed_ref.shape[0]
    seqs, seq_rows = targets.shape[0], targets.shape[1]
    seq, offset = meta[0] * rows // seq_rows, pl.multiple_of(meta[0] * rows % seq_rows, rows)
    fetch = pltpu.make_async_copy(targets.at[seq, pl.ds(offset, rows), :], s.targets, s.target_sem)
    fetch.start()
    threes = weight_copies(meta, third, s.three, s.sem, 0)
    for copy in threes:
        copy.start()
    rows, width = normed_ref.shape
    s.wait()
    units = vec.up_bias.shape[2]
    fold = width // units
    depth = width // fold
    first = normed_ref[...] * row(vec.first_gain) + row(vec.first_shift)
    s.first[...] = first.astype(BF)
    s.total[...] = first + row(vec.down_bias)
    for copy in threes:
        copy.wait()

    def forward(k, carry):
        pre = vec.up_bias[k, 0:1, :]
        for j in range(fold):
            pre = pre + dot(
                s.first[:, j * depth : (j + 1) * depth], s.three[k, :depth, j * units : (j + 1) * units]
            )
        s.up_pre[k] = pre
        act = (pre * sigmoid(pre)).astype(BF)
        s.act[k] = act
        s.total[...] += dot(act, s.three[k, depth:, :])
        return carry

    lax.fori_loop(0, peers, forward, 0)
    normed, inv = normalise(s.total[...])
    second = normed * row(vec.second_gain) + row(vec.second_shift)
    piece = width // peers
    for b in range(peers):
        out.second[b] = second[:, b * piece : (b + 1) * piece].astype(BF)
    fetch.wait()
    misfit = second - s.targets[...].astype(F32)
    place = lax.broadcasted_iota(jnp.int32, (rows, 1), 0) + (meta[2] * seq_rows + offset)
    weight = (place < lengths[seq]).astype(F32)
    tokens = lengths[0]
    for q in range(1, seqs):
        tokens = tokens + lengths[q]
    true_count = jnp.broadcast_to(tokens, (rows, 1)).astype(F32)
    losses = jnp.sum(misfit * misfit, axis=1, keepdims=True) * (weight / (2.0 * width * true_count))
    out.sums[...] = jnp.zeros_like(out.sums)
    out.up_bias[...] = jnp.zeros_like(out.up_bias)
    lines = width // LANES
    put_line(out.sums, 5 * lines, jnp.broadcast_to(jnp.sum(losses, axis=0, keepdims=True), (1, LANES)))
    grad_out = misfit * (weight * (seqs * seq_rows * ranks / true_count))
    put_line(out.sums, 0, colsum(grad_out * normed))
    put_line(out.sums, lines, colsum(grad_out))
    second_grad = norm_back(grad_out, normed, inv, row(vec.second_gain))
    ffn_grad = second_grad.astype(BF)
    s.grad[...] = ffn_grad
    put_line(out.sums, 2 * lines, colsum(ffn_grad.astype(F32)))
    s.total[...] = second_grad

    def backward(k, carry):
        keep = k // 2
        down = dot_tn(s.act[k], s.grad[...]).astype(BF)
        up_grad = (dot_nt(s.grad[...], s.three[k, depth:, :]) * slope(s.up_pre[k])).astype(BF)
        put_line(out.up_bias.at[meta[0] ^ k], 0, colsum(up_grad.astype(F32)))
        s.upg[...] = up_grad
        ups = [dot_tn(s.first[:, j * depth : (j + 1) * depth], s.upg[...]).astype(BF) for j in range(fold)]

        def store(which):
            out.grads[which][keep, depth:, :] = down
            for j in range(fold):
                out.grads[which][keep, :depth, j * units : (j + 1) * units] = ups[j]

        pl.when(k % 2 == 0)(lambda: store(0))
        pl.when(k % 2 == 1)(lambda: store(1))
        for j in range(fold):
            s.total[:, j * depth : (j + 1) * depth] += dot_nt(
                s.upg[...], s.three[k, :depth, j * units : (j + 1) * units]
            )
        return carry

    lax.fori_loop(0, peers, backward, 0)
    first_grad = s.total[...]
    put_line(out.sums, 3 * lines, colsum(first_grad * normed_ref[...]))
    put_line(out.sums, 4 * lines, colsum(first_grad))
    out.mid_grad[...] = norm_back(first_grad, normed_ref[...], inv_ref[...], row(vec.first_gain))


def attend_back_one(peers, meta, second, mixed_ref, raw_ref, mid_ref, pre_ref, gate_ref, reset_ref, attended_ref, gated_ref, out, s):
    twos = weight_copies(meta, second, s.two, s.sem, 0)
    for copy in twos:
        copy.start()
    rows, wide = mixed_ref.shape
    width = wide // peers
    for b in range(peers):
        s.mixed[b] = mixed_ref[:, b * width : (b + 1) * width]
    mid, gate, pre = mid_ref[...], gate_ref[...], pre_ref[...]
    pre_grad = (mid * gate * slope(pre)).astype(BF)
    s.pre_grad[...] = pre_grad
    gate_grad = (mid * (pre * sigmoid(pre) - raw_ref[...].astype(F32)) * gate * (1.0 - gate)).astype(BF)
    s.gate_grad[...] = gate_grad
    out.direct[...] = mid * (1.0 - gate)
    out.sums[...] = jnp.zeros_like(out.sums)
    out.bias[...] = jnp.zeros_like(out.bias)
    put_line(out.sums, 0, colsum(pre_grad.astype(F32)))
    put_line(out.sums, wide // LANES, colsum(gate_grad.astype(F32)))
    for copy in twos:
        copy.wait()

    def shard(k, carry):
        keep = k // 2
        s.block[...] = s.mixed[meta[0] ^ k]
        update = dot_tn(s.block[...], s.gate_grad[...]).astype(BF)
        mixer = dot_tn(s.block[...], s.pre_grad[...]).astype(BF)
        output = dot_tn(gated_ref[k], s.pre_grad[...]).astype(BF)

        def store(which):
            out.grads[which][keep, :width, :] = update
            out.grads[which][keep, width : 2 * width, :] = mixer
            out.grads[which][keep, 2 * width :, :] = output

        pl.when(k % 2 == 0)(lambda: store(0))
        pl.when(k % 2 == 1)(lambda: store(1))
        out.mixed_grad[k] = dot_nt(s.gate_grad[...], s.two[k, :width, :]) + dot_nt(
            s.pre_grad[...], s.two[k, width : 2 * width, :]
        )
        gated_grad = dot_nt(s.pre_grad[...], s.two[k, 2 * width :, :])
        reset = reset_ref[k]
        out.attend_grad[k] = (gated_grad * (reset * sigmoid(reset))).astype(BF)
        reset_grad = (gated_grad * attended_ref[k] * slope(reset)).astype(BF)
        out.reset_grad[k] = reset_grad
        put_line(out.bias.at[meta[0] ^ k], 0, colsum(reset_grad.astype(F32)))
        return carry

    lax.fori_loop(0, peers, shard, 0)


def attend_back_two(
    peers, meta, first, mixed_ref, raw_ref, value_pre_ref, values_ref, probs_ref, agrad_ref, rgrad_ref, direct_ref, local_ref,
    queries_ref, keys_ref, zeta_pre_ref, second_ref, out, s,
):
    vec = s.vec
    ones = weight_copies(meta, first, s.one, s.sem, 0)
    for copy in ones:
        copy.start()
    rows, wide = mixed_ref.shape
    width = wide // peers
    units = values_ref.shape[2]
    groups = rows // GROUP
    s.wait()
    act = zeta_pre_ref[...] * sigmoid(zeta_pre_ref[...])
    line = lax.broadcasted_iota(jnp.int32, (2 * GROUP, GROUP), 0)
    buckets = jnp.zeros((1, 2 * GROUP), F32)
    for g in range(groups):
        at = slice(g * GROUP, (g + 1) * GROUP)

        def score(k, total):
            return total + dot_nt(agrad_ref[k, at, :], values_ref[k, at, :])

        prob_grad = lax.fori_loop(0, peers, score, jnp.zeros((GROUP, GROUP), F32))
        probs = probs_ref[at, :]
        row_dot = jnp.sum(probs * prob_grad, axis=-1, keepdims=True)
        sgrad = (probs * (prob_grad - row_dot)).astype(BF)
        s.query_grad[at, :] = dot(sgrad, keys_ref[at, :]) * Z**-0.5
        s.key_grad[at, :] = dot_tn(sgrad, queries_ref[at, :]) * Z**-0.5
        ahead = positions_of(vec.positions, meta[0] * rows, g)
        ahead = ahead - ahead[:, 0:1]
        to_row = (line == ahead).astype(BF)
        to_column = (line == 2 * GROUP - 1 - ahead).astype(BF)
        table = dot(to_row, dot_nt(sgrad, to_column).astype(BF))
        buckets = buckets + colsum(pltpu.roll(table, 1, 1, stride=1, stride_axis=0))
    out.rel[...] = jnp.zeros_like(out.rel)
    out.bias[...] = jnp.zeros_like(out.bias)
    put_line(out.rel, 0, buckets)
    query_grad, key_grad = s.query_grad[...], s.key_grad[...]
    zeta_grad = (query_grad * row(vec.query_gain) + key_grad * row(vec.key_gain)) * slope(zeta_pre_ref[...])
    zeta_grad = zeta_grad.astype(BF)
    out.sums[...] = jnp.zeros_like(out.sums)
    out.sums[0:1, :] = colsum(zeta_grad.astype(F32))
    out.sums[1:2, :] = colsum(query_grad * act)
    out.sums[2:3, :] = colsum(query_grad)
    out.sums[3:4, :] = colsum(key_grad * act)
    out.zeta[...] = dot_tn(mixed_ref[...], zeta_grad)
    s.mixed[...] = dot_nt(zeta_grad, vec.zeta[...])
    s.raw[...] = direct_ref[...]
    for copy in ones:
        copy.wait()

    def shard(k, carry):
        keep = k // 2
        for g in range(groups):
            at = slice(g * GROUP, (g + 1) * GROUP)
            vals_grad = dot_tn(probs_ref[at, :].astype(BF), agrad_ref[k, at, :])
            s.vgrad[at, :] = (vals_grad * slope(value_pre_ref[k, at, :])).astype(BF)
        put_line(out.bias.at[meta[0] ^ k], 0, colsum(s.vgrad[...].astype(F32)))
        reset = dot_tn(mixed_ref[...], rgrad_ref[k]).astype(BF)
        value = dot_tn(raw_ref[...], s.vgrad[...]).astype(BF)

        def store(which):
            out.grads[which][keep, :, :units] = reset
            out.grads[which][keep, :, units:] = value

        pl.when(k % 2 == 0)(lambda: store(0))
        pl.when(k % 2 == 1)(lambda: store(1))
        s.mixed[...] += dot_nt(rgrad_ref[k], s.one[k, :wide, :units])
        s.raw[...] += dot_nt(s.vgrad[...], s.one[k, :wide, units:])
        return carry

    lax.fori_loop(0, peers, shard, 0)
    for b in range(peers):
        at = slice(b * width, (b + 1) * width)
        s.mixed_out[b] = (s.mixed[:, at] + local_ref[meta[0] ^ b]).astype(BF)
        s.raw_out[b, :, :width] = s.raw[:, at].astype(BF)
        s.raw_out[b, :, width:] = second_ref[b]
    sends = []
    for k in range(peers):
        sends.append(pltpu.make_async_copy(s.mixed_out.at[meta[0] ^ k], out.m[k], s.sem.at[2 * k]))
        sends.append(pltpu.make_async_copy(s.raw_out.at[meta[0] ^ k], out.r[k], s.sem.at[2 * k + 1]))
    for copy in sends:
        copy.start()
    for copy in sends:
        copy.wait()


def swap(x, axis, by):
    size = lax.axis_size(axis)
    return lax.ppermute(x, axis, [(i, i ^ by) for i in range(size)])


def later_than(x, *marks):
    for mark in marks:
        x, mark.token = lax.optimization_barrier((x, mark.token))
    return x


def exchange(blocks, axis):
    return [blocks[0]] + [swap(blocks[k], axis, k) for k in range(1, len(blocks))]


def group_totals(total, fade, axis, reverse, nears=None):
    result = []
    for bit in bits_of(lax.axis_size(axis)):
        other = swap(total, axis, bit)
        if nears is not None:
            nears.append(beside(0, other))
            other, nears[-1].token = lax.optimization_barrier((other, nears[-1].token))
        result.append(other)
        upper = ((lax.axis_index(axis) // bit) % 2) == (0 if reverse else 1)
        total = jnp.where(upper, total + fade * other, other + fade * total)
        fade = fade * fade
    return result


def far_pieces(pack):
    return [swap(pack.own, "wa", k) for k in range(2, lax.axis_size("wa"), 2)]


def next_pieces(came):
    return [swap(piece, "seq", j) for piece in came for j in range(1, 1 << SHARE_BITS)]


def all_shards(pack, came, beyond):
    others = (1 << SHARE_BITS) - 1
    shards = [[pack.packed]]
    shards += [[came[i]] + beyond[i * others : (i + 1) * others] for i in range(len(came))]
    return [pieces for even in shards for pieces in (even, [swap(piece, "wa", 1) for piece in even])]


def plus(a, b):
    return (a.astype(F32) + b.astype(F32)).astype(a.dtype)


def core_sums(grads, *deps):
    return plus(grads[0], later_than(swap(grads[1], "wa", 1), *deps))


def shard_sum(parts, *deps):
    step = 2
    while parts.shape[0] > 1:
        parts = plus(parts[::2], later_than(swap(parts[1::2], "wa", step), *deps))
        step *= 2
    return parts[0]


def keep_rows(total, bit, *deps):
    here = (lax.axis_index("seq") // bit) % 2
    height = total.shape[-2] // 2
    mine = lax.dynamic_slice_in_dim(total, here * height, height, total.ndim - 2)
    theirs = lax.dynamic_slice_in_dim(total, (1 - here) * height, height, total.ndim - 2)
    return plus(mine, later_than(swap(theirs, "seq", bit), *deps))


def all_rows(total, bits, *deps):
    for bit in bits[::-1]:
        here = (lax.axis_index("seq") // bit) % 2
        other = later_than(swap(total, "seq", bit), *(deps if bit == bits[-1] else ()))
        total = jnp.where(
            here == 0, jnp.concatenate([total, other], axis=0), jnp.concatenate([other, total], axis=0)
        )
    return total


def sum_small(exact, rough, route):
    for axis, bit in route:
        high = lax.reduce_precision(exact, 8, 7)
        sent = jnp.concatenate([high.astype(BF), (exact - high).astype(BF), rough.astype(BF)])
        total = sent.astype(F32) + swap(sent, axis, bit).astype(F32)
        rows = exact.shape[0]
        exact, rough = total[:rows] + total[rows : 2 * rows], total[2 * rows :]
    return exact, rough


def bits_of(size):
    return [1 << b for b in range(size.bit_length() - 1)]


def per_device(
    inputs, targets, lengths, positions, ema_decay, ema_feed, ema_read, ema_skip, zeta_proj, zeta_bias, query_gain, query_shift,
    key_gain, rel_bias, reset_proj, reset_bias, value_proj, value_bias, update_proj, update_bias, mixer_proj, output_proj,
    output_bias, first_gain, first_shift, up_proj, up_bias, down_proj, down_bias, second_gain, second_shift,
):
    seqs, seq_rows, width = inputs.shape
    wide = targets.shape[2]
    comps = ema_decay.shape[1]
    peers, ranks = lax.axis_size("wa"), lax.axis_size("seq")
    me, rank = lax.axis_index("wa"), lax.axis_index("seq")
    tok_rows = seqs * seq_rows
    rows = tok_rows // peers
    n_groups = rows // GROUP
    units, hidden = reset_proj.shape[1], up_proj.shape[1]
    fold = wide // hidden
    depth = wide // fold
    total_tokens = tok_rows * ranks
    groups = lane_groups(seqs, width)
    tiles = len(groups)
    pieces = 1 << SHARE_BITS
    place = rank % pieces
    meta = jnp.stack([me, place, rank]).astype(jnp.int32)
    hbm = pltpu.MemorySpace.HBM
    sems = pltpu.SemaphoreType.DMA

    def packed(kernel, shape, arrays, scratch=None, vectors=None, **outs):
        return run(
            functools.partial(kernel, pieces),
            [(meta, SMEM)] + [(a, VMEM) for a in arrays],
            Box(packed=(shape, BF, VMEM), own=((shape[0] // pieces,) + shape[1:], BF, VMEM), **outs),
            scratch or Box(),
            vectors=vectors,
        )

    one_shape, two_shape, three_shape = (wide + BIAS_ROWS, 2 * units), (2 * width + units, wide), (depth + hidden, wide)
    pack_one = packed(
        pack_first, one_shape, [reset_proj, value_proj, rel_bias],
        Box(rows=pltpu.VMEM((BIAS_ROWS, 2 * units), F32), bias=pltpu.VMEM((BIAS_ROWS, 2 * units), BF)),
        Box(reset=reset_bias, value=value_bias, up=up_bias), rel=((8, 2 * GROUP), F32, VMEM),
    )

    decay_rows, mix_rows = ema_decay.T, (ema_feed * ema_read).T
    skip_row = ema_skip[None, :]
    ends = run(
        functools.partial(ema_ends, groups, comps, peers),
        [(meta, SMEM), (inputs, VMEM), (decay_rows, VMEM)],
        Box(r=[((rows, width), BF, hbm)] * peers, before=((tiles, comps, CHUNKS, LANES), F32, VMEM), end=((tiles, comps, LANES), F32, VMEM), fade=((tiles, comps, LANES), F32, VMEM)),
        Box(x=pltpu.VMEM((tiles, seq_rows, LANES), F32), sem=sems((peers,))),
        after=[pack_one.own],
        hides=HIDE_ENDS,
    )
    def gate(*arrays):
        ends.token, *arrays = lax.optimization_barrier((ends.token,) + arrays)
        return arrays

    pack_two = packed(pack_second, two_shape, gate(update_proj, mixer_proj, output_proj))
    pack_three = packed(pack_third, three_shape, gate(up_proj, down_proj))
    came_one = [later_than(x, ends) for x in far_pieces(pack_one)]
    pack_two.own, came_one[0] = lax.optimization_barrier((pack_two.own, came_one[0]))
    came_two = far_pieces(pack_two)
    next_one = next_pieces(came_one)
    raw_blocks = exchange(ends.r, "wa")
    earlier = group_totals(ends.end, ends.fade, "seq", False)
    earlier[-1], *raw_blocks = lax.optimization_barrier((earlier[-1], *raw_blocks))
    outs = Box(
        value=((seqs, seq_rows, width), F32, VMEM),
        start=((tiles, comps, CHUNKS, LANES), F32, VMEM),
    )
    outs.m = [((rows, width), BF, hbm)] * peers
    ema = run(
        functools.partial(ema_values, groups, comps, peers),
        [(meta, SMEM), (inputs, VMEM), (decay_rows, VMEM), (mix_rows, VMEM), (skip_row, VMEM), (ends.before, VMEM), (earlier, VMEM)],
        outs,
        Box(
            x=pltpu.VMEM((tiles, seq_rows, LANES), F32),
            y=pltpu.VMEM((tiles, seq_rows, LANES), F32),
            mixed=pltpu.VMEM((tok_rows, width), BF),
            sem=sems((peers,)),
        ),
        after=came_two + next_one,
        hides=HIDE_VALUES,
    )
    mixed_blocks = exchange(ema.m, "wa")
    held = (pack_three.own, pack_one.packed, pack_two.packed, *mixed_blocks)
    pack_three.own, pack_one.packed, pack_two.packed, *mixed_blocks = lax.optimization_barrier(held)
    came_three = far_pieces(pack_three)
    shards_one = all_shards(pack_one, came_one, next_one)
    shards_two = all_shards(pack_two, came_two, next_pieces(came_two))
    shards_three = all_shards(pack_three, came_three, next_pieces(came_three))

    count = len(jax.tree.leaves(shards_one))
    vec = Box(
        zeta=zeta_proj, zeta_bias=zeta_bias, query_gain=query_gain, query_shift=query_shift,
        key_gain=key_gain, rel=pack_one.rel, positions=positions,
        output_bias=output_bias, update_bias=update_bias,
    )
    fwd = run(
        functools.partial(attend_forward, peers),
        [(meta, SMEM), (mixed_blocks, hbm), (raw_blocks, hbm), (shards_one, hbm), (shards_two, hbm)],
        Box(
            mixed=((rows, wide), BF, VMEM), raw=((rows, wide), BF, VMEM), zeta_pre=((rows, Z), F32, VMEM),
            queries=((rows, Z), BF, VMEM), keys=((rows, Z), BF, VMEM), probs=((rows, GROUP), F32, VMEM),
            reset_pre=((peers, rows, units), F32, VMEM), value_pre=((peers, rows, units), F32, VMEM),
            values=((peers, rows, units), BF, VMEM), attended=((peers, rows, units), F32, VMEM),
            gated=((peers, rows, units), BF, VMEM), out_pre=((rows, wide), F32, VMEM), gate=((rows, wide), F32, VMEM),
            normed=((rows, wide), F32, VMEM), inv=((rows, 1), F32, VMEM), up_bias=((peers, 8, units), F32, VMEM),
        ),
        Box(
            mixed=pltpu.VMEM((peers, rows, width), BF), raw=pltpu.VMEM((peers, rows, width), BF),
            one=pltpu.VMEM((peers,) + one_shape, BF), two=pltpu.VMEM((peers,) + two_shape, BF),
            pre=pltpu.VMEM((rows, wide), F32), gate=pltpu.VMEM((rows, wide), F32),
            sem=sems((2 * peers + 2 * count,)),
        ),
        vectors=vec,
        limit=62,
    )

    vec = Box(
        first_gain=first_gain, first_shift=first_shift, down_bias=down_bias,
        second_gain=second_gain, second_shift=second_shift, up_bias=fwd.up_bias,
    )
    outs = Box(
        mid_grad=((rows, wide), F32, VMEM), second=((peers, rows, width), BF, VMEM), sums=((6 * wide // LANES // 8 * 8 + 8, LANES), F32, VMEM), up_bias=((peers, 8, LANES), F32, VMEM),
        grads=[((peers // 2,) + three_shape, BF, VMEM)] * 2,
    )
    ffn = run(
        functools.partial(feed_forward, peers, ranks),
        [(meta, SMEM), (lengths, SMEM), (shards_three, hbm), (fwd.normed, VMEM), (fwd.inv, VMEM), (targets, hbm)],
        outs,
        Box(
            three=pltpu.VMEM((peers,) + three_shape, BF), first=pltpu.VMEM((rows, wide), BF),
            total=pltpu.VMEM((rows, wide), F32), up_pre=pltpu.VMEM((peers, rows, hidden), F32),
            act=pltpu.VMEM((peers, rows, hidden), BF), grad=pltpu.VMEM((rows, wide), BF),
            upg=pltpu.VMEM((rows, hidden), BF), sem=sems((count,)), targets=pltpu.VMEM((rows, wide), BF), target_sem=sems(()),
        ),
        vectors=vec,
    )
    row_bits = bits_of(ranks)
    third_parts = core_sums(ffn.grads)

    one = run(
        functools.partial(attend_back_one, peers),
        [(meta, SMEM), (shards_two, hbm), (fwd.mixed, VMEM), (fwd.raw, VMEM), (ffn.mid_grad, VMEM), (fwd.out_pre, VMEM),
         (fwd.gate, VMEM), (fwd.reset_pre, VMEM), (fwd.attended, VMEM), (fwd.gated, VMEM)],
        Box(
            direct=((rows, wide), F32, VMEM), sums=((2 * wide // LANES // 8 * 8 + 8, LANES), F32, VMEM), mixed_grad=((peers, rows, width), F32, VMEM),
            attend_grad=((peers, rows, units), BF, VMEM), reset_grad=((peers, rows, units), BF, VMEM),
            bias=((peers, 8, LANES), F32, VMEM),
            grads=[((peers // 2,) + two_shape, BF, VMEM)] * 2,
        ),
        Box(
            two=pltpu.VMEM((peers,) + two_shape, BF), mixed=pltpu.VMEM((peers, rows, width), BF),
            block=pltpu.VMEM((rows, width), BF), pre_grad=pltpu.VMEM((rows, wide), BF),
            gate_grad=pltpu.VMEM((rows, wide), BF), sem=sems((count,)),
        ),
        after=[third_parts],
        hides=HIDE_ONE,
    )
    vec = Box(
        zeta=zeta_proj, query_gain=query_gain, key_gain=key_gain, positions=positions,
    )
    outs = Box(
        rel=((8, LANES), F32, VMEM), sums=((8, Z), F32, VMEM), zeta=((wide, Z), F32, VMEM),
        bias=((peers, 8, LANES), F32, VMEM),
        grads=[((peers // 2, wide, 2 * units), BF, VMEM)] * 2,
    )
    outs.m = [((rows, width), BF, hbm)] * peers
    outs.r = [((rows, 2 * width), BF, hbm)] * peers
    two = run(
        functools.partial(attend_back_two, peers),
        [(meta, SMEM), (shards_one, hbm), (fwd.mixed, VMEM), (fwd.raw, VMEM), (fwd.value_pre, VMEM), (fwd.values, VMEM),
         (fwd.probs, VMEM), (one.attend_grad, VMEM), (one.reset_grad, VMEM), (one.direct, VMEM), (one.mixed_grad, VMEM),
         (fwd.queries, VMEM), (fwd.keys, VMEM), (fwd.zeta_pre, VMEM), (ffn.second, VMEM)],
        outs,
        Box(
            one=pltpu.VMEM((peers,) + one_shape, BF), query_grad=pltpu.VMEM((rows, Z), F32),
            key_grad=pltpu.VMEM((rows, Z), F32), mixed=pltpu.VMEM((rows, wide), F32), raw=pltpu.VMEM((rows, wide), F32),
            vgrad=pltpu.VMEM((rows, units), BF), mixed_out=pltpu.VMEM((peers, rows, width), BF),
            raw_out=pltpu.VMEM((peers, rows, 2 * width), BF), sem=sems((max(count, 2 * peers),)),
        ),
        vectors=vec,
    )
    grad_blocks = exchange(two.m, "wa")
    third_rows = keep_rows(third_parts, row_bits[0], two)
    mark = beside(HIDE_TWO, two.rel)
    second_parts = core_sums(one.grads, mark)
    first_parts = core_sums(two.grads, mark)

    back = run(
        functools.partial(ema_back_ends, groups, comps, peers),
        [(meta, SMEM), (grad_blocks, hbm), (ema.value, VMEM), (decay_rows, VMEM)],
        Box(
            grad=((tiles, seq_rows, LANES), F32, VMEM), after=((tiles, comps, CHUNKS, LANES), F32, VMEM),
            first=((tiles, comps, LANES), F32, VMEM),
        ),
        Box(grad=pltpu.VMEM((tok_rows, width), BF), sem=sems((peers,))),
        after=[second_parts, first_parts, third_rows],
        hides=HIDE_BACK,
    )
    third_rows = shard_sum(third_rows, back)
    nears = []
    later = group_totals(back.first, ends.fade, "seq", True, nears)
    near = nears[-1]
    for bit in row_bits[1:-1]:
        third_rows = keep_rows(third_rows, bit, nears[0])
    third_rows = plus(third_rows, later_than(swap(third_rows, "seq", row_bits[-1]), near))
    first_sum = keep_rows(first_parts, row_bits[0], near)
    second_sum = shard_sum(second_parts, near)
    last = run(
        functools.partial(ema_back, groups, comps),
        [(meta, SMEM), (inputs, VMEM), (back.grad, VMEM), (decay_rows, VMEM), (mix_rows, VMEM), (skip_row, VMEM),
         (ema.start, VMEM), (back.after, VMEM), (later, VMEM)],
        Box(part=((tiles, seq_rows, LANES), F32, VMEM), sums=((-(-width // LANES), 2 * comps + 8, LANES), F32, VMEM)),
        Box(
            x=pltpu.VMEM((tiles, seq_rows, LANES), F32),
            states=pltpu.VMEM((seq_rows // CHUNKS, comps, CHUNKS, LANES), F32),
        ),
        after=[third_rows, first_sum, second_sum],
        hides=HIDE_LAST,
    )
    first_rows = shard_sum(first_sum, last)
    second_rows = keep_rows(second_sum, row_bits[0], last)
    first_rows, *rest_sent = lax.optimization_barrier((first_rows, *two.r))
    rest_blocks = exchange(rest_sent, "wa")
    joined = run(
        functools.partial(ema_join, groups, peers),
        [(meta, SMEM), (last.part, VMEM), (rest_blocks, hbm)],
        Box(grad=((seqs, seq_rows, width), F32, VMEM), block=((seqs, seq_rows, width), BF, VMEM)),
        Box(rest=pltpu.VMEM((tok_rows, 2 * width), BF), sem=sems((peers,))),
    )

    totals = []
    for rows_left in (third_rows, second_rows, first_rows):
        is_third = rows_left is third_rows
        if not is_third:
            for bit in row_bits[1:-1]:
                rows_left = keep_rows(rows_left, bit)
            rows_left = plus(rows_left, swap(rows_left, "seq", row_bits[-1]))
        totals.append(all_rows(rows_left, row_bits[:-1], *([last] if is_third else [])))
    third_total, second_total, first_total = totals
    small = [ffn.sums, one.sums, two.sums, two.rel] + [a.reshape(-1, LANES) for a in (ffn.up_bias, one.bias, two.bias)]
    places = [0]
    for part in small:
        places.append(places[-1] + part.shape[0])
    small += [mark.token] + [mark.token for mark in nears] + [two.token, back.token, ema.token, ends.token, last.token]
    small.append(jnp.zeros((-sum(part.shape[0] for part in small) % 16, LANES), F32))
    small, zeta_grad = sum_small(jnp.concatenate(small, axis=0), two.zeta, [("wa", bit) for bit in bits_of(peers)])
    count = small.shape[0]
    small = jnp.concatenate([small, last.sums.reshape(-1, LANES)])
    small, zeta_grad = sum_small(small, zeta_grad, [("seq", bit) for bit in row_bits])
    ema_sums = small[count:].reshape(last.sums.shape)
    ema_sums = jnp.concatenate(list(ema_sums), axis=1)[:, :width]
    decay_grad = ema_sums[:comps].T * (ema_feed * ema_read)
    moment = ema_sums[comps : 2 * comps].T
    feed_grad, read_grad = moment * ema_read, moment * ema_feed
    skip_grad = ema_sums[2 * comps]
    parts = [small[a:b] for a, b in zip(places, places[1:])]
    tall = wide // LANES
    lines = [parts[0][i * tall : (i + 1) * tall].reshape(wide) for i in range(5)]
    lines += [parts[1][i * tall : (i + 1) * tall].reshape(wide) for i in range(2)]
    loss = parts[0][5 * tall, 0] + last.token[0, 0]
    zsums, rel_grad = parts[2], parts[3][:2].reshape(2 * GROUP)[: rel_bias.shape[0]]
    up_bias_grad, reset_bias_grad, value_bias_grad = (
        lax.dynamic_slice_in_dim(part, me * 8, 8, 0).reshape(8 * LANES)[:units] for part in parts[4:]
    )

    up_grad = jnp.concatenate([third_total[:depth, j * hidden : (j + 1) * hidden] for j in range(fold)], axis=0)
    return (
        joined.block, joined.grad, loss, decay_grad, feed_grad, read_grad, skip_grad, zeta_grad, zsums[0], zsums[1], zsums[2],
        zsums[3], rel_grad, first_total[:, :units].astype(F32), reset_bias_grad, first_total[:, units:].astype(F32), value_bias_grad,
        second_total[:width].astype(F32), lines[6], second_total[width : 2 * width].astype(F32), second_total[2 * width :].astype(F32), lines[5], lines[3],
        lines[4], up_grad.astype(F32), up_bias_grad, third_total[depth:].astype(F32), lines[2], lines[0], lines[1],
    )


def solution(mesh):
    return jax.shard_map(
        per_device,
        mesh=mesh,
        in_specs=(
            P(None, "seq", "wa"), P(None, "seq", None), P(), P(None, "seq"), P("wa", None), P("wa", None), P("wa", None), P("wa"),
            P(), P(), P(), P(), P(), P(), P(None, "wa"), P("wa"), P(None, "wa"), P("wa"), P("wa", None), P(), P("wa", None),
            P("wa", None), P(), P(), P(), P(None, "wa"), P("wa"), P("wa", None), P(), P(), P(),
        ),
        out_specs=(
            P(None, "seq", "wa"), P(None, "seq", "wa"), P(), P("wa", None), P("wa", None), P("wa", None), P("wa"), P(), P(), P(),
            P(), P(), P(), P(None, "wa"), P("wa"), P(None, "wa"), P("wa"), P("wa", None), P(), P("wa", None), P("wa", None), P(),
            P(), P(), P(None, "wa"), P("wa"), P("wa", None), P(), P(), P(),
        ),
        check_vma=False,
    )
```

```python
import functools

import jax
import jax.numpy as jnp
from jax import lax
from jax.experimental import pallas as pl
from jax.experimental.pallas import tpu as pltpu
from jax.sharding import PartitionSpec as P

Z = 128
GROUP = 128
LANES = 128
CHUNKS = 8
BIAS_ROWS = 32
HIDE_ENDS, HIDE_VALUES, HIDE_ATTEND, HIDE_ONE, HIDE_TWO, HIDE_BACK, HIDE_LAST = 20, 20, 20, 20, 40, 60, 15
SHARE_BITS = 1
EPSILON = 1e-05
BF = jnp.bfloat16
F32 = jnp.float32
VMEM = pltpu.MemorySpace.VMEM
SMEM = pltpu.MemorySpace.SMEM


def dot(a, b):
    return jnp.dot(a, b, preferred_element_type=F32)


def dot_nt(a, b):
    return lax.dot_general(a, b, (((1,), (1,)), ((), ())), preferred_element_type=F32)


def dot_tn(a, b):
    return lax.dot_general(a, b, (((0,), (0,)), ((), ())), preferred_element_type=F32)


def sigmoid(v):
    return 1.0 / (1.0 + jnp.exp(-v))


def slope(v):
    s = sigmoid(v)
    return s * (1.0 + v * (1.0 - s))


def row(ref):
    return ref[...].reshape(1, ref.shape[0])


def put_line(ref, at, line):
    for j in range(0, line.shape[1], LANES):
        piece = line[:, j : j + LANES]
        ref[at + j // LANES : at + j // LANES + 1, : piece.shape[1]] = piece


def colsum(v):
    return jnp.sum(v, axis=0, keepdims=True)


def normalise(v):
    center = v - jnp.mean(v, axis=-1, keepdims=True)
    inv = lax.rsqrt(jnp.mean(center * center, axis=-1, keepdims=True) + EPSILON)
    return center * inv, inv


def norm_back(grad, normed, inv, gain):
    scaled = grad * gain
    one = jnp.mean(scaled, axis=-1, keepdims=True)
    two = jnp.mean(scaled * normed, axis=-1, keepdims=True)
    return inv * (scaled - one - normed * two)


class Box:
    def __init__(self, **parts):
        self.__dict__.update(parts)


jax.tree_util.register_pytree_node(
    Box, lambda box: (tuple(vars(box).values()), tuple(vars(box))), lambda names, parts: Box(**dict(zip(names, parts)))
)


def whole(space=VMEM):
    return pl.BlockSpec(memory_space=space)


def run(kernel, ins, outs, scratch, after=(), vectors=None, limit=48, hides=0):
    body, count = kernel, len(ins)
    vectors = vectors or Box()
    outs.token = ((8, LANES), F32, VMEM)
    fetched = len(vars(vectors))
    ins = ins + [(vectors, pltpu.MemorySpace.HBM), (list(after), pl.ANY)]
    scratch = Box(
        body=scratch, vec=jax.tree.map(lambda a: pltpu.VMEM(a.shape, a.dtype), vectors),
        sem=pltpu.SemaphoreType.DMA((max(fetched, 1),)),
    )

    def kernel(*refs):
        hbm, out, s = refs[count], refs[count + 2], refs[count + 3]
        copies = [
            pltpu.make_async_copy(vars(hbm)[name], vars(s.vec)[name], s.sem.at[i]) for i, name in enumerate(vars(hbm))
        ]
        for copy in copies:
            copy.start()
        if fetched:
            s.body.vec = s.vec
            s.body.wait = lambda: [copy.wait() for copy in copies]
        out.token[...] = jnp.zeros_like(out.token)
        body(*refs[:count], out, s.body)

    specs = [jax.tree.map(lambda _, space=space: whole(space), tree) for tree, space in ins]
    trees = [tree for tree, _ in ins]
    leaf = lambda entry: isinstance(entry, tuple)
    shapes = jax.tree.map(lambda e: jax.ShapeDtypeStruct(e[0], e[1]), outs, is_leaf=leaf)
    out_specs = jax.tree.map(lambda e: whole(e[2]), outs, is_leaf=leaf)
    return pl.pallas_call(
        kernel,
        out_shape=(shapes,),
        in_specs=specs,
        out_specs=(out_specs,),
        scratch_shapes=[scratch],
        compiler_params=pltpu.CompilerParams(vmem_limit_bytes=limit * 2**20),
        cost_estimate=pl.CostEstimate(flops=1 + int(hides * 1.15e9), bytes_accessed=1, transcendentals=0),
    )(*trees)[0]


def beside(hides, *deps):
    def kernel(ins, out, s):
        pass

    return run(kernel, [(list(deps), pl.ANY)], Box(), Box(), hides=hides)


def pack(pieces, meta, regions, out):
    height = out.own.shape[0]
    for ref, at, rows, top, left in regions:
        out.packed[top : top + rows, left : left + ref.shape[1]] = ref[at : at + rows, :]

    def piece(j):
        for ref, at, rows, top, left in regions:
            low, high = max(top, j * height), min(top + rows, (j + 1) * height)
            if low < high:
                out.own[low - j * height : high - j * height, left : left + ref.shape[1]] = ref[at + low - top : at + high - top, :]

    for j in range(pieces):
        pl.when(meta[1] == j)(lambda j=j: piece(j))


def pack_first(pieces, meta, reset, value, rel, out, s):
    units = reset.shape[1]
    s.wait()
    s.rows[...] = jnp.zeros_like(s.rows)
    for left, ref in ((0, s.vec.reset), (units, s.vec.value)):
        rest = row(ref)
        for i in range(3):
            high = rest.astype(BF).astype(F32)
            s.rows[i : i + 1, left : left + units] = high
            rest = rest - high
    s.rows[3:4, :units] = row(s.vec.up).astype(F32)
    s.bias[...] = s.rows[...].astype(BF)
    out.rel[...] = jnp.zeros_like(out.rel)
    out.rel[0:1, : rel.shape[0]] = row(rel)
    wide = reset.shape[0]
    pack(pieces, meta, [(reset, 0, wide, 0, 0), (value, 0, wide, 0, units), (s.bias, 0, BIAS_ROWS, wide, 0)], out)


def pack_second(pieces, meta, update, mixer, output, out, s):
    width, units = update.shape[0], output.shape[0]
    pack(pieces, meta, [(update, 0, width, 0, 0), (mixer, 0, width, width, 0), (output, 0, units, 2 * width, 0)], out)


def pack_third(pieces, meta, up, down, out, s):
    hidden = up.shape[1]
    depth = up.shape[0] // (down.shape[1] // hidden)
    regions = [(up, at, depth, 0, at // depth * hidden) for at in range(0, up.shape[0], depth)]
    pack(pieces, meta, regions + [(down, 0, hidden, depth, 0)], out)


def lane_groups(seqs, width):
    groups = []
    rest = width % LANES
    for s in range(seqs):
        for c in range(0, width - rest, LANES):
            groups.append([(s, c, LANES, 0)])
    tile, lane = [], 0
    for s in range(seqs if rest else 0):
        if lane + rest > LANES:
            groups.append(tile)
            tile, lane = [], 0
        tile.append((s, width - rest, rest, lane))
        lane += rest
    if tile:
        groups.append(tile)
    return groups


def join(parts):
    rows = parts[0].shape[0]
    used = sum(p.shape[1] for p in parts)
    if used < LANES:
        parts = parts + [jnp.zeros((rows, LANES - used), parts[0].dtype)]
    return parts[0] if len(parts) == 1 else jnp.concatenate(parts, axis=1)


def rows_of(group, ref):
    return join([ref[:, c : c + w] for _, c, w, _ in group])


def tokens_of(group, get):
    return join([get(s, c, w) for s, c, w, _ in group])


def spread(row):
    return jnp.broadcast_to(row, (CHUNKS, LANES))


def power(v, count):
    while count > 1:
        v = v * v
        count //= 2
    return v


def shifted(v, by):
    at = lax.broadcasted_iota(jnp.int32, v.shape, 0)
    moved = pltpu.roll(v, by % CHUNKS, 0)
    keep = at >= by if by > 0 else at < CHUNKS + by
    return jnp.where(keep, moved, 0.0)


def chunk_scan(ends, chunk_decay, sign):
    run_sum, factor, step = ends, chunk_decay, 1
    while step < CHUNKS:
        run_sum = run_sum + factor * shifted(run_sum, sign * step)
        factor, step = factor * factor, step * 2
    return run_sum, shifted(run_sum, sign)


def rank_power(chunk_decay, reverse):
    at = lax.broadcasted_iota(jnp.int32, chunk_decay.shape, 0)
    at = CHUNKS - 1 - at if reverse else at
    result, factor, bit = jnp.ones_like(chunk_decay), chunk_decay, 1
    while bit < CHUNKS:
        result = jnp.where((at & bit) != 0, result * factor, result)
        factor, bit = factor * factor, bit * 2
    return result


def steps_of(length, body, carry, reverse=False, unroll=4):
    def block(i, state):
        for u in range(unroll):
            t = i * unroll + u
            state = body(length - 1 - t if reverse else t, state)
        return state

    return lax.fori_loop(0, length // unroll, block, carry)


def at_step(ref, g, t, length):
    return ref.at[g, pl.ds(t, CHUNKS, stride=length), :]


def ema_ends(groups, comps, blocks, meta, x_ref, decay_ref, out, s):
    rows = x_ref.shape[1]
    part = x_ref.shape[0] * rows // blocks
    copies = []
    for k in range(blocks):
        at = (meta[0] ^ k) * part
        source = x_ref.at[at // rows, pl.ds(pl.multiple_of(at % rows, part), part), :]
        copies.append(pltpu.make_async_copy(source, out.r[k], s.sem.at[k]))
    for copy in copies:
        copy.start()
    length = x_ref.shape[1] // CHUNKS
    for g, group in enumerate(groups):
        s.x[g] = tokens_of(group, lambda q, c, w: x_ref[q, :, c : c + w].astype(F32))
        decay = rows_of(group, decay_ref)
        decays = [spread(decay[n : n + 1]) for n in range(comps)]

        def body(t, state):
            now = at_step(s.x, g, t, length)[...]
            return tuple(decays[n] * state[n] + now for n in range(comps))

        ends = steps_of(length, body, (jnp.zeros((CHUNKS, LANES), F32),) * comps)
        for n in range(comps):
            total, before = chunk_scan(ends[n], power(decays[n], length), 1)
            out.before[g, n] = before
            out.fade[g, n : n + 1, :] = power(decay[n : n + 1], length * CHUNKS)
            out.end[g, n : n + 1, :] = total[CHUNKS - 1 :]
    for copy in copies:
        copy.wait()


def carried(parts, device_decay, rank, reverse):
    total, passed = jnp.zeros_like(device_decay), jnp.ones_like(device_decay)
    for i, part in enumerate(parts):
        counts = ((rank // (1 << i)) % 2) == (0 if reverse else 1)
        total = jnp.where(counts, total + passed * part, total)
        passed = jnp.where(counts, passed * device_decay, passed)
        device_decay = device_decay * device_decay
    return total


def ema_values(groups, comps, blocks, meta, x_ref, decay_ref, mix_ref, skip_ref, before_ref, got, out, s):
    length = x_ref.shape[1] // CHUNKS
    width = x_ref.shape[2]
    seqs, rows = x_ref.shape[0], x_ref.shape[1]
    for g, group in enumerate(groups):
        s.x[g] = tokens_of(group, lambda q, c, w: x_ref[q, :, c : c + w].astype(F32))
        decay, mix, skip = rows_of(group, decay_ref), rows_of(group, mix_ref), rows_of(group, skip_ref)
        decays = [spread(decay[n : n + 1]) for n in range(comps)]
        mixes = [spread(mix[n : n + 1]) for n in range(comps)]
        skip = spread(skip)
        state_in = carried([part[g] for part in got], power(decay, length * CHUNKS), meta[2], False)
        start = []
        for n in range(comps):
            ranks = rank_power(power(decays[n], length), False)
            start.append(before_ref[g, n] + ranks * spread(state_in[n : n + 1]))
            out.start[g, n] = start[n]

        def body(t, state):
            now = at_step(s.x, g, t, length)[...]
            state = tuple(decays[n] * state[n] + now for n in range(comps))
            terms = [mixes[n] * state[n] for n in range(comps)] + [skip * now]
            while len(terms) > 1:
                terms = [a + b for a, b in zip(terms[::2], terms[1::2])] + (terms[-1:] if len(terms) % 2 else [])
            at_step(s.y, g, t, length)[...] = terms[0]
            return state

        steps_of(length, body, tuple(start))
        for q, c, w, lane in group:
            value = s.y[g, :, lane : lane + w]
            out.value[q, :, c : c + w] = value
            s.mixed[pl.ds(q * rows, rows), c : c + w] = (value * sigmoid(value)).astype(BF)
    part = seqs * rows // blocks
    copies = [
        pltpu.make_async_copy(
            s.mixed.at[pl.ds(pl.multiple_of((meta[0] ^ k) * part, part), part), :], out.m[k], s.sem.at[k]
        )
        for k in range(blocks)
    ]
    for copy in copies:
        copy.start()
    for copy in copies:
        copy.wait()


def ema_back_ends(groups, comps, blocks, meta, grads, value_ref, decay_ref, out, s):
    length = value_ref.shape[1] // CHUNKS
    rows = value_ref.shape[1]
    part = value_ref.shape[0] * rows // blocks
    copies = [
        pltpu.make_async_copy(
            grads[k], s.grad.at[pl.ds(pl.multiple_of((meta[0] ^ k) * part, part), part), :], s.sem.at[k]
        )
        for k in range(blocks)
    ]
    for copy in copies:
        copy.start()
    for copy in copies:
        copy.wait()
    for g, group in enumerate(groups):

        def load(q, c, w):
            return s.grad[pl.ds(q * rows, rows), c : c + w].astype(F32) * slope(value_ref[q, :, c : c + w])

        out.grad[g] = tokens_of(group, load)
        decay = rows_of(group, decay_ref)
        decays = [spread(decay[n : n + 1]) for n in range(comps)]

        def body(t, state):
            now = at_step(out.grad, g, t, length)[...]
            return tuple(decays[n] * state[n] + now for n in range(comps))

        ends = steps_of(length, body, (jnp.zeros((CHUNKS, LANES), F32),) * comps, reverse=True)
        for n in range(comps):
            total, after = chunk_scan(ends[n], power(decays[n], length), -1)
            out.after[g, n] = after
            out.first[g, n : n + 1, :] = total[:1]


def ema_join(groups, blocks, meta, part_ref, rests, out, s):
    seqs, rows, width = out.grad.shape
    part = seqs * rows // blocks
    copies = [
        pltpu.make_async_copy(
            rests[k], s.rest.at[pl.ds(pl.multiple_of((meta[0] ^ k) * part, part), part), :], s.sem.at[k]
        )
        for k in range(blocks)
    ]
    for copy in copies:
        copy.start()
    for copy in copies:
        copy.wait()
    for q in range(seqs):
        out.block[q] = s.rest[pl.ds(q * rows, rows), width:]
    for g, group in enumerate(groups):
        for q, c, w, lane in group:
            rest = s.rest[pl.ds(q * rows, rows), c : c + w].astype(F32)
            out.grad[q, :, c : c + w] = part_ref[g, :, lane : lane + w] + rest


def ema_back(groups, comps, meta, x_ref, grad_ref, decay_ref, mix_ref, skip_ref, start_ref, after_ref, got, out, s):
    length = x_ref.shape[1] // CHUNKS
    out.sums[...] = jnp.zeros_like(out.sums)
    half = comps // 2
    for g, group in enumerate(groups):
        s.x[g] = tokens_of(group, lambda q, c, w: x_ref[q, :, c : c + w].astype(F32))
        decay, mix, skip = rows_of(group, decay_ref), rows_of(group, mix_ref), rows_of(group, skip_ref)
        decays = [spread(decay[n : n + 1]) for n in range(comps)]
        mixes = [spread(mix[n : n + 1]) for n in range(comps)]
        skip = spread(skip)

        def forward(t, state):
            now = at_step(s.x, g, t, length)[...]
            for n in range(comps):
                s.states[t, n] = state[n]
            return tuple(decays[n] * state[n] + now for n in range(comps))

        steps_of(length, forward, tuple(start_ref[g, n] for n in range(comps)))
        grad_in = carried([p[g] for p in got], power(decay, length * CHUNKS), meta[2], True)
        for h in range(2):
            mine = range(h * half, (h + 1) * half)
            begin = []
            for n in mine:
                ranks = rank_power(power(decays[n], length), True)
                begin.append(after_ref[g, n] + ranks * spread(grad_in[n : n + 1]))
            zero = (jnp.zeros((CHUNKS, LANES), F32),) * half

            def backward(t, carry):
                grads, moments, changes, skips = carry
                now, up = at_step(s.x, g, t, length)[...], at_step(grad_ref, g, t, length)[...]
                grads = tuple(decays[n] * grads[i] + up for i, n in enumerate(mine))
                moments = tuple(moments[i] + grads[i] * now for i in range(half))
                changes = tuple(changes[i] + grads[i] * s.states[t, n] for i, n in enumerate(mine))
                terms = [mixes[n] * grads[i] for i, n in enumerate(mine)]
                if h == 0:
                    terms.append(skip * up)
                    skips = skips + up * now
                else:
                    terms.append(at_step(out.part, g, t, length)[...])
                while len(terms) > 1:
                    terms = [a + b for a, b in zip(terms[::2], terms[1::2])] + (terms[-1:] if len(terms) % 2 else [])
                at_step(out.part, g, t, length)[...] = terms[0]
                return grads, moments, changes, skips

            _, moments, changes, skips = steps_of(length, backward, (tuple(begin), zero, zero, zero[0]), reverse=True, unroll=2)
            for q, c, w, lane in group:
                for i, n in enumerate(mine):
                    out.sums[c // LANES, n : n + 1, :w] += colsum(changes[i])[:, lane : lane + w]
                    out.sums[c // LANES, comps + n : comps + n + 1, :w] += colsum(moments[i])[:, lane : lane + w]
                if h == 0:
                    out.sums[c // LANES, 2 * comps : 2 * comps + 1, :w] += colsum(skips)[:, lane : lane + w]


def weight_copies(meta, shards, dst, sem, first):
    copies = []
    for k, pieces in enumerate(shards):
        height = dst.shape[1] // len(pieces)
        for j, piece in enumerate(pieces):
            target = dst.at[k]
            if len(pieces) > 1:
                target = dst.at[k, pl.ds(pl.multiple_of((meta[1] ^ j) * height, height), height), :]
            copies.append(pltpu.make_async_copy(piece, target, sem.at[first + len(copies)]))
    return copies


def block_copies(meta, blocks, dst, sem, first):
    return [
        pltpu.make_async_copy(block, dst.at[meta[0] ^ k], sem.at[first + k]) for k, block in enumerate(blocks)
    ]


def positions_of(ref, start, g):
    at = start + g * GROUP
    length = ref.shape[1]
    columns = pl.ds(pl.multiple_of(at % length, GROUP), GROUP)
    place = ref[0:1, columns]
    for q in range(1, ref.shape[0]):
        place = jnp.where(at // length == q, ref[q : q + 1, columns], place)
    return place


def attend_forward(peers, meta, mixed, raw, first, second, out, s):
    vec = s.vec
    blocks = block_copies(meta, mixed, s.mixed, s.sem, 0)
    blocks += block_copies(meta, raw, s.raw, s.sem, peers)
    ones = weight_copies(meta, first, s.one, s.sem, 2 * peers)
    twos = weight_copies(meta, second, s.two, s.sem, 2 * peers + len(ones))
    for copy in blocks + ones + twos:
        copy.start()
    for copy in blocks:
        copy.wait()
    width = s.mixed.shape[2]
    units = s.one.shape[2] // 2
    rows, wide = out.mixed.shape
    groups = rows // GROUP
    for b in range(peers):
        out.mixed[:, b * width : (b + 1) * width] = s.mixed[b]
        out.raw[:, b * width : (b + 1) * width] = s.raw[b]
    s.wait()
    zeta_pre = dot(out.mixed[...], vec.zeta[...]) + row(vec.zeta_bias)
    out.zeta_pre[...] = zeta_pre
    act = zeta_pre * sigmoid(zeta_pre)
    queries = (act * row(vec.query_gain) + row(vec.query_shift)).astype(BF)
    keys = (act * row(vec.key_gain)).astype(BF)
    out.queries[...] = queries
    out.keys[...] = keys
    causal = lax.broadcasted_iota(jnp.int32, (GROUP, GROUP), 0) >= lax.broadcasted_iota(jnp.int32, (GROUP, GROUP), 1)
    for g in range(groups):
        at = slice(g * GROUP, (g + 1) * GROUP)
        place = jnp.broadcast_to(positions_of(vec.positions, meta[0] * rows, g).astype(F32), (GROUP, GROUP))
        distance = jnp.clip((place.T - place).astype(jnp.int32), 0, 2 * GROUP - 2)
        low = jnp.take_along_axis(
            jnp.broadcast_to(vec.rel[0:1, :GROUP], (GROUP, GROUP)), distance & (GROUP - 1), axis=1
        )
        high = jnp.take_along_axis(
            jnp.broadcast_to(vec.rel[0:1, GROUP:], (GROUP, GROUP)), distance & (GROUP - 1), axis=1
        )
        scores = dot_nt(queries[at], keys[at]) * Z**-0.5 + jnp.where(distance < GROUP, low, high)
        scores = jnp.where(causal, scores, -jnp.inf)
        shifted_exp = jnp.exp(scores - jnp.max(scores, axis=-1, keepdims=True))
        out.probs[at, :] = shifted_exp / jnp.sum(shifted_exp, axis=-1, keepdims=True)
    for copy in ones:
        copy.wait()
    for copy in twos:
        copy.wait()
    s.pre[...] = jnp.zeros_like(s.pre)
    s.gate[...] = jnp.zeros_like(s.gate)

    def shard(k, carry):
        biases = s.one[k, wide : wide + 16, :].astype(F32)
        bias = biases[0:1] + biases[1:2] + biases[2:3]
        out.up_bias[k] = jnp.broadcast_to(biases[3:4, :units], (8, units))
        reset_pre = dot(out.mixed[...], s.one[k, :wide, :units]) + bias[:, :units]
        value_pre = dot(out.raw[...], s.one[k, :wide, units:]) + bias[:, units:]
        values = (value_pre * sigmoid(value_pre)).astype(BF)
        out.reset_pre[k] = reset_pre
        out.value_pre[k] = value_pre
        out.values[k] = values
        for g in range(groups):
            at = slice(g * GROUP, (g + 1) * GROUP)
            out.attended[k, at, :] = dot(out.probs[at, :].astype(BF), values[at])
        gated = (reset_pre * sigmoid(reset_pre) * out.attended[k]).astype(BF)
        out.gated[k] = gated
        block = s.mixed[meta[0] ^ k]
        s.gate[...] += dot(block, s.two[k, :width, :])
        s.pre[...] += dot(block, s.two[k, width : 2 * width, :]) + dot(gated, s.two[k, 2 * width :, :])
        return carry

    lax.fori_loop(0, peers, shard, 0)
    out_pre = s.pre[...] + row(vec.output_bias)
    out.out_pre[...] = out_pre
    gate = sigmoid(s.gate[...] + row(vec.update_bias))
    out.gate[...] = gate
    mid = gate * (out_pre * sigmoid(out_pre)) + (1.0 - gate) * out.raw[...].astype(F32)
    normed, inv = normalise(mid)
    out.normed[...] = normed
    out.inv[...] = inv


def feed_forward(peers, ranks, meta, lengths, third, normed_ref, inv_ref, targets, out, s):
    vec = s.vec
    rows = normed_ref.shape[0]
    seqs, seq_rows = targets.shape[0], targets.shape[1]
    seq, offset = meta[0] * rows // seq_rows, pl.multiple_of(meta[0] * rows % seq_rows, rows)
    fetch = pltpu.make_async_copy(targets.at[seq, pl.ds(offset, rows), :], s.targets, s.target_sem)
    fetch.start()
    threes = weight_copies(meta, third, s.three, s.sem, 0)
    for copy in threes:
        copy.start()
    rows, width = normed_ref.shape
    s.wait()
    units = vec.up_bias.shape[2]
    fold = width // units
    depth = width // fold
    first = normed_ref[...] * row(vec.first_gain) + row(vec.first_shift)
    s.first[...] = first.astype(BF)
    s.total[...] = first + row(vec.down_bias)
    for copy in threes:
        copy.wait()

    def forward(k, carry):
        pre = vec.up_bias[k, 0:1, :]
        for j in range(fold):
            pre = pre + dot(
                s.first[:, j * depth : (j + 1) * depth], s.three[k, :depth, j * units : (j + 1) * units]
            )
        s.up_pre[k] = pre
        act = (pre * sigmoid(pre)).astype(BF)
        s.act[k] = act
        s.total[...] += dot(act, s.three[k, depth:, :])
        return carry

    lax.fori_loop(0, peers, forward, 0)
    normed, inv = normalise(s.total[...])
    second = normed * row(vec.second_gain) + row(vec.second_shift)
    piece = width // peers
    for b in range(peers):
        out.second[b] = second[:, b * piece : (b + 1) * piece].astype(BF)
    fetch.wait()
    misfit = second - s.targets[...].astype(F32)
    place = lax.broadcasted_iota(jnp.int32, (rows, 1), 0) + (meta[2] * seq_rows + offset)
    weight = (place < lengths[seq]).astype(F32)
    tokens = lengths[0]
    for q in range(1, seqs):
        tokens = tokens + lengths[q]
    true_count = jnp.broadcast_to(tokens, (rows, 1)).astype(F32)
    losses = jnp.sum(misfit * misfit, axis=1, keepdims=True) * (weight / (2.0 * width * true_count))
    out.sums[...] = jnp.zeros_like(out.sums)
    out.up_bias[...] = jnp.zeros_like(out.up_bias)
    lines = width // LANES
    put_line(out.sums, 5 * lines, jnp.broadcast_to(jnp.sum(losses, axis=0, keepdims=True), (1, LANES)))
    grad_out = misfit * (weight * (seqs * seq_rows * ranks / true_count))
    put_line(out.sums, 0, colsum(grad_out * normed))
    put_line(out.sums, lines, colsum(grad_out))
    second_grad = norm_back(grad_out, normed, inv, row(vec.second_gain))
    ffn_grad = second_grad.astype(BF)
    s.grad[...] = ffn_grad
    put_line(out.sums, 2 * lines, colsum(ffn_grad.astype(F32)))
    s.total[...] = second_grad

    def backward(k, carry):
        keep = k // 2
        down = dot_tn(s.act[k], s.grad[...]).astype(BF)
        up_grad = (dot_nt(s.grad[...], s.three[k, depth:, :]) * slope(s.up_pre[k])).astype(BF)
        put_line(out.up_bias.at[meta[0] ^ k], 0, colsum(up_grad.astype(F32)))
        s.upg[...] = up_grad
        ups = [dot_tn(s.first[:, j * depth : (j + 1) * depth], s.upg[...]).astype(BF) for j in range(fold)]

        def store(which):
            out.grads[which][keep, depth:, :] = down
            for j in range(fold):
                out.grads[which][keep, :depth, j * units : (j + 1) * units] = ups[j]

        pl.when(k % 2 == 0)(lambda: store(0))
        pl.when(k % 2 == 1)(lambda: store(1))
        for j in range(fold):
            s.total[:, j * depth : (j + 1) * depth] += dot_nt(
                s.upg[...], s.three[k, :depth, j * units : (j + 1) * units]
            )
        return carry

    lax.fori_loop(0, peers, backward, 0)
    first_grad = s.total[...]
    put_line(out.sums, 3 * lines, colsum(first_grad * normed_ref[...]))
    put_line(out.sums, 4 * lines, colsum(first_grad))
    out.mid_grad[...] = norm_back(first_grad, normed_ref[...], inv_ref[...], row(vec.first_gain))


def attend_back_one(peers, meta, second, mixed_ref, raw_ref, mid_ref, pre_ref, gate_ref, reset_ref, attended_ref, gated_ref, out, s):
    twos = weight_copies(meta, second, s.two, s.sem, 0)
    for copy in twos:
        copy.start()
    rows, wide = mixed_ref.shape
    width = wide // peers
    for b in range(peers):
        s.mixed[b] = mixed_ref[:, b * width : (b + 1) * width]
    mid, gate, pre = mid_ref[...], gate_ref[...], pre_ref[...]
    pre_grad = (mid * gate * slope(pre)).astype(BF)
    s.pre_grad[...] = pre_grad
    gate_grad = (mid * (pre * sigmoid(pre) - raw_ref[...].astype(F32)) * gate * (1.0 - gate)).astype(BF)
    s.gate_grad[...] = gate_grad
    out.direct[...] = mid * (1.0 - gate)
    out.sums[...] = jnp.zeros_like(out.sums)
    out.bias[...] = jnp.zeros_like(out.bias)
    put_line(out.sums, 0, colsum(pre_grad.astype(F32)))
    put_line(out.sums, wide // LANES, colsum(gate_grad.astype(F32)))
    for copy in twos:
        copy.wait()

    def shard(k, carry):
        keep = k // 2
        s.block[...] = s.mixed[meta[0] ^ k]
        update = dot_tn(s.block[...], s.gate_grad[...]).astype(BF)
        mixer = dot_tn(s.block[...], s.pre_grad[...]).astype(BF)
        output = dot_tn(gated_ref[k], s.pre_grad[...]).astype(BF)

        def store(which):
            out.grads[which][keep, :width, :] = update
            out.grads[which][keep, width : 2 * width, :] = mixer
            out.grads[which][keep, 2 * width :, :] = output

        pl.when(k % 2 == 0)(lambda: store(0))
        pl.when(k % 2 == 1)(lambda: store(1))
        out.mixed_grad[k] = dot_nt(s.gate_grad[...], s.two[k, :width, :]) + dot_nt(
            s.pre_grad[...], s.two[k, width : 2 * width, :]
        )
        gated_grad = dot_nt(s.pre_grad[...], s.two[k, 2 * width :, :])
        reset = reset_ref[k]
        out.attend_grad[k] = (gated_grad * (reset * sigmoid(reset))).astype(BF)
        reset_grad = (gated_grad * attended_ref[k] * slope(reset)).astype(BF)
        out.reset_grad[k] = reset_grad
        put_line(out.bias.at[meta[0] ^ k], 0, colsum(reset_grad.astype(F32)))
        return carry

    lax.fori_loop(0, peers, shard, 0)


def attend_back_two(
    peers, meta, first, mixed_ref, raw_ref, value_pre_ref, values_ref, probs_ref, agrad_ref, rgrad_ref, direct_ref, local_ref,
    queries_ref, keys_ref, zeta_pre_ref, second_ref, out, s,
):
    vec = s.vec
    ones = weight_copies(meta, first, s.one, s.sem, 0)
    for copy in ones:
        copy.start()
    rows, wide = mixed_ref.shape
    width = wide // peers
    units = values_ref.shape[2]
    groups = rows // GROUP
    s.wait()
    act = zeta_pre_ref[...] * sigmoid(zeta_pre_ref[...])
    line = lax.broadcasted_iota(jnp.int32, (2 * GROUP, GROUP), 0)
    buckets = jnp.zeros((1, 2 * GROUP), F32)
    for g in range(groups):
        at = slice(g * GROUP, (g + 1) * GROUP)

        def score(k, total):
            return total + dot_nt(agrad_ref[k, at, :], values_ref[k, at, :])

        prob_grad = lax.fori_loop(0, peers, score, jnp.zeros((GROUP, GROUP), F32))
        probs = probs_ref[at, :]
        row_dot = jnp.sum(probs * prob_grad, axis=-1, keepdims=True)
        sgrad = (probs * (prob_grad - row_dot)).astype(BF)
        s.query_grad[at, :] = dot(sgrad, keys_ref[at, :]) * Z**-0.5
        s.key_grad[at, :] = dot_tn(sgrad, queries_ref[at, :]) * Z**-0.5
        ahead = positions_of(vec.positions, meta[0] * rows, g)
        ahead = ahead - ahead[:, 0:1]
        to_row = (line == ahead).astype(BF)
        to_column = (line == 2 * GROUP - 1 - ahead).astype(BF)
        table = dot(to_row, dot_nt(sgrad, to_column).astype(BF))
        buckets = buckets + colsum(pltpu.roll(table, 1, 1, stride=1, stride_axis=0))
    out.rel[...] = jnp.zeros_like(out.rel)
    out.bias[...] = jnp.zeros_like(out.bias)
    put_line(out.rel, 0, buckets)
    query_grad, key_grad = s.query_grad[...], s.key_grad[...]
    zeta_grad = (query_grad * row(vec.query_gain) + key_grad * row(vec.key_gain)) * slope(zeta_pre_ref[...])
    zeta_grad = zeta_grad.astype(BF)
    out.sums[...] = jnp.zeros_like(out.sums)
    out.sums[0:1, :] = colsum(zeta_grad.astype(F32))
    out.sums[1:2, :] = colsum(query_grad * act)
    out.sums[2:3, :] = colsum(query_grad)
    out.sums[3:4, :] = colsum(key_grad * act)
    out.zeta[...] = dot_tn(mixed_ref[...], zeta_grad)
    s.mixed[...] = dot_nt(zeta_grad, vec.zeta[...])
    s.raw[...] = direct_ref[...]
    for copy in ones:
        copy.wait()

    def shard(k, carry):
        keep = k // 2
        for g in range(groups):
            at = slice(g * GROUP, (g + 1) * GROUP)
            vals_grad = dot_tn(probs_ref[at, :].astype(BF), agrad_ref[k, at, :])
            s.vgrad[at, :] = (vals_grad * slope(value_pre_ref[k, at, :])).astype(BF)
        put_line(out.bias.at[meta[0] ^ k], 0, colsum(s.vgrad[...].astype(F32)))
        reset = dot_tn(mixed_ref[...], rgrad_ref[k]).astype(BF)
        value = dot_tn(raw_ref[...], s.vgrad[...]).astype(BF)

        def store(which):
            out.grads[which][keep, :, :units] = reset
            out.grads[which][keep, :, units:] = value

        pl.when(k % 2 == 0)(lambda: store(0))
        pl.when(k % 2 == 1)(lambda: store(1))
        s.mixed[...] += dot_nt(rgrad_ref[k], s.one[k, :wide, :units])
        s.raw[...] += dot_nt(s.vgrad[...], s.one[k, :wide, units:])
        return carry

    lax.fori_loop(0, peers, shard, 0)
    for b in range(peers):
        at = slice(b * width, (b + 1) * width)
        s.mixed_out[b] = (s.mixed[:, at] + local_ref[meta[0] ^ b]).astype(BF)
        s.raw_out[b, :, :width] = s.raw[:, at].astype(BF)
        s.raw_out[b, :, width:] = second_ref[b]
    sends = []
    for k in range(peers):
        sends.append(pltpu.make_async_copy(s.mixed_out.at[meta[0] ^ k], out.m[k], s.sem.at[2 * k]))
        sends.append(pltpu.make_async_copy(s.raw_out.at[meta[0] ^ k], out.r[k], s.sem.at[2 * k + 1]))
    for copy in sends:
        copy.start()
    for copy in sends:
        copy.wait()


def swap(x, axis, by):
    size = lax.axis_size(axis)
    return lax.ppermute(x, axis, [(i, i ^ by) for i in range(size)])


def later_than(x, *marks):
    for mark in marks:
        x, mark.token = lax.optimization_barrier((x, mark.token))
    return x


def exchange(blocks, axis):
    return [blocks[0]] + [swap(blocks[k], axis, k) for k in range(1, len(blocks))]


def group_totals(total, fade, axis, reverse, nears=None):
    result = []
    for bit in bits_of(lax.axis_size(axis)):
        other = swap(total, axis, bit)
        if nears is not None:
            nears.append(beside(0, other))
            other, nears[-1].token = lax.optimization_barrier((other, nears[-1].token))
        result.append(other)
        upper = ((lax.axis_index(axis) // bit) % 2) == (0 if reverse else 1)
        total = jnp.where(upper, total + fade * other, other + fade * total)
        fade = fade * fade
    return result


def far_pieces(pack):
    return [swap(pack.own, "wa", k) for k in range(2, lax.axis_size("wa"), 2)]


def next_pieces(came):
    return [swap(piece, "seq", j) for piece in came for j in range(1, 1 << SHARE_BITS)]


def all_shards(pack, came, beyond):
    others = (1 << SHARE_BITS) - 1
    shards = [[pack.packed]]
    shards += [[came[i]] + beyond[i * others : (i + 1) * others] for i in range(len(came))]
    return [pieces for even in shards for pieces in (even, [swap(piece, "wa", 1) for piece in even])]


def plus(a, b):
    return (a.astype(F32) + b.astype(F32)).astype(a.dtype)


def core_sums(grads, *deps):
    return plus(grads[0], later_than(swap(grads[1], "wa", 1), *deps))


def shard_sum(parts, *deps):
    step = 2
    while parts.shape[0] > 1:
        parts = plus(parts[::2], later_than(swap(parts[1::2], "wa", step), *deps))
        step *= 2
    return parts[0]


def keep_rows(total, bit, *deps):
    here = (lax.axis_index("seq") // bit) % 2
    height = total.shape[-2] // 2
    mine = lax.dynamic_slice_in_dim(total, here * height, height, total.ndim - 2)
    theirs = lax.dynamic_slice_in_dim(total, (1 - here) * height, height, total.ndim - 2)
    return plus(mine, later_than(swap(theirs, "seq", bit), *deps))


def all_rows(total, bits, *deps):
    for bit in bits[::-1]:
        here = (lax.axis_index("seq") // bit) % 2
        other = later_than(swap(total, "seq", bit), *(deps if bit == bits[-1] else ()))
        total = jnp.where(
            here == 0, jnp.concatenate([total, other], axis=0), jnp.concatenate([other, total], axis=0)
        )
    return total


def sum_small(exact, rough, route):
    for axis, bit in route:
        high = lax.reduce_precision(exact, 8, 7)
        sent = jnp.concatenate([high.astype(BF), (exact - high).astype(BF), rough.astype(BF)])
        total = sent.astype(F32) + swap(sent, axis, bit).astype(F32)
        rows = exact.shape[0]
        exact, rough = total[:rows] + total[rows : 2 * rows], total[2 * rows :]
    return exact, rough


def bits_of(size):
    return [1 << b for b in range(size.bit_length() - 1)]


def per_device(
    inputs, targets, lengths, positions, ema_decay, ema_feed, ema_read, ema_skip, zeta_proj, zeta_bias, query_gain, query_shift,
    key_gain, rel_bias, reset_proj, reset_bias, value_proj, value_bias, update_proj, update_bias, mixer_proj, output_proj,
    output_bias, first_gain, first_shift, up_proj, up_bias, down_proj, down_bias, second_gain, second_shift,
):
    seqs, seq_rows, width = inputs.shape
    wide = targets.shape[2]
    comps = ema_decay.shape[1]
    peers, ranks = lax.axis_size("wa"), lax.axis_size("seq")
    me, rank = lax.axis_index("wa"), lax.axis_index("seq")
    tok_rows = seqs * seq_rows
    rows = tok_rows // peers
    n_groups = rows // GROUP
    units, hidden = reset_proj.shape[1], up_proj.shape[1]
    fold = wide // hidden
    depth = wide // fold
    total_tokens = tok_rows * ranks
    groups = lane_groups(seqs, width)
    tiles = len(groups)
    pieces = 1 << SHARE_BITS
    place = rank % pieces
    meta = jnp.stack([me, place, rank]).astype(jnp.int32)
    hbm = pltpu.MemorySpace.HBM
    sems = pltpu.SemaphoreType.DMA

    def packed(kernel, shape, arrays, scratch=None, vectors=None, **outs):
        return run(
            functools.partial(kernel, pieces),
            [(meta, SMEM)] + [(a, VMEM) for a in arrays],
            Box(packed=(shape, BF, VMEM), own=((shape[0] // pieces,) + shape[1:], BF, VMEM), **outs),
            scratch or Box(),
            vectors=vectors,
        )

    one_shape, two_shape, three_shape = (wide + BIAS_ROWS, 2 * units), (2 * width + units, wide), (depth + hidden, wide)
    pack_one = packed(
        pack_first, one_shape, [reset_proj, value_proj, rel_bias],
        Box(rows=pltpu.VMEM((BIAS_ROWS, 2 * units), F32), bias=pltpu.VMEM((BIAS_ROWS, 2 * units), BF)),
        Box(reset=reset_bias, value=value_bias, up=up_bias), rel=((8, 2 * GROUP), F32, VMEM),
    )

    decay_rows, mix_rows = ema_decay.T, (ema_feed * ema_read).T
    skip_row = ema_skip[None, :]
    ends = run(
        functools.partial(ema_ends, groups, comps, peers),
        [(meta, SMEM), (inputs, VMEM), (decay_rows, VMEM)],
        Box(r=[((rows, width), BF, hbm)] * peers, before=((tiles, comps, CHUNKS, LANES), F32, VMEM), end=((tiles, comps, LANES), F32, VMEM), fade=((tiles, comps, LANES), F32, VMEM)),
        Box(x=pltpu.VMEM((tiles, seq_rows, LANES), F32), sem=sems((peers,))),
        after=[pack_one.own],
        hides=HIDE_ENDS,
    )
    def gate(*arrays):
        ends.token, *arrays = lax.optimization_barrier((ends.token,) + arrays)
        return arrays

    pack_two = packed(pack_second, two_shape, gate(update_proj, mixer_proj, output_proj))
    pack_three = packed(pack_third, three_shape, gate(up_proj, down_proj))
    came_one = [later_than(x, ends) for x in far_pieces(pack_one)]
    pack_two.own, came_one[0] = lax.optimization_barrier((pack_two.own, came_one[0]))
    came_two = far_pieces(pack_two)
    next_one = next_pieces(came_one)
    raw_blocks = exchange(ends.r, "wa")
    earlier = group_totals(ends.end, ends.fade, "seq", False)
    earlier[-1], *raw_blocks = lax.optimization_barrier((earlier[-1], *raw_blocks))
    outs = Box(
        value=((seqs, seq_rows, width), F32, VMEM),
        start=((tiles, comps, CHUNKS, LANES), F32, VMEM),
    )
    outs.m = [((rows, width), BF, hbm)] * peers
    ema = run(
        functools.partial(ema_values, groups, comps, peers),
        [(meta, SMEM), (inputs, VMEM), (decay_rows, VMEM), (mix_rows, VMEM), (skip_row, VMEM), (ends.before, VMEM), (earlier, VMEM)],
        outs,
        Box(
            x=pltpu.VMEM((tiles, seq_rows, LANES), F32),
            y=pltpu.VMEM((tiles, seq_rows, LANES), F32),
            mixed=pltpu.VMEM((tok_rows, width), BF),
            sem=sems((peers,)),
        ),
        after=came_two + next_one,
        hides=HIDE_VALUES,
    )
    mixed_blocks = exchange(ema.m, "wa")
    held = (pack_three.own, pack_one.packed, pack_two.packed, *mixed_blocks)
    pack_three.own, pack_one.packed, pack_two.packed, *mixed_blocks = lax.optimization_barrier(held)
    came_three = far_pieces(pack_three)
    shards_one = all_shards(pack_one, came_one, next_one)
    next_two = next_pieces(came_two)
    next_two[0], came_three[0] = lax.optimization_barrier((next_two[0], came_three[0]))
    shards_two = all_shards(pack_two, came_two, next_two)

    count = len(jax.tree.leaves(shards_one))
    vec = Box(
        zeta=zeta_proj, zeta_bias=zeta_bias, query_gain=query_gain, query_shift=query_shift,
        key_gain=key_gain, rel=pack_one.rel, positions=positions,
        output_bias=output_bias, update_bias=update_bias,
    )
    fwd = run(
        functools.partial(attend_forward, peers),
        [(meta, SMEM), (mixed_blocks, hbm), (raw_blocks, hbm), (shards_one, hbm), (shards_two, hbm)],
        Box(
            mixed=((rows, wide), BF, VMEM), raw=((rows, wide), BF, VMEM), zeta_pre=((rows, Z), F32, VMEM),
            queries=((rows, Z), BF, VMEM), keys=((rows, Z), BF, VMEM), probs=((rows, GROUP), F32, VMEM),
            reset_pre=((peers, rows, units), F32, VMEM), value_pre=((peers, rows, units), F32, VMEM),
            values=((peers, rows, units), BF, VMEM), attended=((peers, rows, units), F32, VMEM),
            gated=((peers, rows, units), BF, VMEM), out_pre=((rows, wide), F32, VMEM), gate=((rows, wide), F32, VMEM),
            normed=((rows, wide), F32, VMEM), inv=((rows, 1), F32, VMEM), up_bias=((peers, 8, units), F32, VMEM),
        ),
        Box(
            mixed=pltpu.VMEM((peers, rows, width), BF), raw=pltpu.VMEM((peers, rows, width), BF),
            one=pltpu.VMEM((peers,) + one_shape, BF), two=pltpu.VMEM((peers,) + two_shape, BF),
            pre=pltpu.VMEM((rows, wide), F32), gate=pltpu.VMEM((rows, wide), F32),
            sem=sems((2 * peers + 2 * count,)),
        ),
        vectors=vec,
        limit=62,
        hides=HIDE_ATTEND,
    )
    next_three = [later_than(x, fwd) for x in next_pieces(came_three)]
    shards_three = all_shards(pack_three, came_three, next_three)

    vec = Box(
        first_gain=first_gain, first_shift=first_shift, down_bias=down_bias,
        second_gain=second_gain, second_shift=second_shift, up_bias=fwd.up_bias,
    )
    outs = Box(
        mid_grad=((rows, wide), F32, VMEM), second=((peers, rows, width), BF, VMEM), sums=((6 * wide // LANES // 8 * 8 + 8, LANES), F32, VMEM), up_bias=((peers, 8, LANES), F32, VMEM),
        grads=[((peers // 2,) + three_shape, BF, VMEM)] * 2,
    )
    ffn = run(
        functools.partial(feed_forward, peers, ranks),
        [(meta, SMEM), (lengths, SMEM), (shards_three, hbm), (fwd.normed, VMEM), (fwd.inv, VMEM), (targets, hbm)],
        outs,
        Box(
            three=pltpu.VMEM((peers,) + three_shape, BF), first=pltpu.VMEM((rows, wide), BF),
            total=pltpu.VMEM((rows, wide), F32), up_pre=pltpu.VMEM((peers, rows, hidden), F32),
            act=pltpu.VMEM((peers, rows, hidden), BF), grad=pltpu.VMEM((rows, wide), BF),
            upg=pltpu.VMEM((rows, hidden), BF), sem=sems((count,)), targets=pltpu.VMEM((rows, wide), BF), target_sem=sems(()),
        ),
        vectors=vec,
    )
    row_bits = bits_of(ranks)
    third_parts = core_sums(ffn.grads)

    one = run(
        functools.partial(attend_back_one, peers),
        [(meta, SMEM), (shards_two, hbm), (fwd.mixed, VMEM), (fwd.raw, VMEM), (ffn.mid_grad, VMEM), (fwd.out_pre, VMEM),
         (fwd.gate, VMEM), (fwd.reset_pre, VMEM), (fwd.attended, VMEM), (fwd.gated, VMEM)],
        Box(
            direct=((rows, wide), F32, VMEM), sums=((2 * wide // LANES // 8 * 8 + 8, LANES), F32, VMEM), mixed_grad=((peers, rows, width), F32, VMEM),
            attend_grad=((peers, rows, units), BF, VMEM), reset_grad=((peers, rows, units), BF, VMEM),
            bias=((peers, 8, LANES), F32, VMEM),
            grads=[((peers // 2,) + two_shape, BF, VMEM)] * 2,
        ),
        Box(
            two=pltpu.VMEM((peers,) + two_shape, BF), mixed=pltpu.VMEM((peers, rows, width), BF),
            block=pltpu.VMEM((rows, width), BF), pre_grad=pltpu.VMEM((rows, wide), BF),
            gate_grad=pltpu.VMEM((rows, wide), BF), sem=sems((count,)),
        ),
        after=[third_parts],
        hides=HIDE_ONE,
    )
    vec = Box(
        zeta=zeta_proj, query_gain=query_gain, key_gain=key_gain, positions=positions,
    )
    outs = Box(
        rel=((8, LANES), F32, VMEM), sums=((8, Z), F32, VMEM), zeta=((wide, Z), F32, VMEM),
        bias=((peers, 8, LANES), F32, VMEM),
        grads=[((peers // 2, wide, 2 * units), BF, VMEM)] * 2,
    )
    outs.m = [((rows, width), BF, hbm)] * peers
    outs.r = [((rows, 2 * width), BF, hbm)] * peers
    two = run(
        functools.partial(attend_back_two, peers),
        [(meta, SMEM), (shards_one, hbm), (fwd.mixed, VMEM), (fwd.raw, VMEM), (fwd.value_pre, VMEM), (fwd.values, VMEM),
         (fwd.probs, VMEM), (one.attend_grad, VMEM), (one.reset_grad, VMEM), (one.direct, VMEM), (one.mixed_grad, VMEM),
         (fwd.queries, VMEM), (fwd.keys, VMEM), (fwd.zeta_pre, VMEM), (ffn.second, VMEM)],
        outs,
        Box(
            one=pltpu.VMEM((peers,) + one_shape, BF), query_grad=pltpu.VMEM((rows, Z), F32),
            key_grad=pltpu.VMEM((rows, Z), F32), mixed=pltpu.VMEM((rows, wide), F32), raw=pltpu.VMEM((rows, wide), F32),
            vgrad=pltpu.VMEM((rows, units), BF), mixed_out=pltpu.VMEM((peers, rows, width), BF),
            raw_out=pltpu.VMEM((peers, rows, 2 * width), BF), sem=sems((max(count, 2 * peers),)),
        ),
        vectors=vec,
    )
    grad_blocks = exchange(two.m, "wa")
    third_rows = keep_rows(third_parts, row_bits[0], two)
    mark = beside(HIDE_TWO, two.rel)
    second_parts = core_sums(one.grads, mark)
    first_parts = core_sums(two.grads, mark)

    back = run(
        functools.partial(ema_back_ends, groups, comps, peers),
        [(meta, SMEM), (grad_blocks, hbm), (ema.value, VMEM), (decay_rows, VMEM)],
        Box(
            grad=((tiles, seq_rows, LANES), F32, VMEM), after=((tiles, comps, CHUNKS, LANES), F32, VMEM),
            first=((tiles, comps, LANES), F32, VMEM),
        ),
        Box(grad=pltpu.VMEM((tok_rows, width), BF), sem=sems((peers,))),
        after=[second_parts, first_parts, third_rows],
        hides=HIDE_BACK,
    )
    nears = []
    later = group_totals(back.first, ends.fade, "seq", True, nears)
    near = nears[-1]
    third_rows = shard_sum(third_rows, nears[0])
    for bit in row_bits[1:-1]:
        third_rows = keep_rows(third_rows, bit, nears[1])
    third_rows = plus(third_rows, later_than(swap(third_rows, "seq", row_bits[-1]), near))
    first_sum = keep_rows(first_parts, row_bits[0], nears[1])
    second_sum = shard_sum(second_parts, near)
    last = run(
        functools.partial(ema_back, groups, comps),
        [(meta, SMEM), (inputs, VMEM), (back.grad, VMEM), (decay_rows, VMEM), (mix_rows, VMEM), (skip_row, VMEM),
         (ema.start, VMEM), (back.after, VMEM), (later, VMEM)],
        Box(part=((tiles, seq_rows, LANES), F32, VMEM), sums=((-(-width // LANES), 2 * comps + 8, LANES), F32, VMEM)),
        Box(
            x=pltpu.VMEM((tiles, seq_rows, LANES), F32),
            states=pltpu.VMEM((seq_rows // CHUNKS, comps, CHUNKS, LANES), F32),
        ),
        after=[third_rows, first_sum, second_sum],
        hides=HIDE_LAST,
    )
    first_rows = shard_sum(first_sum, last)
    second_rows = keep_rows(second_sum, row_bits[0], last)
    def summed(total):
        for bit in row_bits[1:-1]:
            total = keep_rows(total, bit)
        return plus(total, swap(total, "seq", row_bits[-1]))

    first_rows, second_rows = summed(first_rows), summed(second_rows)
    first_rows, *rest_sent = lax.optimization_barrier((first_rows, *two.r))
    rest_blocks = exchange(rest_sent, "wa")
    joined = run(
        functools.partial(ema_join, groups, peers),
        [(meta, SMEM), (last.part, VMEM), (rest_blocks, hbm)],
        Box(grad=((seqs, seq_rows, width), F32, VMEM), block=((seqs, seq_rows, width), BF, VMEM)),
        Box(rest=pltpu.VMEM((tok_rows, 2 * width), BF), sem=sems((peers,))),
    )

    third_total = all_rows(third_rows, row_bits[:-1], last)
    second_total, first_total = all_rows(second_rows, row_bits[:-1]), all_rows(first_rows, row_bits[:-1])
    small = [ffn.sums, one.sums, two.sums, two.rel] + [a.reshape(-1, LANES) for a in (ffn.up_bias, one.bias, two.bias)]
    places = [0]
    for part in small:
        places.append(places[-1] + part.shape[0])
    small += [mark.token] + [mark.token for mark in nears] + [two.token, back.token, ema.token, ends.token, last.token, fwd.token]
    small.append(jnp.zeros((-sum(part.shape[0] for part in small) % 16, LANES), F32))
    small, zeta_grad = sum_small(jnp.concatenate(small, axis=0), two.zeta, [("wa", bit) for bit in bits_of(peers)])
    count = small.shape[0]
    small = jnp.concatenate([small, last.sums.reshape(-1, LANES)])
    small, zeta_grad = sum_small(small, zeta_grad, [("seq", bit) for bit in row_bits])
    ema_sums = small[count:].reshape(last.sums.shape)
    ema_sums = jnp.concatenate(list(ema_sums), axis=1)[:, :width]
    decay_grad = ema_sums[:comps].T * (ema_feed * ema_read)
    moment = ema_sums[comps : 2 * comps].T
    feed_grad, read_grad = moment * ema_read, moment * ema_feed
    skip_grad = ema_sums[2 * comps]
    parts = [small[a:b] for a, b in zip(places, places[1:])]
    tall = wide // LANES
    lines = [parts[0][i * tall : (i + 1) * tall].reshape(wide) for i in range(5)]
    lines += [parts[1][i * tall : (i + 1) * tall].reshape(wide) for i in range(2)]
    loss = parts[0][5 * tall, 0] + last.token[0, 0]
    zsums, rel_grad = parts[2], parts[3][:2].reshape(2 * GROUP)[: rel_bias.shape[0]]
    up_bias_grad, reset_bias_grad, value_bias_grad = (
        lax.dynamic_slice_in_dim(part, me * 8, 8, 0).reshape(8 * LANES)[:units] for part in parts[4:]
    )

    up_grad = jnp.concatenate([third_total[:depth, j * hidden : (j + 1) * hidden] for j in range(fold)], axis=0)
    return (
        joined.block, joined.grad, loss, decay_grad, feed_grad, read_grad, skip_grad, zeta_grad, zsums[0], zsums[1], zsums[2],
        zsums[3], rel_grad, first_total[:, :units].astype(F32), reset_bias_grad, first_total[:, units:].astype(F32), value_bias_grad,
        second_total[:width].astype(F32), lines[6], second_total[width : 2 * width].astype(F32), second_total[2 * width :].astype(F32), lines[5], lines[3],
        lines[4], up_grad.astype(F32), up_bias_grad, third_total[depth:].astype(F32), lines[2], lines[0], lines[1],
    )


def solution(mesh):
    return jax.shard_map(
        per_device,
        mesh=mesh,
        in_specs=(
            P(None, "seq", "wa"), P(None, "seq", None), P(), P(None, "seq"), P("wa", None), P("wa", None), P("wa", None), P("wa"),
            P(), P(), P(), P(), P(), P(), P(None, "wa"), P("wa"), P(None, "wa"), P("wa"), P("wa", None), P(), P("wa", None),
            P("wa", None), P(), P(), P(), P(None, "wa"), P("wa"), P("wa", None), P(), P(), P(),
        ),
        out_specs=(
            P(None, "seq", "wa"), P(None, "seq", "wa"), P(), P("wa", None), P("wa", None), P("wa", None), P("wa"), P(), P(), P(),
            P(), P(), P(), P(None, "wa"), P("wa"), P(None, "wa"), P("wa"), P("wa", None), P(), P("wa", None), P("wa", None), P(),
            P(), P(), P(None, "wa"), P("wa"), P("wa", None), P(), P(), P(),
        ),
        check_vma=False,
    )
```

```python
import functools

import jax
import jax.numpy as jnp
from jax import lax
from jax.experimental import pallas as pl
from jax.experimental.pallas import tpu as pltpu
from jax.sharding import PartitionSpec as P

Z = 128
GROUP = 128
LANES = 128
CHUNKS = 8
BIAS_ROWS = 32
HIDE_ENDS, HIDE_VALUES, HIDE_ATTEND, HIDE_ONE, HIDE_TWO, HIDE_BACK, HIDE_LAST, HIDE_JOIN = 20, 20, 20, 20, 40, 60, 15, 30
SHARE_BITS = 1
EPSILON = 1e-05
BF = jnp.bfloat16
F32 = jnp.float32
VMEM = pltpu.MemorySpace.VMEM
SMEM = pltpu.MemorySpace.SMEM


def dot(a, b):
    return jnp.dot(a, b, preferred_element_type=F32)


def dot_nt(a, b):
    return lax.dot_general(a, b, (((1,), (1,)), ((), ())), preferred_element_type=F32)


def dot_tn(a, b):
    return lax.dot_general(a, b, (((0,), (0,)), ((), ())), preferred_element_type=F32)


def sigmoid(v):
    return 1.0 / (1.0 + jnp.exp(-v))


def slope(v):
    s = sigmoid(v)
    return s * (1.0 + v * (1.0 - s))


def row(ref):
    return ref[...].reshape(1, ref.shape[0])


def put_line(ref, at, line):
    for j in range(0, line.shape[1], LANES):
        piece = line[:, j : j + LANES]
        ref[at + j // LANES : at + j // LANES + 1, : piece.shape[1]] = piece


def colsum(v):
    return jnp.sum(v, axis=0, keepdims=True)


def normalise(v):
    center = v - jnp.mean(v, axis=-1, keepdims=True)
    inv = lax.rsqrt(jnp.mean(center * center, axis=-1, keepdims=True) + EPSILON)
    return center * inv, inv


def norm_back(grad, normed, inv, gain):
    scaled = grad * gain
    one = jnp.mean(scaled, axis=-1, keepdims=True)
    two = jnp.mean(scaled * normed, axis=-1, keepdims=True)
    return inv * (scaled - one - normed * two)


class Box:
    def __init__(self, **parts):
        self.__dict__.update(parts)


jax.tree_util.register_pytree_node(
    Box, lambda box: (tuple(vars(box).values()), tuple(vars(box))), lambda names, parts: Box(**dict(zip(names, parts)))
)


def whole(space=VMEM):
    return pl.BlockSpec(memory_space=space)


def run(kernel, ins, outs, scratch, after=(), vectors=None, limit=48, hides=0):
    body, count = kernel, len(ins)
    vectors = vectors or Box()
    outs.token = ((8, LANES), F32, VMEM)
    fetched = len(vars(vectors))
    ins = ins + [(vectors, pltpu.MemorySpace.HBM), (list(after), pl.ANY)]
    scratch = Box(
        body=scratch, vec=jax.tree.map(lambda a: pltpu.VMEM(a.shape, a.dtype), vectors),
        sem=pltpu.SemaphoreType.DMA((max(fetched, 1),)),
    )

    def kernel(*refs):
        hbm, out, s = refs[count], refs[count + 2], refs[count + 3]
        copies = [
            pltpu.make_async_copy(vars(hbm)[name], vars(s.vec)[name], s.sem.at[i]) for i, name in enumerate(vars(hbm))
        ]
        for copy in copies:
            copy.start()
        if fetched:
            s.body.vec = s.vec
            s.body.wait = lambda: [copy.wait() for copy in copies]
        out.token[...] = jnp.zeros_like(out.token)
        body(*refs[:count], out, s.body)

    specs = [jax.tree.map(lambda _, space=space: whole(space), tree) for tree, space in ins]
    trees = [tree for tree, _ in ins]
    leaf = lambda entry: isinstance(entry, tuple)
    shapes = jax.tree.map(lambda e: jax.ShapeDtypeStruct(e[0], e[1]), outs, is_leaf=leaf)
    out_specs = jax.tree.map(lambda e: whole(e[2]), outs, is_leaf=leaf)
    return pl.pallas_call(
        kernel,
        out_shape=(shapes,),
        in_specs=specs,
        out_specs=(out_specs,),
        scratch_shapes=[scratch],
        compiler_params=pltpu.CompilerParams(vmem_limit_bytes=limit * 2**20),
        cost_estimate=pl.CostEstimate(flops=1 + int(hides * 1.15e9), bytes_accessed=1, transcendentals=0),
    )(*trees)[0]


def beside(hides, *deps):
    def kernel(ins, out, s):
        pass

    return run(kernel, [(list(deps), pl.ANY)], Box(), Box(), hides=hides)


def pack(pieces, meta, regions, out):
    height = out.own.shape[0]
    for ref, at, rows, top, left in regions:
        out.packed[top : top + rows, left : left + ref.shape[1]] = ref[at : at + rows, :]

    def piece(j):
        for ref, at, rows, top, left in regions:
            low, high = max(top, j * height), min(top + rows, (j + 1) * height)
            if low < high:
                out.own[low - j * height : high - j * height, left : left + ref.shape[1]] = ref[at + low - top : at + high - top, :]

    for j in range(pieces):
        pl.when(meta[1] == j)(lambda j=j: piece(j))


def pack_first(pieces, meta, reset, value, rel, out, s):
    units = reset.shape[1]
    s.wait()
    s.rows[...] = jnp.zeros_like(s.rows)
    for left, ref in ((0, s.vec.reset), (units, s.vec.value)):
        rest = row(ref)
        for i in range(3):
            high = rest.astype(BF).astype(F32)
            s.rows[i : i + 1, left : left + units] = high
            rest = rest - high
    s.rows[3:4, :units] = row(s.vec.up).astype(F32)
    s.bias[...] = s.rows[...].astype(BF)
    out.rel[...] = jnp.zeros_like(out.rel)
    out.rel[0:1, : rel.shape[0]] = row(rel)
    wide = reset.shape[0]
    pack(pieces, meta, [(reset, 0, wide, 0, 0), (value, 0, wide, 0, units), (s.bias, 0, BIAS_ROWS, wide, 0)], out)


def pack_second(pieces, meta, update, mixer, output, out, s):
    width, units = update.shape[0], output.shape[0]
    pack(pieces, meta, [(update, 0, width, 0, 0), (mixer, 0, width, width, 0), (output, 0, units, 2 * width, 0)], out)


def pack_third(pieces, meta, up, down, out, s):
    hidden = up.shape[1]
    depth = up.shape[0] // (down.shape[1] // hidden)
    regions = [(up, at, depth, 0, at // depth * hidden) for at in range(0, up.shape[0], depth)]
    pack(pieces, meta, regions + [(down, 0, hidden, depth, 0)], out)


def lane_groups(seqs, width):
    groups = []
    rest = width % LANES
    for s in range(seqs):
        for c in range(0, width - rest, LANES):
            groups.append([(s, c, LANES, 0)])
    tile, lane = [], 0
    for s in range(seqs if rest else 0):
        if lane + rest > LANES:
            groups.append(tile)
            tile, lane = [], 0
        tile.append((s, width - rest, rest, lane))
        lane += rest
    if tile:
        groups.append(tile)
    return groups


def join(parts):
    rows = parts[0].shape[0]
    used = sum(p.shape[1] for p in parts)
    if used < LANES:
        parts = parts + [jnp.zeros((rows, LANES - used), parts[0].dtype)]
    return parts[0] if len(parts) == 1 else jnp.concatenate(parts, axis=1)


def rows_of(group, ref):
    return join([ref[:, c : c + w] for _, c, w, _ in group])


def tokens_of(group, get):
    return join([get(s, c, w) for s, c, w, _ in group])


def spread(row):
    return jnp.broadcast_to(row, (CHUNKS, LANES))


def power(v, count):
    while count > 1:
        v = v * v
        count //= 2
    return v


def shifted(v, by):
    at = lax.broadcasted_iota(jnp.int32, v.shape, 0)
    moved = pltpu.roll(v, by % CHUNKS, 0)
    keep = at >= by if by > 0 else at < CHUNKS + by
    return jnp.where(keep, moved, 0.0)


def chunk_scan(ends, chunk_decay, sign):
    run_sum, factor, step = ends, chunk_decay, 1
    while step < CHUNKS:
        run_sum = run_sum + factor * shifted(run_sum, sign * step)
        factor, step = factor * factor, step * 2
    return run_sum, shifted(run_sum, sign)


def rank_power(chunk_decay, reverse):
    at = lax.broadcasted_iota(jnp.int32, chunk_decay.shape, 0)
    at = CHUNKS - 1 - at if reverse else at
    result, factor, bit = jnp.ones_like(chunk_decay), chunk_decay, 1
    while bit < CHUNKS:
        result = jnp.where((at & bit) != 0, result * factor, result)
        factor, bit = factor * factor, bit * 2
    return result


def steps_of(length, body, carry, reverse=False, unroll=4):
    def block(i, state):
        for u in range(unroll):
            t = i * unroll + u
            state = body(length - 1 - t if reverse else t, state)
        return state

    return lax.fori_loop(0, length // unroll, block, carry)


def at_step(ref, g, t, length):
    return ref.at[g, pl.ds(t, CHUNKS, stride=length), :]


def ema_ends(groups, comps, blocks, meta, x_ref, decay_ref, out, s):
    rows = x_ref.shape[1]
    part = x_ref.shape[0] * rows // blocks
    copies = []
    for k in range(blocks):
        at = (meta[0] ^ k) * part
        source = x_ref.at[at // rows, pl.ds(pl.multiple_of(at % rows, part), part), :]
        copies.append(pltpu.make_async_copy(source, out.r[k], s.sem.at[k]))
    for copy in copies:
        copy.start()
    length = x_ref.shape[1] // CHUNKS
    for g, group in enumerate(groups):
        s.x[g] = tokens_of(group, lambda q, c, w: x_ref[q, :, c : c + w].astype(F32))
        decay = rows_of(group, decay_ref)
        decays = [spread(decay[n : n + 1]) for n in range(comps)]

        def body(t, state):
            now = at_step(s.x, g, t, length)[...]
            return tuple(decays[n] * state[n] + now for n in range(comps))

        ends = steps_of(length, body, (jnp.zeros((CHUNKS, LANES), F32),) * comps)
        for n in range(comps):
            total, before = chunk_scan(ends[n], power(decays[n], length), 1)
            out.before[g, n] = before
            out.fade[g, n : n + 1, :] = power(decay[n : n + 1], length * CHUNKS)
            out.end[g, n : n + 1, :] = total[CHUNKS - 1 :]
    for copy in copies:
        copy.wait()


def carried(parts, device_decay, rank, reverse):
    total, passed = jnp.zeros_like(device_decay), jnp.ones_like(device_decay)
    for i, part in enumerate(parts):
        counts = ((rank // (1 << i)) % 2) == (0 if reverse else 1)
        total = jnp.where(counts, total + passed * part, total)
        passed = jnp.where(counts, passed * device_decay, passed)
        device_decay = device_decay * device_decay
    return total


def ema_values(groups, comps, blocks, meta, x_ref, decay_ref, mix_ref, skip_ref, before_ref, got, out, s):
    length = x_ref.shape[1] // CHUNKS
    width = x_ref.shape[2]
    seqs, rows = x_ref.shape[0], x_ref.shape[1]
    for g, group in enumerate(groups):
        s.x[g] = tokens_of(group, lambda q, c, w: x_ref[q, :, c : c + w].astype(F32))
        decay, mix, skip = rows_of(group, decay_ref), rows_of(group, mix_ref), rows_of(group, skip_ref)
        decays = [spread(decay[n : n + 1]) for n in range(comps)]
        mixes = [spread(mix[n : n + 1]) for n in range(comps)]
        skip = spread(skip)
        state_in = carried([part[g] for part in got], power(decay, length * CHUNKS), meta[2], False)
        start = []
        for n in range(comps):
            ranks = rank_power(power(decays[n], length), False)
            start.append(before_ref[g, n] + ranks * spread(state_in[n : n + 1]))
            out.start[g, n] = start[n]

        def body(t, state):
            now = at_step(s.x, g, t, length)[...]
            state = tuple(decays[n] * state[n] + now for n in range(comps))
            terms = [mixes[n] * state[n] for n in range(comps)] + [skip * now]
            while len(terms) > 1:
                terms = [a + b for a, b in zip(terms[::2], terms[1::2])] + (terms[-1:] if len(terms) % 2 else [])
            at_step(s.y, g, t, length)[...] = terms[0]
            return state

        steps_of(length, body, tuple(start))
        for q, c, w, lane in group:
            value = s.y[g, :, lane : lane + w]
            out.value[q, :, c : c + w] = value
            s.mixed[pl.ds(q * rows, rows), c : c + w] = (value * sigmoid(value)).astype(BF)
    part = seqs * rows // blocks
    copies = [
        pltpu.make_async_copy(
            s.mixed.at[pl.ds(pl.multiple_of((meta[0] ^ k) * part, part), part), :], out.m[k], s.sem.at[k]
        )
        for k in range(blocks)
    ]
    for copy in copies:
        copy.start()
    for copy in copies:
        copy.wait()


def ema_back_ends(groups, comps, blocks, meta, grads, value_ref, decay_ref, out, s):
    length = value_ref.shape[1] // CHUNKS
    rows = value_ref.shape[1]
    part = value_ref.shape[0] * rows // blocks
    copies = [
        pltpu.make_async_copy(
            grads[k], s.grad.at[pl.ds(pl.multiple_of((meta[0] ^ k) * part, part), part), :], s.sem.at[k]
        )
        for k in range(blocks)
    ]
    for copy in copies:
        copy.start()
    for copy in copies:
        copy.wait()
    for g, group in enumerate(groups):

        def load(q, c, w):
            return s.grad[pl.ds(q * rows, rows), c : c + w].astype(F32) * slope(value_ref[q, :, c : c + w])

        out.grad[g] = tokens_of(group, load)
        decay = rows_of(group, decay_ref)
        decays = [spread(decay[n : n + 1]) for n in range(comps)]

        def body(t, state):
            now = at_step(out.grad, g, t, length)[...]
            return tuple(decays[n] * state[n] + now for n in range(comps))

        ends = steps_of(length, body, (jnp.zeros((CHUNKS, LANES), F32),) * comps, reverse=True)
        for n in range(comps):
            total, after = chunk_scan(ends[n], power(decays[n], length), -1)
            out.after[g, n] = after
            out.first[g, n : n + 1, :] = total[:1]


def ema_join(groups, blocks, meta, part_ref, rests, out, s):
    seqs, rows, width = out.grad.shape
    part = seqs * rows // blocks
    copies = [
        pltpu.make_async_copy(
            rests[k], s.rest.at[pl.ds(pl.multiple_of((meta[0] ^ k) * part, part), part), :], s.sem.at[k]
        )
        for k in range(blocks)
    ]
    for copy in copies:
        copy.start()
    for copy in copies:
        copy.wait()
    for q in range(seqs):
        out.block[q] = s.rest[pl.ds(q * rows, rows), width:]
    for g, group in enumerate(groups):
        for q, c, w, lane in group:
            rest = s.rest[pl.ds(q * rows, rows), c : c + w].astype(F32)
            out.grad[q, :, c : c + w] = part_ref[g, :, lane : lane + w] + rest


def ema_back(groups, comps, meta, x_ref, grad_ref, decay_ref, mix_ref, skip_ref, start_ref, after_ref, got, out, s):
    length = x_ref.shape[1] // CHUNKS
    out.sums[...] = jnp.zeros_like(out.sums)
    half = comps // 2
    for g, group in enumerate(groups):
        s.x[g] = tokens_of(group, lambda q, c, w: x_ref[q, :, c : c + w].astype(F32))
        decay, mix, skip = rows_of(group, decay_ref), rows_of(group, mix_ref), rows_of(group, skip_ref)
        decays = [spread(decay[n : n + 1]) for n in range(comps)]
        mixes = [spread(mix[n : n + 1]) for n in range(comps)]
        skip = spread(skip)

        def forward(t, state):
            now = at_step(s.x, g, t, length)[...]
            for n in range(comps):
                s.states[t, n] = state[n]
            return tuple(decays[n] * state[n] + now for n in range(comps))

        steps_of(length, forward, tuple(start_ref[g, n] for n in range(comps)))
        grad_in = carried([p[g] for p in got], power(decay, length * CHUNKS), meta[2], True)
        for h in range(2):
            mine = range(h * half, (h + 1) * half)
            begin = []
            for n in mine:
                ranks = rank_power(power(decays[n], length), True)
                begin.append(after_ref[g, n] + ranks * spread(grad_in[n : n + 1]))
            zero = (jnp.zeros((CHUNKS, LANES), F32),) * half

            def backward(t, carry):
                grads, moments, changes, skips = carry
                now, up = at_step(s.x, g, t, length)[...], at_step(grad_ref, g, t, length)[...]
                grads = tuple(decays[n] * grads[i] + up for i, n in enumerate(mine))
                moments = tuple(moments[i] + grads[i] * now for i in range(half))
                changes = tuple(changes[i] + grads[i] * s.states[t, n] for i, n in enumerate(mine))
                terms = [mixes[n] * grads[i] for i, n in enumerate(mine)]
                if h == 0:
                    terms.append(skip * up)
                    skips = skips + up * now
                else:
                    terms.append(at_step(out.part, g, t, length)[...])
                while len(terms) > 1:
                    terms = [a + b for a, b in zip(terms[::2], terms[1::2])] + (terms[-1:] if len(terms) % 2 else [])
                at_step(out.part, g, t, length)[...] = terms[0]
                return grads, moments, changes, skips

            _, moments, changes, skips = steps_of(length, backward, (tuple(begin), zero, zero, zero[0]), reverse=True, unroll=2)
            for q, c, w, lane in group:
                for i, n in enumerate(mine):
                    out.sums[c // LANES, n : n + 1, :w] += colsum(changes[i])[:, lane : lane + w]
                    out.sums[c // LANES, comps + n : comps + n + 1, :w] += colsum(moments[i])[:, lane : lane + w]
                if h == 0:
                    out.sums[c // LANES, 2 * comps : 2 * comps + 1, :w] += colsum(skips)[:, lane : lane + w]


def weight_copies(meta, shards, dst, sem, first):
    copies = []
    for k, pieces in enumerate(shards):
        height = dst.shape[1] // len(pieces)
        for j, piece in enumerate(pieces):
            target = dst.at[k]
            if len(pieces) > 1:
                target = dst.at[k, pl.ds(pl.multiple_of((meta[1] ^ j) * height, height), height), :]
            copies.append(pltpu.make_async_copy(piece, target, sem.at[first + len(copies)]))
    return copies


def block_copies(meta, blocks, dst, sem, first):
    return [
        pltpu.make_async_copy(block, dst.at[meta[0] ^ k], sem.at[first + k]) for k, block in enumerate(blocks)
    ]


def positions_of(ref, start, g):
    at = start + g * GROUP
    length = ref.shape[1]
    columns = pl.ds(pl.multiple_of(at % length, GROUP), GROUP)
    place = ref[0:1, columns]
    for q in range(1, ref.shape[0]):
        place = jnp.where(at // length == q, ref[q : q + 1, columns], place)
    return place


def attend_forward(peers, meta, mixed, raw, first, second, out, s):
    vec = s.vec
    blocks = block_copies(meta, mixed, s.mixed, s.sem, 0)
    blocks += block_copies(meta, raw, s.raw, s.sem, peers)
    ones = weight_copies(meta, first, s.one, s.sem, 2 * peers)
    twos = weight_copies(meta, second, s.two, s.sem, 2 * peers + len(ones))
    for copy in blocks + ones + twos:
        copy.start()
    for copy in blocks:
        copy.wait()
    width = s.mixed.shape[2]
    units = s.one.shape[2] // 2
    rows, wide = out.mixed.shape
    groups = rows // GROUP
    for b in range(peers):
        out.mixed[:, b * width : (b + 1) * width] = s.mixed[b]
        out.raw[:, b * width : (b + 1) * width] = s.raw[b]
    s.wait()
    zeta_pre = dot(out.mixed[...], vec.zeta[...]) + row(vec.zeta_bias)
    out.zeta_pre[...] = zeta_pre
    act = zeta_pre * sigmoid(zeta_pre)
    queries = (act * row(vec.query_gain) + row(vec.query_shift)).astype(BF)
    keys = (act * row(vec.key_gain)).astype(BF)
    out.queries[...] = queries
    out.keys[...] = keys
    causal = lax.broadcasted_iota(jnp.int32, (GROUP, GROUP), 0) >= lax.broadcasted_iota(jnp.int32, (GROUP, GROUP), 1)
    for g in range(groups):
        at = slice(g * GROUP, (g + 1) * GROUP)
        place = jnp.broadcast_to(positions_of(vec.positions, meta[0] * rows, g).astype(F32), (GROUP, GROUP))
        distance = jnp.clip((place.T - place).astype(jnp.int32), 0, 2 * GROUP - 2)
        low = jnp.take_along_axis(
            jnp.broadcast_to(vec.rel[0:1, :GROUP], (GROUP, GROUP)), distance & (GROUP - 1), axis=1
        )
        high = jnp.take_along_axis(
            jnp.broadcast_to(vec.rel[0:1, GROUP:], (GROUP, GROUP)), distance & (GROUP - 1), axis=1
        )
        scores = dot_nt(queries[at], keys[at]) * Z**-0.5 + jnp.where(distance < GROUP, low, high)
        scores = jnp.where(causal, scores, -jnp.inf)
        shifted_exp = jnp.exp(scores - jnp.max(scores, axis=-1, keepdims=True))
        out.probs[at, :] = shifted_exp / jnp.sum(shifted_exp, axis=-1, keepdims=True)
    for copy in ones:
        copy.wait()
    for copy in twos:
        copy.wait()
    s.pre[...] = jnp.zeros_like(s.pre)
    s.gate[...] = jnp.zeros_like(s.gate)

    def shard(k, carry):
        biases = s.one[k, wide : wide + 16, :].astype(F32)
        bias = biases[0:1] + biases[1:2] + biases[2:3]
        out.up_bias[k] = jnp.broadcast_to(biases[3:4, :units], (8, units))
        reset_pre = dot(out.mixed[...], s.one[k, :wide, :units]) + bias[:, :units]
        value_pre = dot(out.raw[...], s.one[k, :wide, units:]) + bias[:, units:]
        values = (value_pre * sigmoid(value_pre)).astype(BF)
        out.reset_pre[k] = reset_pre
        out.value_pre[k] = value_pre
        out.values[k] = values
        for g in range(groups):
            at = slice(g * GROUP, (g + 1) * GROUP)
            out.attended[k, at, :] = dot(out.probs[at, :].astype(BF), values[at])
        gated = (reset_pre * sigmoid(reset_pre) * out.attended[k]).astype(BF)
        out.gated[k] = gated
        block = s.mixed[meta[0] ^ k]
        s.gate[...] += dot(block, s.two[k, :width, :])
        s.pre[...] += dot(block, s.two[k, width : 2 * width, :]) + dot(gated, s.two[k, 2 * width :, :])
        return carry

    lax.fori_loop(0, peers, shard, 0)
    out_pre = s.pre[...] + row(vec.output_bias)
    out.out_pre[...] = out_pre
    gate = sigmoid(s.gate[...] + row(vec.update_bias))
    out.gate[...] = gate
    mid = gate * (out_pre * sigmoid(out_pre)) + (1.0 - gate) * out.raw[...].astype(F32)
    normed, inv = normalise(mid)
    out.normed[...] = normed
    out.inv[...] = inv


def feed_forward(peers, ranks, meta, lengths, third, normed_ref, inv_ref, targets, out, s):
    vec = s.vec
    rows = normed_ref.shape[0]
    seqs, seq_rows = targets.shape[0], targets.shape[1]
    seq, offset = meta[0] * rows // seq_rows, pl.multiple_of(meta[0] * rows % seq_rows, rows)
    fetch = pltpu.make_async_copy(targets.at[seq, pl.ds(offset, rows), :], s.targets, s.target_sem)
    fetch.start()
    threes = weight_copies(meta, third, s.three, s.sem, 0)
    for copy in threes:
        copy.start()
    rows, width = normed_ref.shape
    s.wait()
    units = vec.up_bias.shape[2]
    fold = width // units
    depth = width // fold
    first = normed_ref[...] * row(vec.first_gain) + row(vec.first_shift)
    s.first[...] = first.astype(BF)
    s.total[...] = first + row(vec.down_bias)
    for copy in threes:
        copy.wait()

    def forward(k, carry):
        pre = vec.up_bias[k, 0:1, :]
        for j in range(fold):
            pre = pre + dot(
                s.first[:, j * depth : (j + 1) * depth], s.three[k, :depth, j * units : (j + 1) * units]
            )
        s.up_pre[k] = pre
        act = (pre * sigmoid(pre)).astype(BF)
        s.act[k] = act
        s.total[...] += dot(act, s.three[k, depth:, :])
        return carry

    lax.fori_loop(0, peers, forward, 0)
    normed, inv = normalise(s.total[...])
    second = normed * row(vec.second_gain) + row(vec.second_shift)
    piece = width // peers
    for b in range(peers):
        out.second[b] = second[:, b * piece : (b + 1) * piece].astype(BF)
    fetch.wait()
    misfit = second - s.targets[...].astype(F32)
    place = lax.broadcasted_iota(jnp.int32, (rows, 1), 0) + (meta[2] * seq_rows + offset)
    weight = (place < lengths[seq]).astype(F32)
    tokens = lengths[0]
    for q in range(1, seqs):
        tokens = tokens + lengths[q]
    true_count = jnp.broadcast_to(tokens, (rows, 1)).astype(F32)
    losses = jnp.sum(misfit * misfit, axis=1, keepdims=True) * (weight / (2.0 * width * true_count))
    out.sums[...] = jnp.zeros_like(out.sums)
    out.up_bias[...] = jnp.zeros_like(out.up_bias)
    lines = width // LANES
    put_line(out.sums, 5 * lines, jnp.broadcast_to(jnp.sum(losses, axis=0, keepdims=True), (1, LANES)))
    grad_out = misfit * (weight * (seqs * seq_rows * ranks / true_count))
    put_line(out.sums, 0, colsum(grad_out * normed))
    put_line(out.sums, lines, colsum(grad_out))
    second_grad = norm_back(grad_out, normed, inv, row(vec.second_gain))
    ffn_grad = second_grad.astype(BF)
    s.grad[...] = ffn_grad
    put_line(out.sums, 2 * lines, colsum(ffn_grad.astype(F32)))
    s.total[...] = second_grad

    def backward(k, carry):
        keep = k // 2
        down = dot_tn(s.act[k], s.grad[...]).astype(BF)
        up_grad = (dot_nt(s.grad[...], s.three[k, depth:, :]) * slope(s.up_pre[k])).astype(BF)
        put_line(out.up_bias.at[meta[0] ^ k], 0, colsum(up_grad.astype(F32)))
        s.upg[...] = up_grad
        ups = [dot_tn(s.first[:, j * depth : (j + 1) * depth], s.upg[...]).astype(BF) for j in range(fold)]

        def store(which):
            out.grads[which][keep, depth:, :] = down
            for j in range(fold):
                out.grads[which][keep, :depth, j * units : (j + 1) * units] = ups[j]

        pl.when(k % 2 == 0)(lambda: store(0))
        pl.when(k % 2 == 1)(lambda: store(1))
        for j in range(fold):
            s.total[:, j * depth : (j + 1) * depth] += dot_nt(
                s.upg[...], s.three[k, :depth, j * units : (j + 1) * units]
            )
        return carry

    lax.fori_loop(0, peers, backward, 0)
    first_grad = s.total[...]
    put_line(out.sums, 3 * lines, colsum(first_grad * normed_ref[...]))
    put_line(out.sums, 4 * lines, colsum(first_grad))
    out.mid_grad[...] = norm_back(first_grad, normed_ref[...], inv_ref[...], row(vec.first_gain))


def attend_back_one(peers, meta, second, mixed_ref, raw_ref, mid_ref, pre_ref, gate_ref, reset_ref, attended_ref, gated_ref, out, s):
    twos = weight_copies(meta, second, s.two, s.sem, 0)
    for copy in twos:
        copy.start()
    rows, wide = mixed_ref.shape
    width = wide // peers
    for b in range(peers):
        s.mixed[b] = mixed_ref[:, b * width : (b + 1) * width]
    mid, gate, pre = mid_ref[...], gate_ref[...], pre_ref[...]
    pre_grad = (mid * gate * slope(pre)).astype(BF)
    s.pre_grad[...] = pre_grad
    gate_grad = (mid * (pre * sigmoid(pre) - raw_ref[...].astype(F32)) * gate * (1.0 - gate)).astype(BF)
    s.gate_grad[...] = gate_grad
    out.direct[...] = mid * (1.0 - gate)
    out.sums[...] = jnp.zeros_like(out.sums)
    out.bias[...] = jnp.zeros_like(out.bias)
    put_line(out.sums, 0, colsum(pre_grad.astype(F32)))
    put_line(out.sums, wide // LANES, colsum(gate_grad.astype(F32)))
    for copy in twos:
        copy.wait()

    def shard(k, carry):
        keep = k // 2
        s.block[...] = s.mixed[meta[0] ^ k]
        update = dot_tn(s.block[...], s.gate_grad[...]).astype(BF)
        mixer = dot_tn(s.block[...], s.pre_grad[...]).astype(BF)
        output = dot_tn(gated_ref[k], s.pre_grad[...]).astype(BF)

        def store(which):
            out.grads[which][keep, :width, :] = update
            out.grads[which][keep, width : 2 * width, :] = mixer
            out.grads[which][keep, 2 * width :, :] = output

        pl.when(k % 2 == 0)(lambda: store(0))
        pl.when(k % 2 == 1)(lambda: store(1))
        out.mixed_grad[k] = dot_nt(s.gate_grad[...], s.two[k, :width, :]) + dot_nt(
            s.pre_grad[...], s.two[k, width : 2 * width, :]
        )
        gated_grad = dot_nt(s.pre_grad[...], s.two[k, 2 * width :, :])
        reset = reset_ref[k]
        out.attend_grad[k] = (gated_grad * (reset * sigmoid(reset))).astype(BF)
        reset_grad = (gated_grad * attended_ref[k] * slope(reset)).astype(BF)
        out.reset_grad[k] = reset_grad
        put_line(out.bias.at[meta[0] ^ k], 0, colsum(reset_grad.astype(F32)))
        return carry

    lax.fori_loop(0, peers, shard, 0)


def attend_back_two(
    peers, meta, first, mixed_ref, raw_ref, value_pre_ref, values_ref, probs_ref, agrad_ref, rgrad_ref, direct_ref, local_ref,
    queries_ref, keys_ref, zeta_pre_ref, second_ref, out, s,
):
    vec = s.vec
    ones = weight_copies(meta, first, s.one, s.sem, 0)
    for copy in ones:
        copy.start()
    rows, wide = mixed_ref.shape
    width = wide // peers
    units = values_ref.shape[2]
    groups = rows // GROUP
    s.wait()
    act = zeta_pre_ref[...] * sigmoid(zeta_pre_ref[...])
    line = lax.broadcasted_iota(jnp.int32, (2 * GROUP, GROUP), 0)
    buckets = jnp.zeros((1, 2 * GROUP), F32)
    for g in range(groups):
        at = slice(g * GROUP, (g + 1) * GROUP)

        def score(k, total):
            return total + dot_nt(agrad_ref[k, at, :], values_ref[k, at, :])

        prob_grad = lax.fori_loop(0, peers, score, jnp.zeros((GROUP, GROUP), F32))
        probs = probs_ref[at, :]
        row_dot = jnp.sum(probs * prob_grad, axis=-1, keepdims=True)
        sgrad = (probs * (prob_grad - row_dot)).astype(BF)
        s.query_grad[at, :] = dot(sgrad, keys_ref[at, :]) * Z**-0.5
        s.key_grad[at, :] = dot_tn(sgrad, queries_ref[at, :]) * Z**-0.5
        ahead = positions_of(vec.positions, meta[0] * rows, g)
        ahead = ahead - ahead[:, 0:1]
        to_row = (line == ahead).astype(BF)
        to_column = (line == 2 * GROUP - 1 - ahead).astype(BF)
        table = dot(to_row, dot_nt(sgrad, to_column).astype(BF))
        buckets = buckets + colsum(pltpu.roll(table, 1, 1, stride=1, stride_axis=0))
    out.rel[...] = jnp.zeros_like(out.rel)
    out.bias[...] = jnp.zeros_like(out.bias)
    put_line(out.rel, 0, buckets)
    query_grad, key_grad = s.query_grad[...], s.key_grad[...]
    zeta_grad = (query_grad * row(vec.query_gain) + key_grad * row(vec.key_gain)) * slope(zeta_pre_ref[...])
    zeta_grad = zeta_grad.astype(BF)
    out.sums[...] = jnp.zeros_like(out.sums)
    out.sums[0:1, :] = colsum(zeta_grad.astype(F32))
    out.sums[1:2, :] = colsum(query_grad * act)
    out.sums[2:3, :] = colsum(query_grad)
    out.sums[3:4, :] = colsum(key_grad * act)
    out.zeta[...] = dot_tn(mixed_ref[...], zeta_grad)
    s.mixed[...] = dot_nt(zeta_grad, vec.zeta[...])
    s.raw[...] = direct_ref[...]
    for copy in ones:
        copy.wait()

    def shard(k, carry):
        keep = k // 2
        for g in range(groups):
            at = slice(g * GROUP, (g + 1) * GROUP)
            vals_grad = dot_tn(probs_ref[at, :].astype(BF), agrad_ref[k, at, :])
            s.vgrad[at, :] = (vals_grad * slope(value_pre_ref[k, at, :])).astype(BF)
        put_line(out.bias.at[meta[0] ^ k], 0, colsum(s.vgrad[...].astype(F32)))
        reset = dot_tn(mixed_ref[...], rgrad_ref[k]).astype(BF)
        value = dot_tn(raw_ref[...], s.vgrad[...]).astype(BF)

        def store(which):
            out.grads[which][keep, :, :units] = reset
            out.grads[which][keep, :, units:] = value

        pl.when(k % 2 == 0)(lambda: store(0))
        pl.when(k % 2 == 1)(lambda: store(1))
        s.mixed[...] += dot_nt(rgrad_ref[k], s.one[k, :wide, :units])
        s.raw[...] += dot_nt(s.vgrad[...], s.one[k, :wide, units:])
        return carry

    lax.fori_loop(0, peers, shard, 0)
    for b in range(peers):
        at = slice(b * width, (b + 1) * width)
        s.mixed_out[b] = (s.mixed[:, at] + local_ref[meta[0] ^ b]).astype(BF)
        s.raw_out[b, :, :width] = s.raw[:, at].astype(BF)
        s.raw_out[b, :, width:] = second_ref[b]
    sends = []
    for k in range(peers):
        sends.append(pltpu.make_async_copy(s.mixed_out.at[meta[0] ^ k], out.m[k], s.sem.at[2 * k]))
        sends.append(pltpu.make_async_copy(s.raw_out.at[meta[0] ^ k], out.r[k], s.sem.at[2 * k + 1]))
    for copy in sends:
        copy.start()
    for copy in sends:
        copy.wait()


def swap(x, axis, by):
    size = lax.axis_size(axis)
    return lax.ppermute(x, axis, [(i, i ^ by) for i in range(size)])


def later_than(x, *marks):
    for mark in marks:
        x, mark.token = lax.optimization_barrier((x, mark.token))
    return x


def exchange(blocks, axis):
    return [blocks[0]] + [swap(blocks[k], axis, k) for k in range(1, len(blocks))]


def group_totals(total, fade, axis, reverse, nears=None):
    result = []
    for bit in bits_of(lax.axis_size(axis)):
        other = swap(total, axis, bit)
        if nears is not None:
            nears.append(beside(0, other))
            other, nears[-1].token = lax.optimization_barrier((other, nears[-1].token))
        result.append(other)
        upper = ((lax.axis_index(axis) // bit) % 2) == (0 if reverse else 1)
        total = jnp.where(upper, total + fade * other, other + fade * total)
        fade = fade * fade
    return result


def far_pieces(pack):
    return [swap(pack.own, "wa", k) for k in range(2, lax.axis_size("wa"), 2)]


def next_pieces(came):
    return [swap(piece, "seq", j) for piece in came for j in range(1, 1 << SHARE_BITS)]


def all_shards(pack, came, beyond):
    others = (1 << SHARE_BITS) - 1
    shards = [[pack.packed]]
    shards += [[came[i]] + beyond[i * others : (i + 1) * others] for i in range(len(came))]
    return [pieces for even in shards for pieces in (even, [swap(piece, "wa", 1) for piece in even])]


def plus(a, b):
    return (a.astype(F32) + b.astype(F32)).astype(a.dtype)


def core_sums(grads, *deps):
    return plus(grads[0], later_than(swap(grads[1], "wa", 1), *deps))


def shard_sum(parts, *deps):
    step = 2
    while parts.shape[0] > 1:
        parts = plus(parts[::2], later_than(swap(parts[1::2], "wa", step), *deps))
        step *= 2
    return parts[0]


def keep_rows(total, bit, *deps):
    here = (lax.axis_index("seq") // bit) % 2
    height = total.shape[-2] // 2
    mine = lax.dynamic_slice_in_dim(total, here * height, height, total.ndim - 2)
    theirs = lax.dynamic_slice_in_dim(total, (1 - here) * height, height, total.ndim - 2)
    return plus(mine, later_than(swap(theirs, "seq", bit), *deps))


def all_rows(total, bits, *deps):
    for bit in bits[::-1]:
        here = (lax.axis_index("seq") // bit) % 2
        other = later_than(swap(total, "seq", bit), *(deps if bit == bits[-1] else ()))
        total = jnp.where(
            here == 0, jnp.concatenate([total, other], axis=0), jnp.concatenate([other, total], axis=0)
        )
    return total


def sum_small(exact, rough, route):
    for axis, bit in route:
        high = lax.reduce_precision(exact, 8, 7)
        sent = jnp.concatenate([high.astype(BF), (exact - high).astype(BF), rough.astype(BF)])
        total = sent.astype(F32) + swap(sent, axis, bit).astype(F32)
        rows = exact.shape[0]
        exact, rough = total[:rows] + total[rows : 2 * rows], total[2 * rows :]
    return exact, rough


def bits_of(size):
    return [1 << b for b in range(size.bit_length() - 1)]


def per_device(
    inputs, targets, lengths, positions, ema_decay, ema_feed, ema_read, ema_skip, zeta_proj, zeta_bias, query_gain, query_shift,
    key_gain, rel_bias, reset_proj, reset_bias, value_proj, value_bias, update_proj, update_bias, mixer_proj, output_proj,
    output_bias, first_gain, first_shift, up_proj, up_bias, down_proj, down_bias, second_gain, second_shift,
):
    seqs, seq_rows, width = inputs.shape
    wide = targets.shape[2]
    comps = ema_decay.shape[1]
    peers, ranks = lax.axis_size("wa"), lax.axis_size("seq")
    me, rank = lax.axis_index("wa"), lax.axis_index("seq")
    tok_rows = seqs * seq_rows
    rows = tok_rows // peers
    n_groups = rows // GROUP
    units, hidden = reset_proj.shape[1], up_proj.shape[1]
    fold = wide // hidden
    depth = wide // fold
    total_tokens = tok_rows * ranks
    groups = lane_groups(seqs, width)
    tiles = len(groups)
    pieces = 1 << SHARE_BITS
    place = rank % pieces
    meta = jnp.stack([me, place, rank]).astype(jnp.int32)
    hbm = pltpu.MemorySpace.HBM
    sems = pltpu.SemaphoreType.DMA

    def packed(kernel, shape, arrays, scratch=None, vectors=None, **outs):
        return run(
            functools.partial(kernel, pieces),
            [(meta, SMEM)] + [(a, VMEM) for a in arrays],
            Box(packed=(shape, BF, VMEM), own=((shape[0] // pieces,) + shape[1:], BF, VMEM), **outs),
            scratch or Box(),
            vectors=vectors,
        )

    one_shape, two_shape, three_shape = (wide + BIAS_ROWS, 2 * units), (2 * width + units, wide), (depth + hidden, wide)
    pack_one = packed(
        pack_first, one_shape, [reset_proj, value_proj, rel_bias],
        Box(rows=pltpu.VMEM((BIAS_ROWS, 2 * units), F32), bias=pltpu.VMEM((BIAS_ROWS, 2 * units), BF)),
        Box(reset=reset_bias, value=value_bias, up=up_bias), rel=((8, 2 * GROUP), F32, VMEM),
    )

    decay_rows, mix_rows = ema_decay.T, (ema_feed * ema_read).T
    skip_row = ema_skip[None, :]
    ends = run(
        functools.partial(ema_ends, groups, comps, peers),
        [(meta, SMEM), (inputs, VMEM), (decay_rows, VMEM)],
        Box(r=[((rows, width), BF, hbm)] * peers, before=((tiles, comps, CHUNKS, LANES), F32, VMEM), end=((tiles, comps, LANES), F32, VMEM), fade=((tiles, comps, LANES), F32, VMEM)),
        Box(x=pltpu.VMEM((tiles, seq_rows, LANES), F32), sem=sems((peers,))),
        after=[pack_one.own],
        hides=HIDE_ENDS,
    )
    def gate(*arrays):
        ends.token, *arrays = lax.optimization_barrier((ends.token,) + arrays)
        return arrays

    pack_two = packed(pack_second, two_shape, gate(update_proj, mixer_proj, output_proj))
    pack_three = packed(pack_third, three_shape, gate(up_proj, down_proj))
    came_one = [later_than(x, ends) for x in far_pieces(pack_one)]
    pack_two.own, came_one[0] = lax.optimization_barrier((pack_two.own, came_one[0]))
    came_two = far_pieces(pack_two)
    next_one = next_pieces(came_one)
    raw_blocks = exchange(ends.r, "wa")
    earlier = group_totals(ends.end, ends.fade, "seq", False)
    earlier[-1], *raw_blocks = lax.optimization_barrier((earlier[-1], *raw_blocks))
    outs = Box(
        value=((seqs, seq_rows, width), F32, VMEM),
        start=((tiles, comps, CHUNKS, LANES), F32, VMEM),
    )
    outs.m = [((rows, width), BF, hbm)] * peers
    ema = run(
        functools.partial(ema_values, groups, comps, peers),
        [(meta, SMEM), (inputs, VMEM), (decay_rows, VMEM), (mix_rows, VMEM), (skip_row, VMEM), (ends.before, VMEM), (earlier, VMEM)],
        outs,
        Box(
            x=pltpu.VMEM((tiles, seq_rows, LANES), F32),
            y=pltpu.VMEM((tiles, seq_rows, LANES), F32),
            mixed=pltpu.VMEM((tok_rows, width), BF),
            sem=sems((peers,)),
        ),
        after=came_two + next_one,
        hides=HIDE_VALUES,
    )
    mixed_blocks = exchange(ema.m, "wa")
    next_two = [later_than(x, ema) for x in next_pieces(came_two)]
    pack_three.own, came_two[0] = lax.optimization_barrier((pack_three.own, came_two[0]))
    came_three = [later_than(x, ema) for x in far_pieces(pack_three)]
    held = (pack_two.packed, next_two[0], came_three[0], *mixed_blocks)
    pack_two.packed, next_two[0], came_three[0], *mixed_blocks = lax.optimization_barrier(held)
    shards_one = all_shards(pack_one, came_one, next_one)
    shards_one[1][0] = later_than(shards_one[1][0], ema)
    shards_two = all_shards(pack_two, came_two, next_two)

    count = len(jax.tree.leaves(shards_one))
    vec = Box(
        zeta=zeta_proj, zeta_bias=zeta_bias, query_gain=query_gain, query_shift=query_shift,
        key_gain=key_gain, rel=pack_one.rel, positions=positions,
        output_bias=output_bias, update_bias=update_bias,
    )
    fwd = run(
        functools.partial(attend_forward, peers),
        [(meta, SMEM), (mixed_blocks, hbm), (raw_blocks, hbm), (shards_one, hbm), (shards_two, hbm)],
        Box(
            mixed=((rows, wide), BF, VMEM), raw=((rows, wide), BF, VMEM), zeta_pre=((rows, Z), F32, VMEM),
            queries=((rows, Z), BF, VMEM), keys=((rows, Z), BF, VMEM), probs=((rows, GROUP), F32, VMEM),
            reset_pre=((peers, rows, units), F32, VMEM), value_pre=((peers, rows, units), F32, VMEM),
            values=((peers, rows, units), BF, VMEM), attended=((peers, rows, units), F32, VMEM),
            gated=((peers, rows, units), BF, VMEM), out_pre=((rows, wide), F32, VMEM), gate=((rows, wide), F32, VMEM),
            normed=((rows, wide), F32, VMEM), inv=((rows, 1), F32, VMEM), up_bias=((peers, 8, units), F32, VMEM),
        ),
        Box(
            mixed=pltpu.VMEM((peers, rows, width), BF), raw=pltpu.VMEM((peers, rows, width), BF),
            one=pltpu.VMEM((peers,) + one_shape, BF), two=pltpu.VMEM((peers,) + two_shape, BF),
            pre=pltpu.VMEM((rows, wide), F32), gate=pltpu.VMEM((rows, wide), F32),
            sem=sems((2 * peers + 2 * count,)),
        ),
        vectors=vec,
        limit=62,
        hides=HIDE_ATTEND,
    )
    next_three = [later_than(x, fwd) for x in next_pieces(came_three)]
    shards_three = all_shards(pack_three, came_three, next_three)

    vec = Box(
        first_gain=first_gain, first_shift=first_shift, down_bias=down_bias,
        second_gain=second_gain, second_shift=second_shift, up_bias=fwd.up_bias,
    )
    outs = Box(
        mid_grad=((rows, wide), F32, VMEM), second=((peers, rows, width), BF, VMEM), sums=((6 * wide // LANES // 8 * 8 + 8, LANES), F32, VMEM), up_bias=((peers, 8, LANES), F32, VMEM),
        grads=[((peers // 2,) + three_shape, BF, VMEM)] * 2,
    )
    ffn = run(
        functools.partial(feed_forward, peers, ranks),
        [(meta, SMEM), (lengths, SMEM), (shards_three, hbm), (fwd.normed, VMEM), (fwd.inv, VMEM), (targets, hbm)],
        outs,
        Box(
            three=pltpu.VMEM((peers,) + three_shape, BF), first=pltpu.VMEM((rows, wide), BF),
            total=pltpu.VMEM((rows, wide), F32), up_pre=pltpu.VMEM((peers, rows, hidden), F32),
            act=pltpu.VMEM((peers, rows, hidden), BF), grad=pltpu.VMEM((rows, wide), BF),
            upg=pltpu.VMEM((rows, hidden), BF), sem=sems((count,)), targets=pltpu.VMEM((rows, wide), BF), target_sem=sems(()),
        ),
        vectors=vec,
    )
    row_bits = bits_of(ranks)
    third_parts = core_sums(ffn.grads)

    one = run(
        functools.partial(attend_back_one, peers),
        [(meta, SMEM), (shards_two, hbm), (fwd.mixed, VMEM), (fwd.raw, VMEM), (ffn.mid_grad, VMEM), (fwd.out_pre, VMEM),
         (fwd.gate, VMEM), (fwd.reset_pre, VMEM), (fwd.attended, VMEM), (fwd.gated, VMEM)],
        Box(
            direct=((rows, wide), F32, VMEM), sums=((2 * wide // LANES // 8 * 8 + 8, LANES), F32, VMEM), mixed_grad=((peers, rows, width), F32, VMEM),
            attend_grad=((peers, rows, units), BF, VMEM), reset_grad=((peers, rows, units), BF, VMEM),
            bias=((peers, 8, LANES), F32, VMEM),
            grads=[((peers // 2,) + two_shape, BF, VMEM)] * 2,
        ),
        Box(
            two=pltpu.VMEM((peers,) + two_shape, BF), mixed=pltpu.VMEM((peers, rows, width), BF),
            block=pltpu.VMEM((rows, width), BF), pre_grad=pltpu.VMEM((rows, wide), BF),
            gate_grad=pltpu.VMEM((rows, wide), BF), sem=sems((count,)),
        ),
        after=[third_parts],
        hides=HIDE_ONE,
    )
    vec = Box(
        zeta=zeta_proj, query_gain=query_gain, key_gain=key_gain, positions=positions,
    )
    outs = Box(
        rel=((8, LANES), F32, VMEM), sums=((8, Z), F32, VMEM), zeta=((wide, Z), F32, VMEM),
        bias=((peers, 8, LANES), F32, VMEM),
        grads=[((peers // 2, wide, 2 * units), BF, VMEM)] * 2,
    )
    outs.m = [((rows, width), BF, hbm)] * peers
    outs.r = [((rows, 2 * width), BF, hbm)] * peers
    two = run(
        functools.partial(attend_back_two, peers),
        [(meta, SMEM), (shards_one, hbm), (fwd.mixed, VMEM), (fwd.raw, VMEM), (fwd.value_pre, VMEM), (fwd.values, VMEM),
         (fwd.probs, VMEM), (one.attend_grad, VMEM), (one.reset_grad, VMEM), (one.direct, VMEM), (one.mixed_grad, VMEM),
         (fwd.queries, VMEM), (fwd.keys, VMEM), (fwd.zeta_pre, VMEM), (ffn.second, VMEM)],
        outs,
        Box(
            one=pltpu.VMEM((peers,) + one_shape, BF), query_grad=pltpu.VMEM((rows, Z), F32),
            key_grad=pltpu.VMEM((rows, Z), F32), mixed=pltpu.VMEM((rows, wide), F32), raw=pltpu.VMEM((rows, wide), F32),
            vgrad=pltpu.VMEM((rows, units), BF), mixed_out=pltpu.VMEM((peers, rows, width), BF),
            raw_out=pltpu.VMEM((peers, rows, 2 * width), BF), sem=sems((max(count, 2 * peers),)),
        ),
        vectors=vec,
    )
    grad_blocks = exchange(two.m, "wa")
    third_rows = keep_rows(third_parts, row_bits[0], two)
    mark = beside(HIDE_TWO, two.rel)
    second_parts = core_sums(one.grads, mark)
    first_parts = core_sums(two.grads, mark)

    back = run(
        functools.partial(ema_back_ends, groups, comps, peers),
        [(meta, SMEM), (grad_blocks, hbm), (ema.value, VMEM), (decay_rows, VMEM)],
        Box(
            grad=((tiles, seq_rows, LANES), F32, VMEM), after=((tiles, comps, CHUNKS, LANES), F32, VMEM),
            first=((tiles, comps, LANES), F32, VMEM),
        ),
        Box(grad=pltpu.VMEM((tok_rows, width), BF), sem=sems((peers,))),
        after=[second_parts, first_parts, third_rows],
        hides=HIDE_BACK,
    )
    nears = []
    later = group_totals(back.first, ends.fade, "seq", True, nears)
    near = nears[-1]
    third_rows = shard_sum(third_rows, nears[0])
    for bit in row_bits[1:-1]:
        third_rows = keep_rows(third_rows, bit, nears[1])
    third_rows = plus(third_rows, later_than(swap(third_rows, "seq", row_bits[-1]), near))
    first_sum = keep_rows(first_parts, row_bits[0], nears[1])
    second_sum = shard_sum(second_parts, near)
    last = run(
        functools.partial(ema_back, groups, comps),
        [(meta, SMEM), (inputs, VMEM), (back.grad, VMEM), (decay_rows, VMEM), (mix_rows, VMEM), (skip_row, VMEM),
         (ema.start, VMEM), (back.after, VMEM), (later, VMEM)],
        Box(part=((tiles, seq_rows, LANES), F32, VMEM), sums=((-(-width // LANES), 2 * comps + 8, LANES), F32, VMEM)),
        Box(
            x=pltpu.VMEM((tiles, seq_rows, LANES), F32),
            states=pltpu.VMEM((seq_rows // CHUNKS, comps, CHUNKS, LANES), F32),
        ),
        after=[third_rows, first_sum, second_sum],
        hides=HIDE_LAST,
    )
    first_rows = shard_sum(first_sum, last)
    second_rows = keep_rows(second_sum, row_bits[0], last)
    def summed(total):
        for bit in row_bits[1:-1]:
            total = keep_rows(total, bit)
        return plus(total, swap(total, "seq", row_bits[-1]))

    first_rows, second_rows = summed(first_rows), summed(second_rows)
    first_rows, *rest_sent = lax.optimization_barrier((first_rows, *two.r))
    rest_blocks = exchange(rest_sent, "wa")
    third_total = all_rows(third_rows, row_bits[:-1], last)
    second_rows, first_rows = all_rows(second_rows, row_bits[1:-1]), all_rows(first_rows, row_bits[1:-1])
    joined = run(
        functools.partial(ema_join, groups, peers),
        [(meta, SMEM), (last.part, VMEM), (rest_blocks, hbm)],
        Box(grad=((seqs, seq_rows, width), F32, VMEM), block=((seqs, seq_rows, width), BF, VMEM)),
        Box(rest=pltpu.VMEM((tok_rows, 2 * width), BF), sem=sems((peers,))),
        after=[second_rows, first_rows],
        hides=HIDE_JOIN,
    )

    second_total = all_rows(second_rows, row_bits[:1], joined)
    first_total = all_rows(first_rows, row_bits[:1], joined)
    small = [ffn.sums, one.sums, two.sums, two.rel] + [a.reshape(-1, LANES) for a in (ffn.up_bias, one.bias, two.bias)]
    places = [0]
    for part in small:
        places.append(places[-1] + part.shape[0])
    small += [mark.token] + [mark.token for mark in nears] + [two.token, back.token, ema.token, ends.token, last.token, fwd.token]
    small.append(jnp.zeros((-sum(part.shape[0] for part in small) % 16, LANES), F32))
    small, zeta_grad = sum_small(jnp.concatenate(small, axis=0), two.zeta, [("wa", bit) for bit in bits_of(peers)])
    count = small.shape[0]
    small = jnp.concatenate([small, last.sums.reshape(-1, LANES)])
    small, zeta_grad = sum_small(small, zeta_grad, [("seq", bit) for bit in row_bits])
    ema_sums = small[count:].reshape(last.sums.shape)
    ema_sums = jnp.concatenate(list(ema_sums), axis=1)[:, :width]
    decay_grad = ema_sums[:comps].T * (ema_feed * ema_read)
    moment = ema_sums[comps : 2 * comps].T
    feed_grad, read_grad = moment * ema_read, moment * ema_feed
    skip_grad = ema_sums[2 * comps]
    parts = [small[a:b] for a, b in zip(places, places[1:])]
    tall = wide // LANES
    lines = [parts[0][i * tall : (i + 1) * tall].reshape(wide) for i in range(5)]
    lines += [parts[1][i * tall : (i + 1) * tall].reshape(wide) for i in range(2)]
    loss = parts[0][5 * tall, 0] + joined.token[0, 0]
    zsums, rel_grad = parts[2], parts[3][:2].reshape(2 * GROUP)[: rel_bias.shape[0]]
    up_bias_grad, reset_bias_grad, value_bias_grad = (
        lax.dynamic_slice_in_dim(part, me * 8, 8, 0).reshape(8 * LANES)[:units] for part in parts[4:]
    )

    up_grad = jnp.concatenate([third_total[:depth, j * hidden : (j + 1) * hidden] for j in range(fold)], axis=0)
    return (
        joined.block, joined.grad, loss, decay_grad, feed_grad, read_grad, skip_grad, zeta_grad, zsums[0], zsums[1], zsums[2],
        zsums[3], rel_grad, first_total[:, :units].astype(F32), reset_bias_grad, first_total[:, units:].astype(F32), value_bias_grad,
        second_total[:width].astype(F32), lines[6], second_total[width : 2 * width].astype(F32), second_total[2 * width :].astype(F32), lines[5], lines[3],
        lines[4], up_grad.astype(F32), up_bias_grad, third_total[depth:].astype(F32), lines[2], lines[0], lines[1],
    )


def solution(mesh):
    return jax.shard_map(
        per_device,
        mesh=mesh,
        in_specs=(
            P(None, "seq", "wa"), P(None, "seq", None), P(), P(None, "seq"), P("wa", None), P("wa", None), P("wa", None), P("wa"),
            P(), P(), P(), P(), P(), P(), P(None, "wa"), P("wa"), P(None, "wa"), P("wa"), P("wa", None), P(), P("wa", None),
            P("wa", None), P(), P(), P(), P(None, "wa"), P("wa"), P("wa", None), P(), P(), P(),
        ),
        out_specs=(
            P(None, "seq", "wa"), P(None, "seq", "wa"), P(), P("wa", None), P("wa", None), P("wa", None), P("wa"), P(), P(), P(),
            P(), P(), P(), P(None, "wa"), P("wa"), P(None, "wa"), P("wa"), P("wa", None), P(), P("wa", None), P("wa", None), P(),
            P(), P(), P(None, "wa"), P("wa"), P("wa", None), P(), P(), P(),
        ),
        check_vma=False,
    )
```

```python
import functools

import jax
import jax.numpy as jnp
from jax import lax
from jax.experimental import pallas as pl
from jax.experimental.pallas import tpu as pltpu
from jax.sharding import PartitionSpec as P

Z = 128
GROUP = 128
LANES = 128
CHUNKS = 8
BIAS_ROWS = 32
HIDE_ENDS, HIDE_VALUES, HIDE_ATTEND, HIDE_ONE, HIDE_TWO, HIDE_BACK, HIDE_LAST, HIDE_JOIN = 20, 20, 20, 20, 40, 60, 15, 30
SHARE_BITS = 1
EPSILON = 1e-05
BF = jnp.bfloat16
F32 = jnp.float32
VMEM = pltpu.MemorySpace.VMEM
SMEM = pltpu.MemorySpace.SMEM


def dot(a, b):
    return jnp.dot(a, b, preferred_element_type=F32)


def dot_nt(a, b):
    return lax.dot_general(a, b, (((1,), (1,)), ((), ())), preferred_element_type=F32)


def dot_tn(a, b):
    return lax.dot_general(a, b, (((0,), (0,)), ((), ())), preferred_element_type=F32)


def sigmoid(v):
    return 1.0 / (1.0 + jnp.exp(-v))


def slope(v):
    s = sigmoid(v)
    return s * (1.0 + v * (1.0 - s))


def row(ref):
    return ref[...].reshape(1, ref.shape[0])


def put_line(ref, at, line):
    for j in range(0, line.shape[1], LANES):
        piece = line[:, j : j + LANES]
        ref[at + j // LANES : at + j // LANES + 1, : piece.shape[1]] = piece


def colsum(v):
    return jnp.sum(v, axis=0, keepdims=True)


def normalise(v):
    center = v - jnp.mean(v, axis=-1, keepdims=True)
    inv = lax.rsqrt(jnp.mean(center * center, axis=-1, keepdims=True) + EPSILON)
    return center * inv, inv


def norm_back(grad, normed, inv, gain):
    scaled = grad * gain
    one = jnp.mean(scaled, axis=-1, keepdims=True)
    two = jnp.mean(scaled * normed, axis=-1, keepdims=True)
    return inv * (scaled - one - normed * two)


class Box:
    def __init__(self, **parts):
        self.__dict__.update(parts)


jax.tree_util.register_pytree_node(
    Box, lambda box: (tuple(vars(box).values()), tuple(vars(box))), lambda names, parts: Box(**dict(zip(names, parts)))
)


def whole(space=VMEM):
    return pl.BlockSpec(memory_space=space)


def run(kernel, ins, outs, scratch, after=(), vectors=None, limit=48, hides=0):
    body, count = kernel, len(ins)
    vectors = vectors or Box()
    outs.token = ((8, LANES), F32, VMEM)
    fetched = len(vars(vectors))
    ins = ins + [(vectors, pltpu.MemorySpace.HBM), (list(after), pl.ANY)]
    scratch = Box(
        body=scratch, vec=jax.tree.map(lambda a: pltpu.VMEM(a.shape, a.dtype), vectors),
        sem=pltpu.SemaphoreType.DMA((max(fetched, 1),)),
    )

    def kernel(*refs):
        hbm, out, s = refs[count], refs[count + 2], refs[count + 3]
        copies = [
            pltpu.make_async_copy(vars(hbm)[name], vars(s.vec)[name], s.sem.at[i]) for i, name in enumerate(vars(hbm))
        ]
        for copy in copies:
            copy.start()
        if fetched:
            s.body.vec = s.vec
            s.body.wait = lambda: [copy.wait() for copy in copies]
        out.token[...] = jnp.zeros_like(out.token)
        body(*refs[:count], out, s.body)

    specs = [jax.tree.map(lambda _, space=space: whole(space), tree) for tree, space in ins]
    trees = [tree for tree, _ in ins]
    leaf = lambda entry: isinstance(entry, tuple)
    shapes = jax.tree.map(lambda e: jax.ShapeDtypeStruct(e[0], e[1]), outs, is_leaf=leaf)
    out_specs = jax.tree.map(lambda e: whole(e[2]), outs, is_leaf=leaf)
    return pl.pallas_call(
        kernel,
        out_shape=(shapes,),
        in_specs=specs,
        out_specs=(out_specs,),
        scratch_shapes=[scratch],
        compiler_params=pltpu.CompilerParams(vmem_limit_bytes=limit * 2**20),
        cost_estimate=pl.CostEstimate(flops=1 + int(hides * 1.15e9), bytes_accessed=1, transcendentals=0),
    )(*trees)[0]


def beside(hides, *deps):
    def kernel(ins, out, s):
        pass

    return run(kernel, [(list(deps), pl.ANY)], Box(), Box(), hides=hides)


def pack(pieces, meta, regions, out):
    height = out.own.shape[0]
    for ref, at, rows, top, left in regions:
        out.packed[top : top + rows, left : left + ref.shape[1]] = ref[at : at + rows, :]

    def piece(j):
        for ref, at, rows, top, left in regions:
            low, high = max(top, j * height), min(top + rows, (j + 1) * height)
            if low < high:
                out.own[low - j * height : high - j * height, left : left + ref.shape[1]] = ref[at + low - top : at + high - top, :]

    for j in range(pieces):
        pl.when(meta[1] == j)(lambda j=j: piece(j))


def pack_first(pieces, meta, reset, value, rel, out, s):
    units = reset.shape[1]
    s.wait()
    s.rows[...] = jnp.zeros_like(s.rows)
    for left, ref in ((0, s.vec.reset), (units, s.vec.value)):
        rest = row(ref)
        for i in range(3):
            high = rest.astype(BF).astype(F32)
            s.rows[i : i + 1, left : left + units] = high
            rest = rest - high
    s.rows[3:4, :units] = row(s.vec.up).astype(F32)
    s.bias[...] = s.rows[...].astype(BF)
    out.rel[...] = jnp.zeros_like(out.rel)
    out.rel[0:1, : rel.shape[0]] = row(rel)
    wide = reset.shape[0]
    pack(pieces, meta, [(reset, 0, wide, 0, 0), (value, 0, wide, 0, units), (s.bias, 0, BIAS_ROWS, wide, 0)], out)


def pack_second(pieces, meta, update, mixer, output, out, s):
    width, units = update.shape[0], output.shape[0]
    pack(pieces, meta, [(update, 0, width, 0, 0), (mixer, 0, width, width, 0), (output, 0, units, 2 * width, 0)], out)


def pack_third(pieces, meta, up, down, out, s):
    hidden = up.shape[1]
    depth = up.shape[0] // (down.shape[1] // hidden)
    regions = [(up, at, depth, 0, at // depth * hidden) for at in range(0, up.shape[0], depth)]
    pack(pieces, meta, regions + [(down, 0, hidden, depth, 0)], out)


def lane_groups(seqs, width):
    groups = []
    rest = width % LANES
    for s in range(seqs):
        for c in range(0, width - rest, LANES):
            groups.append([(s, c, LANES, 0)])
    tile, lane = [], 0
    for s in range(seqs if rest else 0):
        if lane + rest > LANES:
            groups.append(tile)
            tile, lane = [], 0
        tile.append((s, width - rest, rest, lane))
        lane += rest
    if tile:
        groups.append(tile)
    return groups


def join(parts):
    rows = parts[0].shape[0]
    used = sum(p.shape[1] for p in parts)
    if used < LANES:
        parts = parts + [jnp.zeros((rows, LANES - used), parts[0].dtype)]
    return parts[0] if len(parts) == 1 else jnp.concatenate(parts, axis=1)


def rows_of(group, ref):
    return join([ref[:, c : c + w] for _, c, w, _ in group])


def tokens_of(group, get):
    return join([get(s, c, w) for s, c, w, _ in group])


def spread(row):
    return jnp.broadcast_to(row, (CHUNKS, LANES))


def power(v, count):
    while count > 1:
        v = v * v
        count //= 2
    return v


def shifted(v, by):
    at = lax.broadcasted_iota(jnp.int32, v.shape, 0)
    moved = pltpu.roll(v, by % CHUNKS, 0)
    keep = at >= by if by > 0 else at < CHUNKS + by
    return jnp.where(keep, moved, 0.0)


def chunk_scan(ends, chunk_decay, sign):
    run_sum, factor, step = ends, chunk_decay, 1
    while step < CHUNKS:
        run_sum = run_sum + factor * shifted(run_sum, sign * step)
        factor, step = factor * factor, step * 2
    return run_sum, shifted(run_sum, sign)


def rank_power(chunk_decay, reverse):
    at = lax.broadcasted_iota(jnp.int32, chunk_decay.shape, 0)
    at = CHUNKS - 1 - at if reverse else at
    result, factor, bit = jnp.ones_like(chunk_decay), chunk_decay, 1
    while bit < CHUNKS:
        result = jnp.where((at & bit) != 0, result * factor, result)
        factor, bit = factor * factor, bit * 2
    return result


def steps_of(length, body, carry, reverse=False, unroll=4):
    def block(i, state):
        for u in range(unroll):
            t = i * unroll + u
            state = body(length - 1 - t if reverse else t, state)
        return state

    return lax.fori_loop(0, length // unroll, block, carry)


def at_step(ref, g, t, length):
    return ref.at[g, pl.ds(t, CHUNKS, stride=length), :]


def ema_ends(groups, comps, blocks, meta, x_ref, decay_ref, out, s):
    rows = x_ref.shape[1]
    part = x_ref.shape[0] * rows // blocks
    copies = []
    for k in range(blocks):
        at = (meta[0] ^ k) * part
        source = x_ref.at[at // rows, pl.ds(pl.multiple_of(at % rows, part), part), :]
        copies.append(pltpu.make_async_copy(source, out.r[k], s.sem.at[k]))
    for copy in copies:
        copy.start()
    length = x_ref.shape[1] // CHUNKS
    for g, group in enumerate(groups):
        s.x[g] = tokens_of(group, lambda q, c, w: x_ref[q, :, c : c + w].astype(F32))
        decay = rows_of(group, decay_ref)
        decays = [spread(decay[n : n + 1]) for n in range(comps)]

        def body(t, state):
            now = at_step(s.x, g, t, length)[...]
            return tuple(decays[n] * state[n] + now for n in range(comps))

        ends = steps_of(length, body, (jnp.zeros((CHUNKS, LANES), F32),) * comps)
        for n in range(comps):
            total, before = chunk_scan(ends[n], power(decays[n], length), 1)
            out.before[g, n] = before
            out.fade[g, n : n + 1, :] = power(decay[n : n + 1], length * CHUNKS)
            out.end[g, n : n + 1, :] = total[CHUNKS - 1 :]
    for copy in copies:
        copy.wait()


def carried(parts, device_decay, rank, reverse):
    total, passed = jnp.zeros_like(device_decay), jnp.ones_like(device_decay)
    for i, part in enumerate(parts):
        counts = ((rank // (1 << i)) % 2) == (0 if reverse else 1)
        total = jnp.where(counts, total + passed * part, total)
        passed = jnp.where(counts, passed * device_decay, passed)
        device_decay = device_decay * device_decay
    return total


def ema_values(groups, comps, blocks, meta, x_ref, decay_ref, mix_ref, skip_ref, before_ref, got, out, s):
    length = x_ref.shape[1] // CHUNKS
    width = x_ref.shape[2]
    seqs, rows = x_ref.shape[0], x_ref.shape[1]
    for g, group in enumerate(groups):
        s.x[g] = tokens_of(group, lambda q, c, w: x_ref[q, :, c : c + w].astype(F32))
        decay, mix, skip = rows_of(group, decay_ref), rows_of(group, mix_ref), rows_of(group, skip_ref)
        decays = [spread(decay[n : n + 1]) for n in range(comps)]
        mixes = [spread(mix[n : n + 1]) for n in range(comps)]
        skip = spread(skip)
        state_in = carried([part[g] for part in got], power(decay, length * CHUNKS), meta[2], False)
        start = []
        for n in range(comps):
            ranks = rank_power(power(decays[n], length), False)
            start.append(before_ref[g, n] + ranks * spread(state_in[n : n + 1]))
            out.start[g, n] = start[n]

        def body(t, state):
            now = at_step(s.x, g, t, length)[...]
            state = tuple(decays[n] * state[n] + now for n in range(comps))
            terms = [mixes[n] * state[n] for n in range(comps)] + [skip * now]
            while len(terms) > 1:
                terms = [a + b for a, b in zip(terms[::2], terms[1::2])] + (terms[-1:] if len(terms) % 2 else [])
            at_step(s.y, g, t, length)[...] = terms[0]
            return state

        steps_of(length, body, tuple(start))
        for q, c, w, lane in group:
            value = s.y[g, :, lane : lane + w]
            out.value[q, :, c : c + w] = value
            s.mixed[pl.ds(q * rows, rows), c : c + w] = (value * sigmoid(value)).astype(BF)
    part = seqs * rows // blocks
    copies = [
        pltpu.make_async_copy(
            s.mixed.at[pl.ds(pl.multiple_of((meta[0] ^ k) * part, part), part), :], out.m[k], s.sem.at[k]
        )
        for k in range(blocks)
    ]
    for copy in copies:
        copy.start()
    for copy in copies:
        copy.wait()


def ema_back_ends(groups, comps, blocks, meta, grads, value_ref, decay_ref, out, s):
    length = value_ref.shape[1] // CHUNKS
    rows = value_ref.shape[1]
    part = value_ref.shape[0] * rows // blocks
    copies = [
        pltpu.make_async_copy(
            grads[k], s.grad.at[pl.ds(pl.multiple_of((meta[0] ^ k) * part, part), part), :], s.sem.at[k]
        )
        for k in range(blocks)
    ]
    for copy in copies:
        copy.start()
    for copy in copies:
        copy.wait()
    for g, group in enumerate(groups):

        def load(q, c, w):
            return s.grad[pl.ds(q * rows, rows), c : c + w].astype(F32) * slope(value_ref[q, :, c : c + w])

        out.grad[g] = tokens_of(group, load)
        decay = rows_of(group, decay_ref)
        decays = [spread(decay[n : n + 1]) for n in range(comps)]

        def body(t, state):
            now = at_step(out.grad, g, t, length)[...]
            return tuple(decays[n] * state[n] + now for n in range(comps))

        ends = steps_of(length, body, (jnp.zeros((CHUNKS, LANES), F32),) * comps, reverse=True)
        for n in range(comps):
            total, after = chunk_scan(ends[n], power(decays[n], length), -1)
            out.after[g, n] = after
            out.first[g, n : n + 1, :] = total[:1]


def ema_join(groups, blocks, meta, part_ref, rests, out, s):
    seqs, rows, width = out.grad.shape
    part = seqs * rows // blocks
    copies = [
        pltpu.make_async_copy(
            rests[k], s.rest.at[pl.ds(pl.multiple_of((meta[0] ^ k) * part, part), part), :], s.sem.at[k]
        )
        for k in range(blocks)
    ]
    for copy in copies:
        copy.start()
    for copy in copies:
        copy.wait()
    for q in range(seqs):
        out.block[q] = s.rest[pl.ds(q * rows, rows), width:]
    for g, group in enumerate(groups):
        for q, c, w, lane in group:
            rest = s.rest[pl.ds(q * rows, rows), c : c + w].astype(F32)
            out.grad[q, :, c : c + w] = part_ref[g, :, lane : lane + w] + rest


def ema_back(groups, comps, meta, x_ref, grad_ref, decay_ref, mix_ref, skip_ref, start_ref, after_ref, got, out, s):
    length = x_ref.shape[1] // CHUNKS
    out.sums[...] = jnp.zeros_like(out.sums)
    half = comps // 2
    for g, group in enumerate(groups):
        s.x[g] = tokens_of(group, lambda q, c, w: x_ref[q, :, c : c + w].astype(F32))
        decay, mix, skip = rows_of(group, decay_ref), rows_of(group, mix_ref), rows_of(group, skip_ref)
        decays = [spread(decay[n : n + 1]) for n in range(comps)]
        mixes = [spread(mix[n : n + 1]) for n in range(comps)]
        skip = spread(skip)

        def forward(t, state):
            now = at_step(s.x, g, t, length)[...]
            for n in range(comps):
                s.states[t, n] = state[n]
            return tuple(decays[n] * state[n] + now for n in range(comps))

        steps_of(length, forward, tuple(start_ref[g, n] for n in range(comps)))
        grad_in = carried([p[g] for p in got], power(decay, length * CHUNKS), meta[2], True)
        for h in range(2):
            mine = range(h * half, (h + 1) * half)
            begin = []
            for n in mine:
                ranks = rank_power(power(decays[n], length), True)
                begin.append(after_ref[g, n] + ranks * spread(grad_in[n : n + 1]))
            zero = (jnp.zeros((CHUNKS, LANES), F32),) * half

            def backward(t, carry):
                grads, moments, changes, skips = carry
                now, up = at_step(s.x, g, t, length)[...], at_step(grad_ref, g, t, length)[...]
                grads = tuple(decays[n] * grads[i] + up for i, n in enumerate(mine))
                moments = tuple(moments[i] + grads[i] * now for i in range(half))
                changes = tuple(changes[i] + grads[i] * s.states[t, n] for i, n in enumerate(mine))
                terms = [mixes[n] * grads[i] for i, n in enumerate(mine)]
                if h == 0:
                    terms.append(skip * up)
                    skips = skips + up * now
                else:
                    terms.append(at_step(out.part, g, t, length)[...])
                while len(terms) > 1:
                    terms = [a + b for a, b in zip(terms[::2], terms[1::2])] + (terms[-1:] if len(terms) % 2 else [])
                at_step(out.part, g, t, length)[...] = terms[0]
                return grads, moments, changes, skips

            _, moments, changes, skips = steps_of(length, backward, (tuple(begin), zero, zero, zero[0]), reverse=True, unroll=2)
            for q, c, w, lane in group:
                for i, n in enumerate(mine):
                    out.sums[c // LANES, n : n + 1, :w] += colsum(changes[i])[:, lane : lane + w]
                    out.sums[c // LANES, comps + n : comps + n + 1, :w] += colsum(moments[i])[:, lane : lane + w]
                if h == 0:
                    out.sums[c // LANES, 2 * comps : 2 * comps + 1, :w] += colsum(skips)[:, lane : lane + w]


def weight_copies(meta, shards, dst, sem, first):
    copies = []
    for k, pieces in enumerate(shards):
        height = dst.shape[1] // len(pieces)
        for j, piece in enumerate(pieces):
            target = dst.at[k]
            if len(pieces) > 1:
                target = dst.at[k, pl.ds(pl.multiple_of((meta[1] ^ j) * height, height), height), :]
            copies.append(pltpu.make_async_copy(piece, target, sem.at[first + len(copies)]))
    return copies


def block_copies(meta, blocks, dst, sem, first):
    return [
        pltpu.make_async_copy(block, dst.at[meta[0] ^ k], sem.at[first + k]) for k, block in enumerate(blocks)
    ]


def positions_of(ref, start, g):
    at = start + g * GROUP
    length = ref.shape[1]
    columns = pl.ds(pl.multiple_of(at % length, GROUP), GROUP)
    place = ref[0:1, columns]
    for q in range(1, ref.shape[0]):
        place = jnp.where(at // length == q, ref[q : q + 1, columns], place)
    return place


def attend_forward(peers, meta, mixed, raw, first, second, out, s):
    vec = s.vec
    blocks = block_copies(meta, mixed, s.mixed, s.sem, 0)
    blocks += block_copies(meta, raw, s.raw, s.sem, peers)
    ones = weight_copies(meta, first, s.one, s.sem, 2 * peers)
    twos = weight_copies(meta, second, s.two, s.sem, 2 * peers + len(ones))
    for copy in blocks + ones + twos:
        copy.start()
    for copy in blocks:
        copy.wait()
    width = s.mixed.shape[2]
    units = s.one.shape[2] // 2
    rows, wide = out.mixed.shape
    groups = rows // GROUP
    for b in range(peers):
        out.mixed[:, b * width : (b + 1) * width] = s.mixed[b]
        out.raw[:, b * width : (b + 1) * width] = s.raw[b]
    s.wait()
    zeta_pre = dot(out.mixed[...], vec.zeta[...]) + row(vec.zeta_bias)
    out.zeta_pre[...] = zeta_pre
    act = zeta_pre * sigmoid(zeta_pre)
    queries = (act * row(vec.query_gain) + row(vec.query_shift)).astype(BF)
    keys = (act * row(vec.key_gain)).astype(BF)
    out.queries[...] = queries
    out.keys[...] = keys
    causal = lax.broadcasted_iota(jnp.int32, (GROUP, GROUP), 0) >= lax.broadcasted_iota(jnp.int32, (GROUP, GROUP), 1)
    for g in range(groups):
        at = slice(g * GROUP, (g + 1) * GROUP)
        place = jnp.broadcast_to(positions_of(vec.positions, meta[0] * rows, g).astype(F32), (GROUP, GROUP))
        distance = jnp.clip((place.T - place).astype(jnp.int32), 0, 2 * GROUP - 2)
        low = jnp.take_along_axis(
            jnp.broadcast_to(vec.rel[0:1, :GROUP], (GROUP, GROUP)), distance & (GROUP - 1), axis=1
        )
        high = jnp.take_along_axis(
            jnp.broadcast_to(vec.rel[0:1, GROUP:], (GROUP, GROUP)), distance & (GROUP - 1), axis=1
        )
        scores = dot_nt(queries[at], keys[at]) * Z**-0.5 + jnp.where(distance < GROUP, low, high)
        scores = jnp.where(causal, scores, -jnp.inf)
        shifted_exp = jnp.exp(scores - jnp.max(scores, axis=-1, keepdims=True))
        out.probs[at, :] = shifted_exp / jnp.sum(shifted_exp, axis=-1, keepdims=True)
    for copy in ones:
        copy.wait()
    for copy in twos:
        copy.wait()
    s.pre[...] = jnp.zeros_like(s.pre)
    s.gate[...] = jnp.zeros_like(s.gate)

    def shard(k, carry):
        biases = s.one[k, wide : wide + 16, :].astype(F32)
        bias = biases[0:1] + biases[1:2] + biases[2:3]
        out.up_bias[k] = jnp.broadcast_to(biases[3:4, :units], (8, units))
        reset_pre = dot(out.mixed[...], s.one[k, :wide, :units]) + bias[:, :units]
        value_pre = dot(out.raw[...], s.one[k, :wide, units:]) + bias[:, units:]
        values = (value_pre * sigmoid(value_pre)).astype(BF)
        out.reset_pre[k] = reset_pre
        out.value_pre[k] = value_pre
        out.values[k] = values
        for g in range(groups):
            at = slice(g * GROUP, (g + 1) * GROUP)
            out.attended[k, at, :] = dot(out.probs[at, :].astype(BF), values[at])
        gated = (reset_pre * sigmoid(reset_pre) * out.attended[k]).astype(BF)
        out.gated[k] = gated
        block = s.mixed[meta[0] ^ k]
        s.gate[...] += dot(block, s.two[k, :width, :])
        s.pre[...] += dot(block, s.two[k, width : 2 * width, :]) + dot(gated, s.two[k, 2 * width :, :])
        return carry

    lax.fori_loop(0, peers, shard, 0)
    out_pre = s.pre[...] + row(vec.output_bias)
    out.out_pre[...] = out_pre
    gate = sigmoid(s.gate[...] + row(vec.update_bias))
    out.gate[...] = gate
    mid = gate * (out_pre * sigmoid(out_pre)) + (1.0 - gate) * out.raw[...].astype(F32)
    normed, inv = normalise(mid)
    out.normed[...] = normed
    out.inv[...] = inv


def feed_forward(peers, ranks, meta, lengths, third, normed_ref, inv_ref, targets, out, s):
    vec = s.vec
    rows = normed_ref.shape[0]
    seqs, seq_rows = targets.shape[0], targets.shape[1]
    seq, offset = meta[0] * rows // seq_rows, pl.multiple_of(meta[0] * rows % seq_rows, rows)
    fetch = pltpu.make_async_copy(targets.at[seq, pl.ds(offset, rows), :], s.targets, s.target_sem)
    fetch.start()
    threes = weight_copies(meta, third, s.three, s.sem, 0)
    for copy in threes:
        copy.start()
    rows, width = normed_ref.shape
    s.wait()
    units = vec.up_bias.shape[2]
    fold = width // units
    depth = width // fold
    first = normed_ref[...] * row(vec.first_gain) + row(vec.first_shift)
    s.first[...] = first.astype(BF)
    s.total[...] = first + row(vec.down_bias)
    for copy in threes:
        copy.wait()

    def forward(k, carry):
        pre = vec.up_bias[k, 0:1, :]
        for j in range(fold):
            pre = pre + dot(
                s.first[:, j * depth : (j + 1) * depth], s.three[k, :depth, j * units : (j + 1) * units]
            )
        s.up_pre[k] = pre
        act = (pre * sigmoid(pre)).astype(BF)
        s.act[k] = act
        s.total[...] += dot(act, s.three[k, depth:, :])
        return carry

    lax.fori_loop(0, peers, forward, 0)
    normed, inv = normalise(s.total[...])
    second = normed * row(vec.second_gain) + row(vec.second_shift)
    piece = width // peers
    for b in range(peers):
        out.second[b] = second[:, b * piece : (b + 1) * piece].astype(BF)
    fetch.wait()
    misfit = second - s.targets[...].astype(F32)
    place = lax.broadcasted_iota(jnp.int32, (rows, 1), 0) + (meta[2] * seq_rows + offset)
    weight = (place < lengths[seq]).astype(F32)
    tokens = lengths[0]
    for q in range(1, seqs):
        tokens = tokens + lengths[q]
    true_count = jnp.broadcast_to(tokens, (rows, 1)).astype(F32)
    losses = jnp.sum(misfit * misfit, axis=1, keepdims=True) * (weight / (2.0 * width * true_count))
    out.sums[...] = jnp.zeros_like(out.sums)
    out.up_bias[...] = jnp.zeros_like(out.up_bias)
    lines = width // LANES
    put_line(out.sums, 5 * lines, jnp.broadcast_to(jnp.sum(losses, axis=0, keepdims=True), (1, LANES)))
    grad_out = misfit * (weight * (seqs * seq_rows * ranks / true_count))
    put_line(out.sums, 0, colsum(grad_out * normed))
    put_line(out.sums, lines, colsum(grad_out))
    second_grad = norm_back(grad_out, normed, inv, row(vec.second_gain))
    ffn_grad = second_grad.astype(BF)
    s.grad[...] = ffn_grad
    put_line(out.sums, 2 * lines, colsum(ffn_grad.astype(F32)))
    s.total[...] = second_grad

    def backward(k, carry):
        keep = k // 2
        down = dot_tn(s.act[k], s.grad[...]).astype(BF)
        up_grad = (dot_nt(s.grad[...], s.three[k, depth:, :]) * slope(s.up_pre[k])).astype(BF)
        put_line(out.up_bias.at[meta[0] ^ k], 0, colsum(up_grad.astype(F32)))
        s.upg[...] = up_grad
        ups = [dot_tn(s.first[:, j * depth : (j + 1) * depth], s.upg[...]).astype(BF) for j in range(fold)]

        def store(which):
            out.grads[which][keep, depth:, :] = down
            for j in range(fold):
                out.grads[which][keep, :depth, j * units : (j + 1) * units] = ups[j]

        pl.when(k % 2 == 0)(lambda: store(0))
        pl.when(k % 2 == 1)(lambda: store(1))
        for j in range(fold):
            s.total[:, j * depth : (j + 1) * depth] += dot_nt(
                s.upg[...], s.three[k, :depth, j * units : (j + 1) * units]
            )
        return carry

    lax.fori_loop(0, peers, backward, 0)
    first_grad = s.total[...]
    put_line(out.sums, 3 * lines, colsum(first_grad * normed_ref[...]))
    put_line(out.sums, 4 * lines, colsum(first_grad))
    out.mid_grad[...] = norm_back(first_grad, normed_ref[...], inv_ref[...], row(vec.first_gain))


def attend_back_one(peers, meta, second, mixed_ref, raw_ref, mid_ref, pre_ref, gate_ref, reset_ref, attended_ref, gated_ref, out, s):
    twos = weight_copies(meta, second, s.two, s.sem, 0)
    for copy in twos:
        copy.start()
    rows, wide = mixed_ref.shape
    width = wide // peers
    for b in range(peers):
        s.mixed[b] = mixed_ref[:, b * width : (b + 1) * width]
    mid, gate, pre = mid_ref[...], gate_ref[...], pre_ref[...]
    pre_grad = (mid * gate * slope(pre)).astype(BF)
    s.pre_grad[...] = pre_grad
    gate_grad = (mid * (pre * sigmoid(pre) - raw_ref[...].astype(F32)) * gate * (1.0 - gate)).astype(BF)
    s.gate_grad[...] = gate_grad
    out.direct[...] = mid * (1.0 - gate)
    out.sums[...] = jnp.zeros_like(out.sums)
    out.bias[...] = jnp.zeros_like(out.bias)
    put_line(out.sums, 0, colsum(pre_grad.astype(F32)))
    put_line(out.sums, wide // LANES, colsum(gate_grad.astype(F32)))
    for copy in twos:
        copy.wait()

    def shard(k, carry):
        keep = k // 2
        s.block[...] = s.mixed[meta[0] ^ k]
        update = dot_tn(s.block[...], s.gate_grad[...]).astype(BF)
        mixer = dot_tn(s.block[...], s.pre_grad[...]).astype(BF)
        output = dot_tn(gated_ref[k], s.pre_grad[...]).astype(BF)

        def store(which):
            out.grads[which][keep, :width, :] = update
            out.grads[which][keep, width : 2 * width, :] = mixer
            out.grads[which][keep, 2 * width :, :] = output

        pl.when(k % 2 == 0)(lambda: store(0))
        pl.when(k % 2 == 1)(lambda: store(1))
        out.mixed_grad[k] = dot_nt(s.gate_grad[...], s.two[k, :width, :]) + dot_nt(
            s.pre_grad[...], s.two[k, width : 2 * width, :]
        )
        gated_grad = dot_nt(s.pre_grad[...], s.two[k, 2 * width :, :])
        reset = reset_ref[k]
        out.attend_grad[k] = (gated_grad * (reset * sigmoid(reset))).astype(BF)
        reset_grad = (gated_grad * attended_ref[k] * slope(reset)).astype(BF)
        out.reset_grad[k] = reset_grad
        put_line(out.bias.at[meta[0] ^ k], 0, colsum(reset_grad.astype(F32)))
        return carry

    lax.fori_loop(0, peers, shard, 0)


def attend_back_two(
    peers, meta, first, mixed_ref, raw_ref, value_pre_ref, values_ref, probs_ref, agrad_ref, rgrad_ref, direct_ref, local_ref,
    queries_ref, keys_ref, zeta_pre_ref, second_ref, out, s,
):
    vec = s.vec
    ones = weight_copies(meta, first, s.one, s.sem, 0)
    for copy in ones:
        copy.start()
    rows, wide = mixed_ref.shape
    width = wide // peers
    units = values_ref.shape[2]
    groups = rows // GROUP
    s.wait()
    act = zeta_pre_ref[...] * sigmoid(zeta_pre_ref[...])
    line = lax.broadcasted_iota(jnp.int32, (2 * GROUP, GROUP), 0)
    buckets = jnp.zeros((1, 2 * GROUP), F32)
    for g in range(groups):
        at = slice(g * GROUP, (g + 1) * GROUP)

        def score(k, total):
            return total + dot_nt(agrad_ref[k, at, :], values_ref[k, at, :])

        prob_grad = lax.fori_loop(0, peers, score, jnp.zeros((GROUP, GROUP), F32))
        probs = probs_ref[at, :]
        row_dot = jnp.sum(probs * prob_grad, axis=-1, keepdims=True)
        sgrad = (probs * (prob_grad - row_dot)).astype(BF)
        s.query_grad[at, :] = dot(sgrad, keys_ref[at, :]) * Z**-0.5
        s.key_grad[at, :] = dot_tn(sgrad, queries_ref[at, :]) * Z**-0.5
        ahead = positions_of(vec.positions, meta[0] * rows, g)
        ahead = ahead - ahead[:, 0:1]
        to_row = (line == ahead).astype(BF)
        to_column = (line == 2 * GROUP - 1 - ahead).astype(BF)
        table = dot(to_row, dot_nt(sgrad, to_column).astype(BF))
        buckets = buckets + colsum(pltpu.roll(table, 1, 1, stride=1, stride_axis=0))
    out.rel[...] = jnp.zeros_like(out.rel)
    out.bias[...] = jnp.zeros_like(out.bias)
    put_line(out.rel, 0, buckets)
    query_grad, key_grad = s.query_grad[...], s.key_grad[...]
    zeta_grad = (query_grad * row(vec.query_gain) + key_grad * row(vec.key_gain)) * slope(zeta_pre_ref[...])
    zeta_grad = zeta_grad.astype(BF)
    out.sums[...] = jnp.zeros_like(out.sums)
    out.sums[0:1, :] = colsum(zeta_grad.astype(F32))
    out.sums[1:2, :] = colsum(query_grad * act)
    out.sums[2:3, :] = colsum(query_grad)
    out.sums[3:4, :] = colsum(key_grad * act)
    out.zeta[...] = dot_tn(mixed_ref[...], zeta_grad)
    s.mixed[...] = dot_nt(zeta_grad, vec.zeta[...])
    s.raw[...] = direct_ref[...]
    for copy in ones:
        copy.wait()

    def shard(k, carry):
        keep = k // 2
        for g in range(groups):
            at = slice(g * GROUP, (g + 1) * GROUP)
            vals_grad = dot_tn(probs_ref[at, :].astype(BF), agrad_ref[k, at, :])
            s.vgrad[at, :] = (vals_grad * slope(value_pre_ref[k, at, :])).astype(BF)
        put_line(out.bias.at[meta[0] ^ k], 0, colsum(s.vgrad[...].astype(F32)))
        reset = dot_tn(mixed_ref[...], rgrad_ref[k]).astype(BF)
        value = dot_tn(raw_ref[...], s.vgrad[...]).astype(BF)

        def store(which):
            out.grads[which][keep, :, :units] = reset
            out.grads[which][keep, :, units:] = value

        pl.when(k % 2 == 0)(lambda: store(0))
        pl.when(k % 2 == 1)(lambda: store(1))
        s.mixed[...] += dot_nt(rgrad_ref[k], s.one[k, :wide, :units])
        s.raw[...] += dot_nt(s.vgrad[...], s.one[k, :wide, units:])
        return carry

    lax.fori_loop(0, peers, shard, 0)
    for b in range(peers):
        at = slice(b * width, (b + 1) * width)
        s.mixed_out[b] = (s.mixed[:, at] + local_ref[meta[0] ^ b]).astype(BF)
        s.raw_out[b, :, :width] = s.raw[:, at].astype(BF)
        s.raw_out[b, :, width:] = second_ref[b]
    sends = []
    for k in range(peers):
        sends.append(pltpu.make_async_copy(s.mixed_out.at[meta[0] ^ k], out.m[k], s.sem.at[2 * k]))
        sends.append(pltpu.make_async_copy(s.raw_out.at[meta[0] ^ k], out.r[k], s.sem.at[2 * k + 1]))
    for copy in sends:
        copy.start()
    for copy in sends:
        copy.wait()


def swap(x, axis, by):
    size = lax.axis_size(axis)
    return lax.ppermute(x, axis, [(i, i ^ by) for i in range(size)])


def later_than(x, *marks):
    for mark in marks:
        x, mark.token = lax.optimization_barrier((x, mark.token))
    return x


def exchange(blocks, axis):
    return [blocks[0]] + [swap(blocks[k], axis, k) for k in range(1, len(blocks))]


def group_totals(total, fade, axis, reverse, nears=None):
    result = []
    for bit in bits_of(lax.axis_size(axis)):
        other = swap(total, axis, bit)
        if nears is not None:
            nears.append(beside(0, other))
            other, nears[-1].token = lax.optimization_barrier((other, nears[-1].token))
        result.append(other)
        upper = ((lax.axis_index(axis) // bit) % 2) == (0 if reverse else 1)
        total = jnp.where(upper, total + fade * other, other + fade * total)
        fade = fade * fade
    return result


def far_pieces(pack):
    return [swap(pack.own, "wa", k) for k in range(2, lax.axis_size("wa"), 2)]


def next_pieces(came):
    return [swap(piece, "seq", j) for piece in came for j in range(1, 1 << SHARE_BITS)]


def all_shards(pack, came, beyond):
    others = (1 << SHARE_BITS) - 1
    shards = [[pack.packed]]
    shards += [[came[i]] + beyond[i * others : (i + 1) * others] for i in range(len(came))]
    return [pieces for even in shards for pieces in (even, [swap(piece, "wa", 1) for piece in even])]


def plus(a, b):
    return (a.astype(F32) + b.astype(F32)).astype(a.dtype)


def core_sums(grads, *deps):
    return plus(grads[0], later_than(swap(grads[1], "wa", 1), *deps))


def shard_sum(parts, *deps):
    step = 2
    while parts.shape[0] > 1:
        parts = plus(parts[::2], later_than(swap(parts[1::2], "wa", step), *deps))
        step *= 2
    return parts[0]


def keep_rows(total, bit, *deps):
    here = (lax.axis_index("seq") // bit) % 2
    height = total.shape[-2] // 2
    mine = lax.dynamic_slice_in_dim(total, here * height, height, total.ndim - 2)
    theirs = lax.dynamic_slice_in_dim(total, (1 - here) * height, height, total.ndim - 2)
    return plus(mine, later_than(swap(theirs, "seq", bit), *deps))


def all_rows(total, bits, *deps):
    for bit in bits[::-1]:
        here = (lax.axis_index("seq") // bit) % 2
        other = later_than(swap(total, "seq", bit), *(deps if bit == bits[-1] else ()))
        total = jnp.where(
            here == 0, jnp.concatenate([total, other], axis=0), jnp.concatenate([other, total], axis=0)
        )
    return total


def sum_small(exact, rough, route):
    for axis, bit in route:
        high = lax.reduce_precision(exact, 8, 7)
        sent = jnp.concatenate([high.astype(BF), (exact - high).astype(BF), rough.astype(BF)])
        total = sent.astype(F32) + swap(sent, axis, bit).astype(F32)
        rows = exact.shape[0]
        exact, rough = total[:rows] + total[rows : 2 * rows], total[2 * rows :]
    return exact, rough


def bits_of(size):
    return [1 << b for b in range(size.bit_length() - 1)]


def per_device(
    inputs, targets, lengths, positions, ema_decay, ema_feed, ema_read, ema_skip, zeta_proj, zeta_bias, query_gain, query_shift,
    key_gain, rel_bias, reset_proj, reset_bias, value_proj, value_bias, update_proj, update_bias, mixer_proj, output_proj,
    output_bias, first_gain, first_shift, up_proj, up_bias, down_proj, down_bias, second_gain, second_shift,
):
    seqs, seq_rows, width = inputs.shape
    wide = targets.shape[2]
    comps = ema_decay.shape[1]
    peers, ranks = lax.axis_size("wa"), lax.axis_size("seq")
    me, rank = lax.axis_index("wa"), lax.axis_index("seq")
    tok_rows = seqs * seq_rows
    rows = tok_rows // peers
    n_groups = rows // GROUP
    units, hidden = reset_proj.shape[1], up_proj.shape[1]
    fold = wide // hidden
    depth = wide // fold
    total_tokens = tok_rows * ranks
    groups = lane_groups(seqs, width)
    tiles = len(groups)
    pieces = 1 << SHARE_BITS
    place = rank % pieces
    meta = jnp.stack([me, place, rank]).astype(jnp.int32)
    hbm = pltpu.MemorySpace.HBM
    sems = pltpu.SemaphoreType.DMA

    def packed(kernel, shape, arrays, scratch=None, vectors=None, **outs):
        return run(
            functools.partial(kernel, pieces),
            [(meta, SMEM)] + [(a, VMEM) for a in arrays],
            Box(packed=(shape, BF, VMEM), own=((shape[0] // pieces,) + shape[1:], BF, VMEM), **outs),
            scratch or Box(),
            vectors=vectors,
            limit=62,
        )

    one_shape, two_shape, three_shape = (wide + BIAS_ROWS, 2 * units), (2 * width + units, wide), (depth + hidden, wide)
    pack_one = packed(
        pack_first, one_shape, [reset_proj, value_proj, rel_bias],
        Box(rows=pltpu.VMEM((BIAS_ROWS, 2 * units), F32), bias=pltpu.VMEM((BIAS_ROWS, 2 * units), BF)),
        Box(reset=reset_bias, value=value_bias, up=up_bias), rel=((8, 2 * GROUP), F32, VMEM),
    )

    decay_rows, mix_rows = ema_decay.T, (ema_feed * ema_read).T
    skip_row = ema_skip[None, :]
    ends = run(
        functools.partial(ema_ends, groups, comps, peers),
        [(meta, SMEM), (inputs, VMEM), (decay_rows, VMEM)],
        Box(r=[((rows, width), BF, hbm)] * peers, before=((tiles, comps, CHUNKS, LANES), F32, VMEM), end=((tiles, comps, LANES), F32, VMEM), fade=((tiles, comps, LANES), F32, VMEM)),
        Box(x=pltpu.VMEM((tiles, seq_rows, LANES), F32), sem=sems((peers,))),
        after=[pack_one.own],
        hides=HIDE_ENDS,
    )
    def gate(*arrays):
        ends.token, *arrays = lax.optimization_barrier((ends.token,) + arrays)
        return arrays

    pack_two = packed(pack_second, two_shape, gate(update_proj, mixer_proj, output_proj))
    pack_three = packed(pack_third, three_shape, gate(up_proj, down_proj))
    came_one = [later_than(x, ends) for x in far_pieces(pack_one)]
    pack_two.own, came_one[0] = lax.optimization_barrier((pack_two.own, came_one[0]))
    came_two = far_pieces(pack_two)
    next_one = next_pieces(came_one)
    raw_blocks = exchange(ends.r, "wa")
    earlier = group_totals(ends.end, ends.fade, "seq", False)
    earlier[-1], *raw_blocks = lax.optimization_barrier((earlier[-1], *raw_blocks))
    outs = Box(
        value=((seqs, seq_rows, width), F32, VMEM),
        start=((tiles, comps, CHUNKS, LANES), F32, VMEM),
    )
    outs.m = [((rows, width), BF, hbm)] * peers
    ema = run(
        functools.partial(ema_values, groups, comps, peers),
        [(meta, SMEM), (inputs, VMEM), (decay_rows, VMEM), (mix_rows, VMEM), (skip_row, VMEM), (ends.before, VMEM), (earlier, VMEM)],
        outs,
        Box(
            x=pltpu.VMEM((tiles, seq_rows, LANES), F32),
            y=pltpu.VMEM((tiles, seq_rows, LANES), F32),
            mixed=pltpu.VMEM((tok_rows, width), BF),
            sem=sems((peers,)),
        ),
        after=came_two + next_one,
        hides=HIDE_VALUES,
    )
    mixed_blocks = exchange(ema.m, "wa")
    next_two = [later_than(x, ema) for x in next_pieces(came_two)]
    pack_three.own, came_two[0] = lax.optimization_barrier((pack_three.own, came_two[0]))
    came_three = [later_than(x, ema) for x in far_pieces(pack_three)]
    held = (pack_two.packed, next_two[0], came_three[0], *mixed_blocks)
    pack_two.packed, next_two[0], came_three[0], *mixed_blocks = lax.optimization_barrier(held)
    shards_one = all_shards(pack_one, came_one, next_one)
    shards_one[1][0] = later_than(shards_one[1][0], ema)
    shards_two = all_shards(pack_two, came_two, next_two)

    count = len(jax.tree.leaves(shards_one))
    vec = Box(
        zeta=zeta_proj, zeta_bias=zeta_bias, query_gain=query_gain, query_shift=query_shift,
        key_gain=key_gain, rel=pack_one.rel, positions=positions,
        output_bias=output_bias, update_bias=update_bias,
    )
    fwd = run(
        functools.partial(attend_forward, peers),
        [(meta, SMEM), (mixed_blocks, hbm), (raw_blocks, hbm), (shards_one, hbm), (shards_two, hbm)],
        Box(
            mixed=((rows, wide), BF, VMEM), raw=((rows, wide), BF, VMEM), zeta_pre=((rows, Z), F32, VMEM),
            queries=((rows, Z), BF, VMEM), keys=((rows, Z), BF, VMEM), probs=((rows, GROUP), F32, VMEM),
            reset_pre=((peers, rows, units), F32, VMEM), value_pre=((peers, rows, units), F32, VMEM),
            values=((peers, rows, units), BF, VMEM), attended=((peers, rows, units), F32, VMEM),
            gated=((peers, rows, units), BF, VMEM), out_pre=((rows, wide), F32, VMEM), gate=((rows, wide), F32, VMEM),
            normed=((rows, wide), F32, VMEM), inv=((rows, 1), F32, VMEM), up_bias=((peers, 8, units), F32, VMEM),
        ),
        Box(
            mixed=pltpu.VMEM((peers, rows, width), BF), raw=pltpu.VMEM((peers, rows, width), BF),
            one=pltpu.VMEM((peers,) + one_shape, BF), two=pltpu.VMEM((peers,) + two_shape, BF),
            pre=pltpu.VMEM((rows, wide), F32), gate=pltpu.VMEM((rows, wide), F32),
            sem=sems((2 * peers + 2 * count,)),
        ),
        vectors=vec,
        limit=62,
        hides=HIDE_ATTEND,
    )
    next_three = [later_than(x, fwd) for x in next_pieces(came_three)]
    shards_three = all_shards(pack_three, came_three, next_three)

    vec = Box(
        first_gain=first_gain, first_shift=first_shift, down_bias=down_bias,
        second_gain=second_gain, second_shift=second_shift, up_bias=fwd.up_bias,
    )
    outs = Box(
        mid_grad=((rows, wide), F32, VMEM), second=((peers, rows, width), BF, VMEM), sums=((6 * wide // LANES // 8 * 8 + 8, LANES), F32, VMEM), up_bias=((peers, 8, LANES), F32, VMEM),
        grads=[((peers // 2,) + three_shape, BF, VMEM)] * 2,
    )
    ffn = run(
        functools.partial(feed_forward, peers, ranks),
        [(meta, SMEM), (lengths, SMEM), (shards_three, hbm), (fwd.normed, VMEM), (fwd.inv, VMEM), (targets, hbm)],
        outs,
        Box(
            three=pltpu.VMEM((peers,) + three_shape, BF), first=pltpu.VMEM((rows, wide), BF),
            total=pltpu.VMEM((rows, wide), F32), up_pre=pltpu.VMEM((peers, rows, hidden), F32),
            act=pltpu.VMEM((peers, rows, hidden), BF), grad=pltpu.VMEM((rows, wide), BF),
            upg=pltpu.VMEM((rows, hidden), BF), sem=sems((count,)), targets=pltpu.VMEM((rows, wide), BF), target_sem=sems(()),
        ),
        vectors=vec,
    )
    row_bits = bits_of(ranks)
    third_parts = core_sums(ffn.grads)

    one = run(
        functools.partial(attend_back_one, peers),
        [(meta, SMEM), (shards_two, hbm), (fwd.mixed, VMEM), (fwd.raw, VMEM), (ffn.mid_grad, VMEM), (fwd.out_pre, VMEM),
         (fwd.gate, VMEM), (fwd.reset_pre, VMEM), (fwd.attended, VMEM), (fwd.gated, VMEM)],
        Box(
            direct=((rows, wide), F32, VMEM), sums=((2 * wide // LANES // 8 * 8 + 8, LANES), F32, VMEM), mixed_grad=((peers, rows, width), F32, VMEM),
            attend_grad=((peers, rows, units), BF, VMEM), reset_grad=((peers, rows, units), BF, VMEM),
            bias=((peers, 8, LANES), F32, VMEM),
            grads=[((peers // 2,) + two_shape, BF, VMEM)] * 2,
        ),
        Box(
            two=pltpu.VMEM((peers,) + two_shape, BF), mixed=pltpu.VMEM((peers, rows, width), BF),
            block=pltpu.VMEM((rows, width), BF), pre_grad=pltpu.VMEM((rows, wide), BF),
            gate_grad=pltpu.VMEM((rows, wide), BF), sem=sems((count,)),
        ),
        after=[third_parts],
        hides=HIDE_ONE,
        limit=56,
    )
    vec = Box(
        zeta=zeta_proj, query_gain=query_gain, key_gain=key_gain, positions=positions,
    )
    outs = Box(
        rel=((8, LANES), F32, VMEM), sums=((8, Z), F32, VMEM), zeta=((wide, Z), F32, VMEM),
        bias=((peers, 8, LANES), F32, VMEM),
        grads=[((peers // 2, wide, 2 * units), BF, VMEM)] * 2,
    )
    outs.m = [((rows, width), BF, hbm)] * peers
    outs.r = [((rows, 2 * width), BF, hbm)] * peers
    two = run(
        functools.partial(attend_back_two, peers),
        [(meta, SMEM), (shards_one, hbm), (fwd.mixed, VMEM), (fwd.raw, VMEM), (fwd.value_pre, VMEM), (fwd.values, VMEM),
         (fwd.probs, VMEM), (one.attend_grad, VMEM), (one.reset_grad, VMEM), (one.direct, VMEM), (one.mixed_grad, VMEM),
         (fwd.queries, VMEM), (fwd.keys, VMEM), (fwd.zeta_pre, VMEM), (ffn.second, VMEM)],
        outs,
        Box(
            one=pltpu.VMEM((peers,) + one_shape, BF), query_grad=pltpu.VMEM((rows, Z), F32),
            key_grad=pltpu.VMEM((rows, Z), F32), mixed=pltpu.VMEM((rows, wide), F32), raw=pltpu.VMEM((rows, wide), F32),
            vgrad=pltpu.VMEM((rows, units), BF), mixed_out=pltpu.VMEM((peers, rows, width), BF),
            raw_out=pltpu.VMEM((peers, rows, 2 * width), BF), sem=sems((max(count, 2 * peers),)),
        ),
        vectors=vec,
    )
    grad_blocks = exchange(two.m, "wa")
    third_rows = keep_rows(third_parts, row_bits[0], two)
    mark = beside(HIDE_TWO, two.rel)
    second_parts = core_sums(one.grads, mark)
    first_parts = core_sums(two.grads, mark)

    back = run(
        functools.partial(ema_back_ends, groups, comps, peers),
        [(meta, SMEM), (grad_blocks, hbm), (ema.value, VMEM), (decay_rows, VMEM)],
        Box(
            grad=((tiles, seq_rows, LANES), F32, VMEM), after=((tiles, comps, CHUNKS, LANES), F32, VMEM),
            first=((tiles, comps, LANES), F32, VMEM),
        ),
        Box(grad=pltpu.VMEM((tok_rows, width), BF), sem=sems((peers,))),
        after=[second_parts, first_parts, third_rows],
        hides=HIDE_BACK,
    )
    nears = []
    later = group_totals(back.first, ends.fade, "seq", True, nears)
    near = nears[-1]
    third_rows = shard_sum(third_rows, nears[0])
    for bit in row_bits[1:-1]:
        third_rows = keep_rows(third_rows, bit, nears[1])
    third_rows = plus(third_rows, later_than(swap(third_rows, "seq", row_bits[-1]), near))
    first_sum = keep_rows(first_parts, row_bits[0], nears[1])
    second_sum = shard_sum(second_parts, near)
    last = run(
        functools.partial(ema_back, groups, comps),
        [(meta, SMEM), (inputs, VMEM), (back.grad, VMEM), (decay_rows, VMEM), (mix_rows, VMEM), (skip_row, VMEM),
         (ema.start, VMEM), (back.after, VMEM), (later, VMEM)],
        Box(part=((tiles, seq_rows, LANES), F32, VMEM), sums=((-(-width // LANES), 2 * comps + 8, LANES), F32, VMEM)),
        Box(
            x=pltpu.VMEM((tiles, seq_rows, LANES), F32),
            states=pltpu.VMEM((seq_rows // CHUNKS, comps, CHUNKS, LANES), F32),
        ),
        after=[third_rows, first_sum, second_sum],
        hides=HIDE_LAST,
    )
    first_rows = shard_sum(first_sum, last)
    second_rows = keep_rows(second_sum, row_bits[0], last)
    def summed(total):
        for bit in row_bits[1:-1]:
            total = keep_rows(total, bit)
        return plus(total, swap(total, "seq", row_bits[-1]))

    first_rows, second_rows = summed(first_rows), summed(second_rows)
    first_rows, *rest_sent = lax.optimization_barrier((first_rows, *two.r))
    rest_blocks = exchange(rest_sent, "wa")
    third_total = all_rows(third_rows, row_bits[:-1], last)
    second_rows, first_rows = all_rows(second_rows, row_bits[1:-1]), all_rows(first_rows, row_bits[1:-1])
    joined = run(
        functools.partial(ema_join, groups, peers),
        [(meta, SMEM), (last.part, VMEM), (rest_blocks, hbm)],
        Box(grad=((seqs, seq_rows, width), F32, VMEM), block=((seqs, seq_rows, width), BF, VMEM)),
        Box(rest=pltpu.VMEM((tok_rows, 2 * width), BF), sem=sems((peers,))),
        after=[second_rows, first_rows],
        hides=HIDE_JOIN,
    )

    second_total = all_rows(second_rows, row_bits[:1], joined)
    first_total = all_rows(first_rows, row_bits[:1], joined)
    small = [ffn.sums, one.sums, two.sums, two.rel] + [a.reshape(-1, LANES) for a in (ffn.up_bias, one.bias, two.bias)]
    places = [0]
    for part in small:
        places.append(places[-1] + part.shape[0])
    small += [mark.token] + [mark.token for mark in nears] + [two.token, back.token, ema.token, ends.token, last.token, fwd.token]
    small.append(jnp.zeros((-sum(part.shape[0] for part in small) % 16, LANES), F32))
    small, zeta_grad = sum_small(jnp.concatenate(small, axis=0), two.zeta, [("wa", bit) for bit in bits_of(peers)])
    count = small.shape[0]
    small = jnp.concatenate([small, last.sums.reshape(-1, LANES)])
    small, zeta_grad = sum_small(small, zeta_grad, [("seq", bit) for bit in row_bits])
    ema_sums = small[count:].reshape(last.sums.shape)
    ema_sums = jnp.concatenate(list(ema_sums), axis=1)[:, :width]
    decay_grad = ema_sums[:comps].T * (ema_feed * ema_read)
    moment = ema_sums[comps : 2 * comps].T
    feed_grad, read_grad = moment * ema_read, moment * ema_feed
    skip_grad = ema_sums[2 * comps]
    parts = [small[a:b] for a, b in zip(places, places[1:])]
    tall = wide // LANES
    lines = [parts[0][i * tall : (i + 1) * tall].reshape(wide) for i in range(5)]
    lines += [parts[1][i * tall : (i + 1) * tall].reshape(wide) for i in range(2)]
    loss = parts[0][5 * tall, 0] + joined.token[0, 0]
    zsums, rel_grad = parts[2], parts[3][:2].reshape(2 * GROUP)[: rel_bias.shape[0]]
    up_bias_grad, reset_bias_grad, value_bias_grad = (
        lax.dynamic_slice_in_dim(part, me * 8, 8, 0).reshape(8 * LANES)[:units] for part in parts[4:]
    )

    up_grad = jnp.concatenate([third_total[:depth, j * hidden : (j + 1) * hidden] for j in range(fold)], axis=0)
    return (
        joined.block, joined.grad, loss, decay_grad, feed_grad, read_grad, skip_grad, zeta_grad, zsums[0], zsums[1], zsums[2],
        zsums[3], rel_grad, first_total[:, :units].astype(F32), reset_bias_grad, first_total[:, units:].astype(F32), value_bias_grad,
        second_total[:width].astype(F32), lines[6], second_total[width : 2 * width].astype(F32), second_total[2 * width :].astype(F32), lines[5], lines[3],
        lines[4], up_grad.astype(F32), up_bias_grad, third_total[depth:].astype(F32), lines[2], lines[0], lines[1],
    )


def solution(mesh):
    return jax.shard_map(
        per_device,
        mesh=mesh,
        in_specs=(
            P(None, "seq", "wa"), P(None, "seq", None), P(), P(None, "seq"), P("wa", None), P("wa", None), P("wa", None), P("wa"),
            P(), P(), P(), P(), P(), P(), P(None, "wa"), P("wa"), P(None, "wa"), P("wa"), P("wa", None), P(), P("wa", None),
            P("wa", None), P(), P(), P(), P(None, "wa"), P("wa"), P("wa", None), P(), P(), P(),
        ),
        out_specs=(
            P(None, "seq", "wa"), P(None, "seq", "wa"), P(), P("wa", None), P("wa", None), P("wa", None), P("wa"), P(), P(), P(),
            P(), P(), P(), P(None, "wa"), P("wa"), P(None, "wa"), P("wa"), P("wa", None), P(), P("wa", None), P("wa", None), P(),
            P(), P(), P(None, "wa"), P("wa"), P("wa", None), P(), P(), P(),
        ),
        check_vma=False,
    )
```
